512 devices in a mesh: wide: 64 (over z, x, y_hi), narrow: 8 (over y_lo, core).
Axes of the slice: x: 4, y: 8 (y_hi: 2, y_lo: 4; y = y_hi * 4 + y_lo), z: 8, core: 2. Of those that a mesh axis runs over, the one named last changes fastest.
Arguments:
- qkv: float32 [3, 2, 4096, 5120], P(None, None, 'wide', 'narrow'), may hold values from -30 to 30
- eta: float32 [8, 4096], P('narrow', 'wide'), may hold values from 0.01 to 0.1
- fast_weights: float32 [8, 640, 3, 384], P('narrow', 'wide'), may hold values from -0.25 to 0.25
- momentum: float32 [8, 640, 3, 384], P('narrow', 'wide'), may hold values from -50 to 50
- ttt_gain: float32 [5120], P('narrow'), may hold values from 0.5 to 1.5
Outputs:
- mixed: float32 [2, 4096, 5120], P(None, 'wide', 'narrow')
- new_weights: float32 [8, 640, 3, 384], P('narrow', 'wide')
- new_momentum: float32 [8, 640, 3, 384], P('narrow', 'wide')
The draws below stay inside these ranges and needn't reach their ends.
All inputs are finite; a program needn't handle non-finite values.
Results may differ from the reference program's by a relative error of at most 0.0003.
Values sent between devices are 32-bit elements; how exact they have to be, the bound alone decides.
No kernel may reach another device: no remote copies, remote signals or barrier semaphores. Data moves between devices by JAX's collectives and lax.ppermute only.
A program may use at most 64 MiB of HBM per device.

```python
import math
import jax
import jax.numpy as jnp
from jax import lax

D = 640
H = 384
ATT = 128
WINDOW = 128
GROUPS = 2
TOK_DEV = 64
GROUP = 4096
HEADS = 8
DMODEL = 5120


def draw_qkv(key, part):
    pieces = jax.random.split(jax.random.fold_in(key, 11), 1)
    shape = (3, GROUPS, GROUP, DMODEL)
    return jax.random.truncated_normal(pieces[0], -4.0, 4.0, shape, jnp.float32)


def draw_momentum(key, part):
    pieces = jax.random.split(jax.random.fold_in(key, 23), 2)
    shape = (HEADS, D, 3, H)
    trend = 3.0 ** (jnp.arange(D, dtype=jnp.float32) / (D - 1))
    row_scale = trend * 10.0 ** jax.random.uniform(pieces[1], (D,), jnp.float32, 0.0, 1.0)
    row_scale = row_scale[None, :, None, None]
    base = jax.random.truncated_normal(pieces[0], -4.0, 4.0, shape, jnp.float32)
    return 0.3 * base * row_scale


def levels(key, extent, cuts, smallest, high):
    def one(dim, shards_of):
        draws = jax.random.uniform(jax.random.fold_in(jax.random.fold_in(key, 6), dim), (shards_of,), jnp.float32, smallest / len(cuts), high / len(cuts))
        return jnp.repeat(jnp.exp(draws), extent[dim] // shards_of).reshape((-1,) + (1,) * (len(extent) - dim - 1))

    factor_of = one(*cuts[0])
    for cut in cuts[1:]:
        factor_of = factor_of * one(*cut)
    return factor_of


def normal_values(own_key, shape, deviation, most, cuts=(), kind=jnp.bfloat16):
    entries = deviation * jax.random.normal(own_key, shape, jnp.float32)
    if cuts:
        entries = entries * levels(own_key, shape, cuts, -0.22, 0.18)
    return jnp.clip(entries, -most, most).astype(kind)


def setup_inputs(seed: int = 0) -> dict:
    arg_keys = jax.random.split(jax.random.key(seed), 6)
    qkv = draw_qkv(jax.random.fold_in(arg_keys[5], 71), 0)
    eta = jnp.clip(jnp.exp(math.log(0.1) - 2.3025851 * jax.random.uniform(arg_keys[1], (HEADS, GROUP), jnp.float32) ** levels(arg_keys[1], (HEADS, GROUP), ((0, 8), (1, 64)), -0.2, 0.2)), 0.01, 0.1)
    fast_weights = normal_values(arg_keys[2], (HEADS, D, 3, H), D ** -0.5, 0.25, ((0, 8), (1, 64)), jnp.float32)
    momentum = draw_momentum(jax.random.fold_in(arg_keys[5], 71), 0)
    ttt_gain = jnp.clip(1.0 + 0.1 * jax.random.normal(arg_keys[4], (DMODEL,), jnp.float32), 0.5, 1.5)
    return dict(qkv=qkv, eta=eta, fast_weights=fast_weights, momentum=momentum, ttt_gain=ttt_gain)


EPSILON = 1e-06
MOMENTUM_RATE = 0.9
STEP_SIZE = 0.03
PRECISION = lax.Precision.HIGHEST

def product(left, right):
    return jnp.dot(left, right, precision=PRECISION, preferred_element_type=jnp.float32)

def memory_read(inputs, weights):
    gate_pre = product(inputs, weights[:, 0, :])
    up_pre = product(inputs, weights[:, 1, :])
    hidden = jax.nn.silu(gate_pre) * up_pre
    return product(hidden, weights[:, 2, :].T)

def memory_gradient(key_rows, value_rows, rates, weights):
    gate_pre = product(key_rows, weights[:, 0, :])
    up_pre = product(key_rows, weights[:, 1, :])
    sigmoid = jax.nn.sigmoid(gate_pre)
    gated = gate_pre * sigmoid
    hidden = gated * up_pre
    weighted = rates[:, None] * value_rows
    back = -product(weighted, weights[:, 2, :])
    gate_back = back * up_pre * sigmoid * (1.0 + gate_pre * (1.0 - sigmoid))
    up_back = back * gated
    return (weighted, hidden, gate_back, up_back)

def renormalize(weights, moment):
    spread = jnp.sqrt(lax.optimization_barrier(jnp.mean(moment * moment, axis=0)) + EPSILON)
    moved = weights - STEP_SIZE * moment / spread
    ratio = jnp.sqrt(lax.optimization_barrier(jnp.mean(weights * weights, axis=0)) + EPSILON) / jnp.sqrt(lax.optimization_barrier(jnp.mean(moved * moved, axis=0)) + EPSILON)
    return moved * ratio

def reference(qkv, eta, fast_weights, momentum, ttt_gain):
    total = GROUPS * GROUP
    head_count = DMODEL // ATT
    query_all = qkv[0].reshape(total, DMODEL)
    key_all = qkv[1].reshape(total, DMODEL)
    value_all = qkv[2].reshape(total, DMODEL)
    padding = jnp.zeros((WINDOW, DMODEL), jnp.float32)
    key_padded = jnp.concatenate([padding, key_all], axis=0)
    value_padded = jnp.concatenate([padding, value_all], axis=0)

    def attend(block):
        start = block * TOK_DEV
        query_block = lax.dynamic_slice_in_dim(query_all, start, TOK_DEV, 0).reshape(TOK_DEV, head_count, ATT)
        key_block = lax.dynamic_slice_in_dim(key_padded, start, TOK_DEV + WINDOW, 0).reshape(TOK_DEV + WINDOW, head_count, ATT)
        value_block = lax.dynamic_slice_in_dim(value_padded, start, TOK_DEV + WINDOW, 0).reshape(TOK_DEV + WINDOW, head_count, ATT)
        scores = jnp.einsum('qhe,khe->hqk', query_block, key_block, precision=PRECISION) / math.sqrt(ATT)
        query_pos = start + jnp.arange(TOK_DEV, dtype=jnp.int32)
        key_pos = start - WINDOW + jnp.arange(TOK_DEV + WINDOW, dtype=jnp.int32)
        distance = query_pos[:, None] - key_pos[None, :]
        allowed = (distance >= 0) & (distance < WINDOW) & (key_pos >= 0)[None, :]
        scores = jnp.where(allowed[None], scores, -1e+30)
        highest = lax.optimization_barrier(jnp.max(scores, axis=-1, keepdims=True))
        weights = jnp.exp(scores - highest)
        weights = weights / lax.optimization_barrier(jnp.sum(weights, axis=-1, keepdims=True))
        return jnp.einsum('hqk,khe->qhe', weights, value_block, precision=PRECISION).reshape(TOK_DEV, DMODEL)
    attended = lax.map(attend, jnp.arange(total // TOK_DEV, dtype=jnp.int32)).reshape(GROUPS, GROUP, DMODEL)
    readouts = []
    updated_list = []
    moment_list = []
    for memory in range(HEADS):
        lower = memory * D
        weights = fast_weights[memory]
        first_queries = qkv[0, 0, :, lower:lower + D]
        first_keys = qkv[1, 0, :, lower:lower + D]
        first_values = qkv[2, 0, :, lower:lower + D]
        first_read = memory_read(first_queries, weights)
        weighted, hidden, gate_back, up_back = memory_gradient(first_keys, first_values, eta[memory], weights)
        gradient = jnp.stack([product(first_keys.T, gate_back), product(first_keys.T, up_back), -product(weighted.T, hidden)], axis=1)
        moment = MOMENTUM_RATE * momentum[memory] + gradient
        updated = renormalize(weights, moment)
        second_read = memory_read(qkv[0, 1, :, lower:lower + D], updated)
        readouts.append(jnp.stack([first_read, second_read]))
        updated_list.append(updated)
        moment_list.append(moment)
    readout = jnp.concatenate(readouts, axis=-1)
    scale = jnp.sqrt(lax.optimization_barrier(jnp.mean(readout * readout, axis=-1, keepdims=True)) + EPSILON)
    mixed = attended + ttt_gain * (readout / scale)
    return (mixed, jnp.stack(updated_list), jnp.stack(moment_list))
```

```python
import functools
import math

import jax
import jax.numpy as jnp
from jax import lax
from jax.experimental import pallas as pl
from jax.experimental.pallas import tpu as pltpu
from jax.sharding import Mesh
from jax.sharding import PartitionSpec as P

ATT = 128
WINDOW = 128
EPSILON = 1e-06
MOMENTUM_RATE = 0.9
STEP_SIZE = 0.03
PRECISION = lax.Precision.HIGHEST

NZ, NX, NY = 8, 4, 2
BLOCKS = NZ * NX * NY
ROWS = 10
SLICE = 96
LANES = 128
TOK = 64
D = 640
H = 384
NARROW = 8
GROUPS = 2
VMEM_LIMIT = 24 * 1024 * 1024


def dot(left, right, dims=((1,), (0,))):
    return lax.dot_general(
        left, right, (dims, ((), ())), precision=PRECISION, preferred_element_type=jnp.float32
    )


def entry(group, sublane):
    q = group * 8 + sublane
    return (q // 3, q % 3) if q < 3 * ROWS else None


def call(body, outs, cost, *args, scratch=()):
    flops, nbytes = cost
    vmem = pl.BlockSpec(memory_space=pltpu.VMEM)
    return pl.pallas_call(
        body,
        out_shape=[jax.ShapeDtypeStruct(s, jnp.float32) for s in outs],
        in_specs=[pl.BlockSpec(memory_space=pltpu.SMEM) if a.dtype == jnp.int32 else vmem for a in args],
        out_specs=[vmem] * len(outs),
        scratch_shapes=[pltpu.VMEM(s, jnp.float32) for s in scratch],
        compiler_params=pltpu.CompilerParams(vmem_limit_bytes=VMEM_LIMIT),
        cost_estimate=pl.CostEstimate(flops=flops, bytes_accessed=nbytes, transcendentals=0),
    )(*args)


def to_column(row):
    n = row.shape[1]
    same = lax.broadcasted_iota(jnp.int32, (n, n), 0) == lax.broadcasted_iota(jnp.int32, (n, n), 1)
    return jnp.sum(jnp.where(same, row, 0.0), axis=1, keepdims=True)


def to_row(column):
    n = column.shape[0]
    same = lax.broadcasted_iota(jnp.int32, (n, n), 0) == lax.broadcasted_iota(jnp.int32, (n, n), 1)
    return jnp.sum(jnp.where(same, column, 0.0), axis=0, keepdims=True)


def own_packs(own_ref, flat_ref):
    flat_ref[24:32, :] = jnp.zeros((8, H), jnp.float32)
    for r in range(ROWS):
        flat_ref[3 * r : 3 * r + 3, :] = own_ref[r]
    return [
        jnp.concatenate(
            [flat_ref[8 * g : 8 * g + 8, SLICE * x : SLICE * (x + 1)] for g in range(4)], axis=1
        )
        for x in range(NX)
    ]


def prepare_body(fw_ref, mom_ref, eta_ref, key_ref, value_ref, send1_ref, sendx_ref, flat_ref):
    packs = own_packs(fw_ref, flat_ref)
    for z in range(NZ):
        for x in range(NX):
            for y in range(NY):
                for t in range(3):
                    send1_ref[(z * NX + x) * NY + y, 8 * t : 8 * t + 8, :] = packs[x][:, LANES * t : LANES * (t + 1)]
    keys = key_ref[...]
    weighted = to_column(eta_ref[...]) * value_ref[...]
    packs = own_packs(mom_ref, flat_ref)
    for x in range(NX):
        sendx_ref[x, 0:TOK, :] = keys
        sendx_ref[x, TOK : 2 * TOK, :] = weighted
        sendx_ref[x, 2 * TOK : 2 * TOK + 8, 0:H] = packs[x]
        sendx_ref[x, 2 * TOK : 2 * TOK + 8, H:D] = jnp.zeros((8, D - H), jnp.float32)


def widened(part):
    return jnp.concatenate([part, jnp.zeros((part.shape[0], LANES - SLICE), jnp.float32)], axis=1)


def unpack(recv_ref, out_refs, x_stride, y_stride, z_stride):
    for s in range(8):
        for x in range(NX):
            for y in range(NY):
                start = x * x_stride + y * y_stride + s
                rows = jnp.concatenate(
                    [recv_ref[pl.ds(start + 8 * t, NZ, stride=z_stride), :] for t in range(3)], axis=1
                )
                for g in range(4):
                    at = entry(g, s)
                    if at is None:
                        continue
                    r, i = at
                    out_refs[i][pl.ds((x * NY + y) * ROWS + r, NZ, stride=NX * NY * ROWS), :] = widened(
                        rows[:, SLICE * g : SLICE * (g + 1)]
                    )


def pack(in_refs, send_ref, x_stride, y_stride, z_stride):
    for s in range(8):
        for x in range(NX):
            for y in range(NY):
                parts = []
                for g in range(4):
                    at = entry(g, s)
                    if at is None:
                        parts.append(jnp.zeros((NZ, SLICE), jnp.float32))
                        continue
                    r, i = at
                    parts.append(in_refs[i][pl.ds((x * NY + y) * ROWS + r, NZ, stride=NX * NY * ROWS), :][:, :SLICE])
                rows = jnp.concatenate(parts, axis=1)
                start = x * x_stride + y * y_stride + s
                for t in range(3):
                    send_ref[pl.ds(start + 8 * t, NZ, stride=z_stride), :] = rows[:, LANES * t : LANES * (t + 1)]


def token_rows(ref, start):
    return jnp.concatenate([ref[x, start : start + TOK, :] for x in range(NX)], axis=0)


def gradient_body(recv1_ref, recvx_ref, w1_ref, w3_ref, w2_ref, send_ref, g1_ref, g3_ref, g2_ref):
    unpack(recv1_ref, (w1_ref, w3_ref, w2_ref), 48, 24, 192)
    keys = token_rows(recvx_ref, 0)
    weighted = token_rows(recvx_ref, TOK)
    pre = dot(keys, jnp.concatenate([w1_ref[...], w3_ref[...]], axis=1))
    gate_pre, up_pre = pre[:, :LANES], pre[:, LANES:]
    back = -dot(weighted, w2_ref[...])
    sigmoid = jax.nn.sigmoid(gate_pre)
    gated = gate_pre * sigmoid
    hidden = gated * up_pre
    gate_back = back * up_pre * sigmoid * (1.0 + gate_pre * (1.0 - sigmoid))
    up_back = back * gated
    both = dot(keys, jnp.concatenate([gate_back, up_back], axis=1), ((0,), (0,)))
    g1_ref[...] = both[:, :LANES]
    g3_ref[...] = both[:, LANES:]
    g2_ref[...] = -dot(weighted, hidden, ((0,), (0,)))
    pack((g1_ref, g3_ref, g2_ref), send_ref, 24, 96, 192)


def moment_body(recv2_ref, recvx_ref, send3_ref, own_ref):
    total = recv2_ref[0]
    for j in range(1, NZ * NY):
        total = total + recv2_ref[j]
    old = jnp.concatenate(
        [
            recvx_ref[x, 2 * TOK : 2 * TOK + 8, LANES * t : LANES * (t + 1)]
            for x in range(NX)
            for t in range(3)
        ],
        axis=0,
    )
    moment = MOMENTUM_RATE * old + total
    own_ref[...] = moment
    for j in range(NZ * NY):
        send3_ref[j] = moment


def hidden_of(inputs, w1, w3):
    pre = dot(inputs, jnp.concatenate([w1, w3], axis=1))
    gate_pre, up_pre = pre[:, :LANES], pre[:, LANES:]
    return gate_pre * jax.nn.sigmoid(gate_pre) * up_pre


def first_read_body(recvq_ref, w1_ref, w3_ref, w2_ref, moment_ref, send_ref):
    hidden = hidden_of(token_rows(recvq_ref, 0), w1_ref[...], w3_ref[...])
    partial = dot(hidden, w2_ref[...], ((1,), (1,)))
    for x in range(NX):
        send_ref[x, 0:TOK, :] = partial[x * TOK : (x + 1) * TOK]
        for t in range(3):
            send_ref[x, TOK : TOK + 8, LANES * t : LANES * (t + 1)] = moment_ref[24 * x + 8 * t : 24 * x + 8 * t + 8, :]
        send_ref[x, TOK : TOK + 8, H:D] = jnp.zeros((8, D - H), jnp.float32)


def renormalized(weights, moment):
    rate = STEP_SIZE / jnp.sqrt(jnp.mean(moment * moment, axis=0, keepdims=True) + EPSILON)
    moved = weights - moment * rate
    ratio = jnp.sqrt(jnp.mean(weights * weights, axis=0, keepdims=True) + EPSILON) / jnp.sqrt(
        jnp.mean(moved * moved, axis=0, keepdims=True) + EPSILON
    )
    return moved * ratio, rate, ratio


def second_read_body(recv3_ref, recvq_ref, w1_ref, w3_ref, w2_ref, send_ref, m1_ref, m3_ref, m2_ref):
    unpack(recv3_ref, (m1_ref, m3_ref, m2_ref), 24, 96, 192)
    new1, rate1, ratio1 = renormalized(w1_ref[...], m1_ref[...])
    new3, rate3, ratio3 = renormalized(w3_ref[...], m3_ref[...])
    new2, rate2, ratio2 = renormalized(w2_ref[...], m2_ref[...])
    hidden = hidden_of(token_rows(recvq_ref, TOK), new1, new3)
    partial = dot(hidden, new2, ((1,), (1,)))
    stats = [rate1, rate3, rate2, ratio1, ratio3, ratio2, jnp.zeros((2, LANES), jnp.float32)]
    stats = jnp.concatenate(stats, axis=0)
    for x in range(NX):
        send_ref[x, 0:TOK, :] = partial[x * TOK : (x + 1) * TOK]
        send_ref[x, TOK : TOK + 8, 0:LANES] = stats
        send_ref[x, TOK : TOK + 8, LANES:D] = jnp.zeros((8, D - LANES), jnp.float32)


def squares_body(first_ref, second_ref, readout_ref, send_ref):
    rows = []
    for c, ref in enumerate((first_ref, second_ref)):
        total = ref[0, 0:TOK, :]
        for x in range(1, NX):
            total = total + ref[x, 0:TOK, :]
        readout_ref[c] = total
        rows.append(to_row(jnp.sum(total * total, axis=1, keepdims=True)))
    row = jnp.concatenate(rows, axis=1)
    for n in range(NARROW):
        send_ref[n] = jnp.broadcast_to(row, (8, GROUPS * TOK))


def own_rows_body(first_ref, second_ref, fw_ref, new_w_ref, new_m_ref, flat_ref):
    for g in range(4):
        flat_ref[8 * g : 8 * g + 8, :] = jnp.concatenate(
            [first_ref[x, TOK : TOK + 8, SLICE * g : SLICE * (g + 1)] for x in range(NX)], axis=1
        )
    stats = jnp.concatenate([second_ref[x, TOK : TOK + 8, 0:SLICE] for x in range(NX)], axis=1)
    for r in range(ROWS):
        moment = flat_ref[3 * r : 3 * r + 3, :]
        new_m_ref[r] = moment
        new_w_ref[r] = (fw_ref[r] - moment * stats[0:3]) * stats[3:6]


def mix_body(recv_ref, readout_ref, attended_ref, gain_ref, mixed_ref):
    total = recv_ref[0, 0:1, :]
    for n in range(1, NARROW):
        total = total + recv_ref[n, 0:1, :]
    scale = to_column(1.0 / jnp.sqrt(total / (D * NARROW) + EPSILON))
    for c in range(GROUPS):
        mixed_ref[c] = attended_ref[c] + gain_ref[...] * (readout_ref[c] * scale[c * TOK : (c + 1) * TOK])


def attention_body(position_ref, q_ref, k_ref, v_ref, near_ref, far_ref, out_ref):
    position = position_ref[0]
    row = lax.broadcasted_iota(jnp.int32, (TOK, 3 * TOK), 0) + 2 * TOK
    col = lax.broadcasted_iota(jnp.int32, (TOK, 3 * TOK), 1)
    window = (row - col >= 0) & (row - col < WINDOW)
    for c in range(GROUPS):
        if c == 0:
            first = jnp.where(position >= 2, 0, jnp.where(position >= 1, TOK, 2 * TOK))
            allowed = window & (col >= first)
        else:
            allowed = window
        for h in range(D // ATT):
            at = slice(h * ATT, (h + 1) * ATT)
            parts = []
            for a in range(2):
                own = (k_ref, v_ref)[a]
                if c == 0:
                    far, near = far_ref[a, 0, :, at], near_ref[a, 0, :, at]
                else:
                    far = jnp.where(position >= 2, far_ref[a, 1, :, at], far_ref[a, 0, :, at])
                    near = jnp.where(position >= 1, near_ref[a, 1, :, at], near_ref[a, 0, :, at])
                parts.append(jnp.concatenate([far, near, own[c, :, at]], axis=0))
            keys, values = parts
            scores = dot(q_ref[c, :, at], keys, ((1,), (1,))) * (1.0 / math.sqrt(ATT))
            scores = jnp.where(allowed, scores, -1e30)
            weights = jnp.exp(scores - jnp.max(scores, axis=1, keepdims=True))
            weights = weights / jnp.sum(weights, axis=1, keepdims=True)
            out_ref[c, :, at] = dot(weights, values)


def behind(block, distance):
    axes = ("z", "x", "yh")
    return lax.ppermute(block, axes, [((i - distance) % BLOCKS, i) for i in range(BLOCKS)])


def exchange(pieces, axes):
    return lax.all_to_all(pieces, axes, split_axis=0, concat_axis=0, tiled=True)


def local(qkv, eta, fast_weights, momentum, ttt_gain):
    queries = qkv[0]
    own_weights, own_moment = fast_weights[0], momentum[0]
    position = (lax.axis_index("z") * NX + lax.axis_index("x")) * NY + lax.axis_index("yh")
    send1, sendx = call(
        prepare_body, [(BLOCKS, 24, LANES), (NX, 2 * TOK + 8, D)], (10**6, 3 * 10**6),
        own_weights, own_moment, eta, qkv[1, 0], qkv[2, 0], scratch=[(32, H)],
    )
    recvx = exchange(sendx, "x")
    recv1 = exchange(send1, ("z", "x", "yh"))
    near = behind(qkv[1:], 1)
    far = behind(qkv[1:], 2)
    w1, w3, w2, send2 = call(
        gradient_body, [(D, LANES)] * 3 + [(BLOCKS * 24, LANES)], (3 * 10**9, 4 * 10**6),
        recv1.reshape(BLOCKS * 24, LANES), recvx, scratch=[(D, LANES)] * 3,
    )
    recv2 = exchange(send2.reshape(NZ * NY, NX * 24, LANES), ("z", "yh"))
    recvq = exchange(jnp.broadcast_to(queries.reshape(1, 2 * TOK, D), (NX, 2 * TOK, D)), "x")
    (attended,) = call(
        attention_body, [(GROUPS, TOK, D)], (3 * 10**9, 4 * 10**6),
        jnp.reshape(position, (1,)).astype(jnp.int32), queries, qkv[1], qkv[2], near, far,
    )
    send3, moment = call(moment_body, [(NZ * NY, NX * 24, LANES), (NX * 24, LANES)], (10**6, 2 * 10**6), recv2, recvx)
    recv3 = exchange(send3, ("z", "yh"))
    (send_first,) = call(first_read_body, [(NX, TOK + 8, D)], (10**9, 3 * 10**6), recvq, w1, w3, w2, moment)
    first = exchange(send_first, "x")
    (send_second,) = call(
        second_read_body, [(NX, TOK + 8, D)], (10**9, 3 * 10**6),
        recv3.reshape(BLOCKS * 24, LANES), recvq, w1, w3, w2, scratch=[(D, LANES)] * 3,
    )
    second = exchange(send_second, "x")
    readout, send5 = call(
        squares_body, [(GROUPS, TOK, D), (NARROW, 8, GROUPS * TOK)], (10**6, 2 * 10**6), first, second
    )
    recv5 = exchange(send5, "narrow")
    new_weights, new_moment = call(
        own_rows_body, [(ROWS, 3, H), (ROWS, 3, H)], (10**6, 10**6), first, second, own_weights, scratch=[(32, H)]
    )
    (mixed,) = call(
        mix_body, [(GROUPS, TOK, D)], (10**6, 10**6), recv5, readout, attended, ttt_gain.reshape(1, D)
    )
    return mixed, new_weights[None], new_moment[None]


def solution(mesh):
    fine = Mesh(mesh.devices.reshape(NZ, NX, NY, NARROW), ("z", "x", "yh", "narrow"))
    wide = ("z", "x", "yh")
    return jax.shard_map(
        local,
        mesh=fine,
        in_specs=(
            P(None, None, wide, "narrow"),
            P("narrow", wide),
            P("narrow", wide, None, None),
            P("narrow", wide, None, None),
            P("narrow"),
        ),
        out_specs=(
            P(None, wide, "narrow"),
            P("narrow", wide, None, None),
            P("narrow", wide, None, None),
        ),
        check_vma=False,
    )
```

```python
import functools
import math

import jax
import jax.numpy as jnp
from jax import lax
from jax.experimental import pallas as pl
from jax.experimental.pallas import tpu as pltpu
from jax.sharding import Mesh
from jax.sharding import PartitionSpec as P

ATT = 128
WINDOW = 128
EPSILON = 1e-06
MOMENTUM_RATE = 0.9
STEP_SIZE = 0.03
PRECISION = lax.Precision.HIGHEST

NZ, NX, NY = 8, 4, 2
BLOCKS = NZ * NX * NY
ROWS = 10
SLICE = 96
LANES = 128
TOK = 64
D = 640
H = 384
NARROW = 8
GROUPS = 2
VMEM_LIMIT = 16 * 1024 * 1024


def dot(left, right, dims=((1,), (0,))):
    return lax.dot_general(
        left, right, (dims, ((), ())), precision=PRECISION, preferred_element_type=jnp.float32
    )


def entry(group, sublane):
    q = group * 8 + sublane
    return (q // 3, q % 3) if q < 3 * ROWS else None


def call(body, outs, micros, *args, scratch=(), specs=None, after=(), grid=()):
    vmem = pl.BlockSpec(memory_space=pltpu.VMEM)
    specs = dict(specs or {})
    count, skipped, results = len(args), len(after), len(outs)

    def kernel(*refs):
        inputs, rest = refs[:count], refs[count + skipped :]
        targets, held, rest, sems = rest[:results], rest[results : 2 * results], rest[2 * results : -1], rest[-1]
        copies = [pltpu.make_async_copy(held[n], targets[n], sems.at[n]) for n in range(results)]
        started = set()

        def send(n):
            copies[n].start()
            started.add(n)

        body(*inputs, *held, *rest, send)
        for n in range(results):
            if n not in started:
                copies[n].start()
        for copy in copies:
            copy.wait()

    return pl.pallas_call(
        kernel,
        grid=grid,
        out_shape=[jax.ShapeDtypeStruct(s, jnp.float32) for s in outs],
        in_specs=[specs.get(n, vmem) for n in range(count)] + [pl.BlockSpec(memory_space=pl.ANY)] * skipped,
        out_specs=[pl.BlockSpec(memory_space=pltpu.HBM)] * results,
        scratch_shapes=[
            *(pltpu.VMEM(s, jnp.float32) for s in outs),
            *(pltpu.VMEM(s, jnp.float32) for s in scratch),
            pltpu.SemaphoreType.DMA((results,)),
        ],
        compiler_params=pltpu.CompilerParams(vmem_limit_bytes=VMEM_LIMIT),
        cost_estimate=pl.CostEstimate(flops=int(micros * 1e9), bytes_accessed=10**6, transcendentals=0),
    )(*args, *after)


def to_column(row):
    n = row.shape[1]
    same = lax.broadcasted_iota(jnp.int32, (n, n), 0) == lax.broadcasted_iota(jnp.int32, (n, n), 1)
    return jnp.sum(jnp.where(same, row, 0.0), axis=1, keepdims=True)


def to_row(column):
    n = column.shape[0]
    same = lax.broadcasted_iota(jnp.int32, (n, n), 0) == lax.broadcasted_iota(jnp.int32, (n, n), 1)
    return jnp.sum(jnp.where(same, column, 0.0), axis=0, keepdims=True)


def own_packs(own_ref, flat_ref):
    flat_ref[24:32, :] = jnp.zeros((8, H), jnp.float32)
    for q in range(3 * ROWS):
        flat_ref[q : q + 1, :] = own_ref[q]
    return [
        jnp.concatenate(
            [flat_ref[8 * g : 8 * g + 8, SLICE * x : SLICE * (x + 1)] for g in range(4)], axis=1
        )
        for x in range(NX)
    ]


def prepare_weights_body(fw_ref, send1_ref, flat_ref, send):
    packs = own_packs(fw_ref, flat_ref)
    for z in range(NZ):
        for x in range(NX):
            for y in range(NY):
                for t in range(3):
                    send1_ref[(z * NX + x) * NY + y, 8 * t : 8 * t + 8, :] = packs[x][:, LANES * t : LANES * (t + 1)]


def prepare_tokens_body(eta_ref, qkv_ref, mom_ref, pairs_ref, queries_ref, flat_ref, send):
    pairs_ref[0:TOK, :] = qkv_ref[1, 0]
    pairs_ref[TOK : 2 * TOK, :] = to_column(eta_ref[...]) * qkv_ref[2, 0]
    send(0)
    queries_ref[0:TOK, :] = qkv_ref[0, 0]
    queries_ref[TOK : 2 * TOK, :] = qkv_ref[0, 1]
    packs = own_packs(mom_ref, flat_ref)
    for x in range(NX):
        queries_ref[2 * TOK + 8 * x : 2 * TOK + 8 * x + 8, 0:H] = packs[x]
        queries_ref[2 * TOK + 8 * x : 2 * TOK + 8 * x + 8, H:D] = jnp.zeros((8, D - H), jnp.float32)


def widened(part):
    return jnp.concatenate([part, jnp.zeros((part.shape[0], LANES - SLICE), jnp.float32)], axis=1)


def unpack(recv_ref, out_ref, x_stride, y_stride, z_stride):
    for s in range(8):
        for x in range(NX):
            for y in range(NY):
                start = x * x_stride + y * y_stride + s
                rows = jnp.concatenate(
                    [recv_ref[pl.ds(start + 8 * t, NZ, stride=z_stride), :] for t in range(3)], axis=1
                )
                for g in range(4):
                    at = entry(g, s)
                    if at is None:
                        continue
                    r, i = at
                    out_ref[pl.ds(i * D + (x * NY + y) * ROWS + r, NZ, stride=NX * NY * ROWS), :] = widened(
                        rows[:, SLICE * g : SLICE * (g + 1)]
                    )


def pack(in_ref, send_ref, x_stride, y_stride, z_stride):
    for s in range(8):
        for x in range(NX):
            for y in range(NY):
                parts = []
                for g in range(4):
                    at = entry(g, s)
                    if at is None:
                        parts.append(jnp.zeros((NZ, SLICE), jnp.float32))
                        continue
                    r, i = at
                    parts.append(in_ref[pl.ds(i * D + (x * NY + y) * ROWS + r, NZ, stride=NX * NY * ROWS), :][:, :SLICE])
                rows = jnp.concatenate(parts, axis=1)
                start = x * x_stride + y * y_stride + s
                for t in range(3):
                    send_ref[pl.ds(start + 8 * t, NZ, stride=z_stride), :] = rows[:, LANES * t : LANES * (t + 1)]


def token_rows(refs, start):
    return jnp.concatenate([ref[start : start + TOK, :] for ref in refs], axis=0)


def matrix(ref, i):
    return ref[i * D : (i + 1) * D, :]


def gradient_body(recv1_ref, p0_ref, p1_ref, p2_ref, p3_ref, w_ref, send_ref, g_ref, send):
    unpack(recv1_ref, w_ref, 48, 24, 192)
    send(0)
    pairs = (p0_ref, p1_ref, p2_ref, p3_ref)
    keys = token_rows(pairs, 0)
    weighted = token_rows(pairs, TOK)
    pre = dot(keys, jnp.concatenate([matrix(w_ref, 0), matrix(w_ref, 1)], axis=1))
    gate_pre, up_pre = pre[:, :LANES], pre[:, LANES:]
    back = -dot(weighted, matrix(w_ref, 2))
    sigmoid = jax.nn.sigmoid(gate_pre)
    gated = gate_pre * sigmoid
    hidden = gated * up_pre
    gate_back = back * up_pre * sigmoid * (1.0 + gate_pre * (1.0 - sigmoid))
    up_back = back * gated
    both = dot(keys, jnp.concatenate([gate_back, up_back], axis=1), ((0,), (0,)))
    g_ref[0:D, :] = both[:, :LANES]
    g_ref[D : 2 * D, :] = both[:, LANES:]
    g_ref[2 * D : 3 * D, :] = -dot(weighted, hidden, ((0,), (0,)))
    pack(g_ref, send_ref, 24, 96, 192)


def source(x_ref, s):
    return lax.rem(x_ref[0] + NX - s, NX)


def moment_body(x_ref, recv2_ref, q0_ref, q1_ref, q2_ref, q3_ref, send3_ref, own_ref, send):
    total = recv2_ref[0]
    for j in range(1, NZ * NY):
        total = total + recv2_ref[j]
    own_ref[...] = total
    mine = pl.ds(pl.multiple_of(2 * TOK + 8 * x_ref[0], 8), 8)
    for s, ref in enumerate((q0_ref, q1_ref, q2_ref, q3_ref)):
        old = ref[mine, :]
        old = jnp.concatenate([old[:, LANES * t : LANES * (t + 1)] for t in range(3)], axis=0)
        rows = pl.ds(pl.multiple_of(24 * source(x_ref, s), 8), 24)
        own_ref[rows, :] = own_ref[rows, :] + MOMENTUM_RATE * old
    moment = own_ref[...]
    for j in range(NZ * NY):
        send3_ref[j] = moment


def hidden_of(inputs, w1, w3):
    pre = dot(inputs, jnp.concatenate([w1, w3], axis=1))
    gate_pre, up_pre = pre[:, :LANES], pre[:, LANES:]
    return gate_pre * jax.nn.sigmoid(gate_pre) * up_pre


def first_read_body(q0_ref, q1_ref, q2_ref, q3_ref, w_ref, *out_refs):
    out_refs = out_refs[:NX]
    hidden = hidden_of(token_rows((q0_ref, q1_ref, q2_ref, q3_ref), 0), matrix(w_ref, 0), matrix(w_ref, 1))
    partial = dot(hidden, matrix(w_ref, 2), ((1,), (1,)))
    for s in range(NX):
        out_refs[s][...] = partial[s * TOK : (s + 1) * TOK]


def renormalized(weights, moment):
    rate = STEP_SIZE / jnp.sqrt(jnp.mean(moment * moment, axis=0, keepdims=True) + EPSILON)
    moved = weights - moment * rate
    ratio = jnp.sqrt(jnp.mean(weights * weights, axis=0, keepdims=True) + EPSILON) / jnp.sqrt(
        jnp.mean(moved * moved, axis=0, keepdims=True) + EPSILON
    )
    return moved * ratio, rate, ratio


def second_read_body(x_ref, recv3_ref, q0_ref, q1_ref, q2_ref, q3_ref, w_ref, moment_ref, send_ref, m_ref, send):
    unpack(recv3_ref, m_ref, 24, 96, 192)
    new1, rate1, ratio1 = renormalized(matrix(w_ref, 0), matrix(m_ref, 0))
    new3, rate3, ratio3 = renormalized(matrix(w_ref, 1), matrix(m_ref, 1))
    new2, rate2, ratio2 = renormalized(matrix(w_ref, 2), matrix(m_ref, 2))
    hidden = hidden_of(token_rows((q0_ref, q1_ref, q2_ref, q3_ref), TOK), new1, new3)
    partial = dot(hidden, new2, ((1,), (1,)))
    stats = [rate1, rate3, rate2, ratio1, ratio3, ratio2, jnp.zeros((2, LANES), jnp.float32)]
    stats = jnp.concatenate(stats, axis=0)
    for x in range(NX):
        tail = [stats, *(moment_ref[24 * x + 8 * t : 24 * x + 8 * t + 8, :] for t in range(3))]
        tail.append(jnp.zeros((8, LANES), jnp.float32))
        send_ref[x, TOK : TOK + 8, :] = jnp.concatenate(tail, axis=1)
    for s in range(NX):
        send_ref[source(x_ref, s), 0:TOK, :] = partial[s * TOK : (s + 1) * TOK]


def squares_body(f0_ref, f1_ref, f2_ref, f3_ref, second_ref, readout_ref, send_ref, send):
    first = f0_ref[...] + f1_ref[...] + f2_ref[...] + f3_ref[...]
    second = second_ref[0, 0:TOK, :]
    for x in range(1, NX):
        second = second + second_ref[x, 0:TOK, :]
    readout_ref[0] = first
    readout_ref[1] = second
    row = jnp.concatenate(
        [to_row(jnp.sum(total * total, axis=1, keepdims=True)) for total in (first, second)], axis=1
    )
    for n in range(NARROW):
        send_ref[n] = jnp.broadcast_to(row, (8, GROUPS * TOK))


def own_rows_body(second_ref, fw_ref, new_w_ref, new_m_ref, flat_ref, send):
    for g in range(4):
        flat_ref[8 * g : 8 * g + 8, :] = jnp.concatenate(
            [
                second_ref[x, TOK : TOK + 8, LANES + SLICE * g : LANES + SLICE * (g + 1)]
                for x in range(NX)
            ],
            axis=1,
        )
    stats = jnp.concatenate([second_ref[x, TOK : TOK + 8, 0:SLICE] for x in range(NX)], axis=1)
    for q in range(3 * ROWS):
        i = q % 3
        moment = flat_ref[q : q + 1, :]
        new_m_ref[q] = moment
        new_w_ref[q] = (fw_ref[q] - moment * stats[i : i + 1]) * stats[3 + i : 4 + i]


def mix_body(recv_ref, readout_ref, attended_ref, gain_ref, mixed_ref, send):
    total = recv_ref[0, 0:1, :]
    for n in range(1, NARROW):
        total = total + recv_ref[n, 0:1, :]
    scale = to_column(1.0 / jnp.sqrt(total / (D * NARROW) + EPSILON))
    for c in range(GROUPS):
        mixed_ref[c] = attended_ref[c] + gain_ref[...] * (readout_ref[c] * scale[c * TOK : (c + 1) * TOK])


def attention_body(position_ref, qkv_ref, near_ref, far_ref, out_ref, send):
    position = position_ref[0]
    row = lax.broadcasted_iota(jnp.int32, (TOK, 3 * TOK), 0) + 2 * TOK
    col = lax.broadcasted_iota(jnp.int32, (TOK, 3 * TOK), 1)
    window = (row - col >= 0) & (row - col < WINDOW)
    for c in range(GROUPS):
        if c == 0:
            first = jnp.where(position >= 2, 0, jnp.where(position >= 1, TOK, 2 * TOK))
            allowed = window & (col >= first)
        else:
            allowed = window
        for h in range(D // ATT):
            at = slice(h * ATT, (h + 1) * ATT)
            parts = []
            for a in range(2):
                if c == 0:
                    far, near = far_ref[a, 0, :, at], near_ref[a, 0, :, at]
                else:
                    far = jnp.where(position >= 2, far_ref[a, 1, :, at], far_ref[a, 0, :, at])
                    near = jnp.where(position >= 1, near_ref[a, 1, :, at], near_ref[a, 0, :, at])
                parts.append(jnp.concatenate([far, near, qkv_ref[1 + a, c, :, at]], axis=0))
            keys, values = parts
            scores = dot(qkv_ref[0, c, :, at], keys, ((1,), (1,))) * (1.0 / math.sqrt(ATT))
            scores = jnp.where(allowed, scores, -1e30)
            weights = jnp.exp(scores - jnp.max(scores, axis=1, keepdims=True))
            weights = weights / jnp.sum(weights, axis=1, keepdims=True)
            out_ref[c, :, at] = dot(weights, values)


def behind(block, distance):
    axes = ("z", "x", "yh")
    return lax.ppermute(block, axes, [((i - distance) % BLOCKS, i) for i in range(BLOCKS)])


def from_neighbours(block):
    return [block] + [lax.ppermute(block, "x", [((i - s) % NX, i) for i in range(NX)]) for s in range(1, NX)]


def back_to_neighbours(blocks):
    return [blocks[0]] + [
        lax.ppermute(blocks[s], "x", [(i, (i - s) % NX) for i in range(NX)]) for s in range(1, NX)
    ]


def exchange(pieces, axes):
    return lax.all_to_all(pieces, axes, split_axis=0, concat_axis=0, tiled=True)


def scalar(value):
    return jnp.reshape(value, (1,)).astype(jnp.int32)


def local(qkv, eta, fast_weights, momentum, ttt_gain):
    own_weights, own_moment = fast_weights.reshape(3 * ROWS, 1, H), momentum.reshape(3 * ROWS, 1, H)
    x = lax.axis_index("x")
    position = scalar((lax.axis_index("z") * NX + x) * NY + lax.axis_index("yh"))
    x = scalar(x)
    smem = {0: pl.BlockSpec(memory_space=pltpu.SMEM)}
    near = behind(qkv[1:], 1)
    far = behind(qkv[1:], 2)
    (send1,) = call(prepare_weights_body, [(BLOCKS, 24, LANES)], 1, own_weights, scratch=[(32, H)])
    pairs, queries = call(
        prepare_tokens_body, [(2 * TOK, D), (2 * TOK + 32, D)], 1, eta, qkv, own_moment, scratch=[(32, H)]
    )
    recv1 = exchange(send1, ("z", "x", "yh"))
    pairs = from_neighbours(pairs)
    queries = from_neighbours(queries)
    weights, send2 = call(
        gradient_body, [(3 * D, LANES), (BLOCKS * 24, LANES)], 5,
        recv1.reshape(BLOCKS * 24, LANES), *pairs, scratch=[(3 * D, LANES)],
    )
    recv2 = exchange(send2.reshape(NZ * NY, NX * 24, LANES), ("z", "yh"))
    (attended,) = call(attention_body, [(GROUPS, TOK, D)], 9, position, qkv, near, far, specs=smem)
    send3, moment = call(
        moment_body, [(NZ * NY, NX * 24, LANES), (NX * 24, LANES)], 1, x, recv2, *queries,
        specs=smem, after=(attended,),
    )
    recv3 = exchange(send3, ("z", "yh"))
    first = call(first_read_body, [(TOK, D)] * NX, 3, *queries, weights)
    (send_second,) = call(
        second_read_body, [(NX, TOK + 8, D)], 4,
        x, recv3.reshape(BLOCKS * 24, LANES), *queries, weights, moment, scratch=[(3 * D, LANES)],
        specs=smem, after=(first[0],),
    )
    second = exchange(send_second, "x")
    first = back_to_neighbours(first)
    readout, send5 = call(
        squares_body, [(GROUPS, TOK, D), (NARROW, 8, GROUPS * TOK)], 1, *first, second
    )
    recv5 = exchange(send5, "narrow")
    new_weights, new_moment = call(
        own_rows_body, [(3 * ROWS, 1, H), (3 * ROWS, 1, H)], 1, second, own_weights, scratch=[(32, H)]
    )
    (mixed,) = call(
        mix_body, [(GROUPS, TOK, D)], 1, recv5, readout, attended, ttt_gain.reshape(1, D), after=(new_weights,)
    )
    return mixed, new_weights.reshape(1, ROWS, 3, H), new_moment.reshape(1, ROWS, 3, H)


def solution(mesh):
    fine = Mesh(mesh.devices.reshape(NZ, NX, NY, NARROW), ("z", "x", "yh", "narrow"))
    wide = ("z", "x", "yh")
    return jax.shard_map(
        local,
        mesh=fine,
        in_specs=(
            P(None, None, wide, "narrow"),
            P("narrow", wide),
            P("narrow", wide, None, None),
            P("narrow", wide, None, None),
            P("narrow"),
        ),
        out_specs=(
            P(None, wide, "narrow"),
            P("narrow", wide, None, None),
            P("narrow", wide, None, None),
        ),
        check_vma=False,
    )
```

```python
import functools
import math

import jax
import jax.numpy as jnp
from jax import lax
from jax.experimental import pallas as pl
from jax.experimental.pallas import tpu as pltpu
from jax.sharding import Mesh
from jax.sharding import PartitionSpec as P

ATT = 128
WINDOW = 128
EPSILON = 1e-06
MOMENTUM_RATE = 0.9
STEP_SIZE = 0.03
PRECISION = lax.Precision.HIGHEST

NZ, NX, NY = 8, 4, 2
BLOCKS = NZ * NX * NY
ROWS = 10
SLICE = 96
LANES = 128
TOK = 64
D = 640
H = 384
NARROW = 8
GROUPS = 2
VMEM_LIMIT = 58 * 1024 * 1024
ROOM = 8 * 1024 * 1024


def dot(left, right, dims=((1,), (0,))):
    return lax.dot_general(
        left, right, (dims, ((), ())), precision=PRECISION, preferred_element_type=jnp.float32
    )


def entry(group, sublane):
    q = group * 8 + sublane
    return (q // 3, q % 3) if q < 3 * ROWS else None


def call(body, outs, micros, *args, lazy=(), after=(), scratch=(), smem=(), fan=(), room=0):
    vmem, anywhere = pl.BlockSpec(memory_space=pltpu.VMEM), pl.BlockSpec(memory_space=pl.ANY)
    held = [outs[n][1:] if n in fan else outs[n] for n in range(len(outs))]
    lazy_shapes = [a.shape if at is None else a.shape[1:] for a, at in lazy]
    sizes = (len(args), len(lazy), len(after), len(outs), len(outs), len(lazy), len(scratch))
    fetches = max(len(lazy), 1)
    sends = sum(outs[n][0] if n in fan else 1 for n in range(len(outs)))

    def kernel(*refs):
        split, at = [], 0
        for size in sizes:
            split.append(refs[at : at + size])
            at += size
        inputs, sources, _, targets, results, fetched, spare = split
        in_sems, out_sems = refs[at:]
        incoming = [
            pltpu.make_async_copy(ref if lazy[n][1] is None else ref.at[lazy[n][1]], fetched[n], in_sems.at[n])
            for n, ref in enumerate(sources)
        ]
        for copy in incoming:
            copy.start()
        outgoing, base = [], 0
        for n in range(len(outs)):
            places = [targets[n].at[j] for j in range(outs[n][0])] if n in fan else [targets[n]]
            outgoing.append(
                [pltpu.make_async_copy(results[n], place, out_sems.at[base + j]) for j, place in enumerate(places)]
            )
            base += len(places)
        sent = set()

        def need():
            for copy in incoming:
                copy.wait()

        def send(n):
            sent.add(n)
            for copy in outgoing[n]:
                copy.start()

        body(inputs, fetched, results, spare, need, send)
        for n in range(len(outs)):
            if n not in sent:
                send(n)
        for copies in outgoing:
            for copy in copies:
                copy.wait()

    return pl.pallas_call(
        kernel,
        out_shape=[jax.ShapeDtypeStruct(s, jnp.float32) for s in outs],
        in_specs=[pl.BlockSpec(memory_space=pltpu.SMEM) if n in smem else vmem for n in range(len(args))]
        + [anywhere] * (len(lazy) + len(after)),
        out_specs=[anywhere] * len(outs),
        scratch_shapes=[
            *(pltpu.VMEM(tuple(s), jnp.float32) for s in (*held, *lazy_shapes, *scratch)),
            pltpu.SemaphoreType.DMA((fetches,)),
            pltpu.SemaphoreType.DMA((sends,)),
        ],
        compiler_params=pltpu.CompilerParams(vmem_limit_bytes=VMEM_LIMIT - room),
        cost_estimate=pl.CostEstimate(flops=int(micros * 1e9), bytes_accessed=10**6, transcendentals=0),
    )(*args, *(a for a, _ in lazy), *after)


def to_column(row):
    n = row.shape[1]
    same = lax.broadcasted_iota(jnp.int32, (n, n), 0) == lax.broadcasted_iota(jnp.int32, (n, n), 1)
    return jnp.sum(jnp.where(same, row, 0.0), axis=1, keepdims=True)


def to_row(column):
    n = column.shape[0]
    same = lax.broadcasted_iota(jnp.int32, (n, n), 0) == lax.broadcasted_iota(jnp.int32, (n, n), 1)
    return jnp.sum(jnp.where(same, column, 0.0), axis=0, keepdims=True)


def own_packs(own_ref, flat_ref):
    flat_ref[24:32, :] = jnp.zeros((8, H), jnp.float32)
    for q in range(3 * ROWS):
        flat_ref[q : q + 1, :] = own_ref[q]
    return [
        jnp.concatenate(
            [flat_ref[8 * g : 8 * g + 8, SLICE * x : SLICE * (x + 1)] for g in range(4)], axis=1
        )
        for x in range(NX)
    ]


def prepare_weights_body(args, lazy, results, scratch, need, send):
    packs = own_packs(args[0], scratch[0])
    for z in range(NZ):
        for x in range(NX):
            for y in range(NY):
                for t in range(3):
                    results[0][(z * NX + x) * NY + y, 8 * t : 8 * t + 8, :] = packs[x][:, LANES * t : LANES * (t + 1)]


def prepare_pairs_body(args, lazy, results, scratch, need, send):
    eta_ref, qkv_ref = args
    results[0][0:TOK, :] = qkv_ref[1, 0]
    results[0][TOK : 2 * TOK, :] = to_column(eta_ref[...]) * qkv_ref[2, 0]


def prepare_queries_body(args, lazy, results, scratch, need, send):
    (mom_ref,), (qkv_ref,), (queries_ref, tail_ref) = args, lazy, results
    packs = own_packs(mom_ref, scratch[0])
    for x in range(NX):
        queries_ref[2 * TOK + 8 * x : 2 * TOK + 8 * x + 8, 0:H] = packs[x]
        queries_ref[2 * TOK + 8 * x : 2 * TOK + 8 * x + 8, H:D] = jnp.zeros((8, D - H), jnp.float32)
    need()
    queries_ref[0:TOK, :] = qkv_ref[0, 0]
    queries_ref[TOK : 2 * TOK, :] = qkv_ref[0, 1]
    send(0)
    for a in range(2):
        tail_ref[a] = qkv_ref[1 + a, 0]


def prepare_tails_body(args, lazy, results, scratch, need, send):
    (position_ref,), (qkv_ref,) = args, lazy
    position = position_ref[0]
    need()
    for distance, ref in zip((1, 2), results):
        for a in range(2):
            ref[a] = jnp.where(position >= BLOCKS - distance, qkv_ref[1 + a, 0], qkv_ref[1 + a, 1])


def widened(part):
    return jnp.concatenate([part, jnp.zeros((part.shape[0], LANES - SLICE), jnp.float32)], axis=1)


def unpack(recv_ref, out_ref, x_stride, y_stride, z_stride):
    for s in range(8):
        for x in range(NX):
            for y in range(NY):
                start = x * x_stride + y * y_stride + s
                rows = jnp.concatenate(
                    [recv_ref[pl.ds(start + 8 * t, NZ, stride=z_stride), :] for t in range(3)], axis=1
                )
                for g in range(4):
                    at = entry(g, s)
                    if at is None:
                        continue
                    r, i = at
                    out_ref[pl.ds(i * D + (x * NY + y) * ROWS + r, NZ, stride=NX * NY * ROWS), :] = widened(
                        rows[:, SLICE * g : SLICE * (g + 1)]
                    )


def pack(in_ref, send_ref, x_stride, y_stride, z_stride):
    for s in range(8):
        for x in range(NX):
            for y in range(NY):
                parts = []
                for g in range(4):
                    at = entry(g, s)
                    if at is None:
                        parts.append(jnp.zeros((NZ, SLICE), jnp.float32))
                        continue
                    r, i = at
                    parts.append(in_ref[pl.ds(i * D + (x * NY + y) * ROWS + r, NZ, stride=NX * NY * ROWS), :][:, :SLICE])
                rows = jnp.concatenate(parts, axis=1)
                start = x * x_stride + y * y_stride + s
                for t in range(3):
                    send_ref[pl.ds(start + 8 * t, NZ, stride=z_stride), :] = rows[:, LANES * t : LANES * (t + 1)]


def token_rows(refs, start):
    return jnp.concatenate([ref[start : start + TOK, :] for ref in refs], axis=0)


def matrix(ref, i):
    return ref[i * D : (i + 1) * D, :]


def gradient_body(args, pairs, results, scratch, need, send):
    (recv_ref,), (w_ref, send_ref), (g_ref,) = args, results, scratch
    unpack(recv_ref, w_ref, 48, 24, 192)
    send(0)
    need()
    keys = token_rows(pairs, 0)
    weighted = token_rows(pairs, TOK)
    pre = dot(keys, jnp.concatenate([matrix(w_ref, 0), matrix(w_ref, 1)], axis=1))
    gate_pre, up_pre = pre[:, :LANES], pre[:, LANES:]
    back = -dot(weighted, matrix(w_ref, 2))
    sigmoid = jax.nn.sigmoid(gate_pre)
    gated = gate_pre * sigmoid
    hidden = gated * up_pre
    gate_back = back * up_pre * sigmoid * (1.0 + gate_pre * (1.0 - sigmoid))
    up_back = back * gated
    both = dot(keys, jnp.concatenate([gate_back, up_back], axis=1), ((0,), (0,)))
    g_ref[0:D, :] = both[:, :LANES]
    g_ref[D : 2 * D, :] = both[:, LANES:]
    g_ref[2 * D : 3 * D, :] = -dot(weighted, hidden, ((0,), (0,)))
    pack(g_ref, send_ref, 24, 96, 192)


def source(x_ref, s):
    return lax.rem(x_ref[0] + NX - s, NX)


def moment_body(args, queries, results, scratch, need, send):
    (x_ref, recv_ref), (own_ref,) = args, results
    total = recv_ref[0]
    for j in range(1, NZ * NY):
        total = total + recv_ref[j]
    own_ref[...] = total
    need()
    mine = pl.ds(pl.multiple_of(2 * TOK + 8 * x_ref[0], 8), 8)
    for s, ref in enumerate(queries):
        old = ref[mine, :]
        old = jnp.concatenate([old[:, LANES * t : LANES * (t + 1)] for t in range(3)], axis=0)
        rows = pl.ds(pl.multiple_of(24 * source(x_ref, s), 8), 24)
        own_ref[rows, :] = own_ref[rows, :] + MOMENTUM_RATE * old


def hidden_of(inputs, w1, w3):
    pre = dot(inputs, jnp.concatenate([w1, w3], axis=1))
    gate_pre, up_pre = pre[:, :LANES], pre[:, LANES:]
    return gate_pre * jax.nn.sigmoid(gate_pre) * up_pre


def first_read_body(args, lazy, results, scratch, need, send):
    need()
    *queries, w_ref = lazy
    hidden = hidden_of(token_rows(queries, 0), matrix(w_ref, 0), matrix(w_ref, 1))
    partial = dot(hidden, matrix(w_ref, 2), ((1,), (1,)))
    for s in range(NX):
        results[s][...] = partial[s * TOK : (s + 1) * TOK]


def renormalized(weights, moment):
    rate = STEP_SIZE / jnp.sqrt(jnp.mean(moment * moment, axis=0, keepdims=True) + EPSILON)
    moved = weights - moment * rate
    ratio = jnp.sqrt(jnp.mean(weights * weights, axis=0, keepdims=True) + EPSILON) / jnp.sqrt(
        jnp.mean(moved * moved, axis=0, keepdims=True) + EPSILON
    )
    return moved * ratio, rate, ratio


def second_read_body(args, lazy, results, scratch, need, send):
    (x_ref, recv_ref), (*queries, w_ref, moment_ref), (send_ref,), (m_ref,) = args, lazy, results, scratch
    unpack(recv_ref, m_ref, 24, 96, 192)
    need()
    new1, rate1, ratio1 = renormalized(matrix(w_ref, 0), matrix(m_ref, 0))
    new3, rate3, ratio3 = renormalized(matrix(w_ref, 1), matrix(m_ref, 1))
    new2, rate2, ratio2 = renormalized(matrix(w_ref, 2), matrix(m_ref, 2))
    hidden = hidden_of(token_rows(queries, TOK), new1, new3)
    partial = dot(hidden, new2, ((1,), (1,)))
    stats = [rate1, rate3, rate2, ratio1, ratio3, ratio2, jnp.zeros((2, LANES), jnp.float32)]
    stats = jnp.concatenate(stats, axis=0)
    for x in range(NX):
        tail = [stats, *(moment_ref[24 * x + 8 * t : 24 * x + 8 * t + 8, :] for t in range(3))]
        tail.append(jnp.zeros((8, LANES), jnp.float32))
        send_ref[x, TOK : TOK + 8, :] = jnp.concatenate(tail, axis=1)
    for s in range(NX):
        send_ref[source(x_ref, s), 0:TOK, :] = partial[s * TOK : (s + 1) * TOK]


def squares_body(args, lazy, results, scratch, need, send):
    (second_ref,), (readout_ref, send_ref) = args, results
    need()
    first = lazy[0][...] + lazy[1][...] + lazy[2][...] + lazy[3][...]
    second = second_ref[0, 0:TOK, :]
    for x in range(1, NX):
        second = second + second_ref[x, 0:TOK, :]
    readout_ref[0] = first
    readout_ref[1] = second
    row = jnp.concatenate(
        [to_row(jnp.sum(total * total, axis=1, keepdims=True)) for total in (first, second)], axis=1
    )
    send_ref[...] = jnp.broadcast_to(row, (8, GROUPS * TOK))


def own_rows_body(args, lazy, results, scratch, need, send):
    (second_ref, fw_ref), (new_w_ref, new_m_ref), (flat_ref,) = args, results, scratch
    for g in range(4):
        flat_ref[8 * g : 8 * g + 8, :] = jnp.concatenate(
            [
                second_ref[x, TOK : TOK + 8, LANES + SLICE * g : LANES + SLICE * (g + 1)]
                for x in range(NX)
            ],
            axis=1,
        )
    stats = jnp.concatenate([second_ref[x, TOK : TOK + 8, 0:SLICE] for x in range(NX)], axis=1)
    for q in range(3 * ROWS):
        i = q % 3
        moment = flat_ref[q : q + 1, :]
        new_m_ref[q] = moment
        new_w_ref[q] = (fw_ref[q] - moment * stats[i : i + 1]) * stats[3 + i : 4 + i]


def mix_body(args, lazy, results, scratch, need, send):
    (recv_ref, gain_ref), (readout_ref, *attended_refs), (mixed_ref,) = args, lazy, results
    total = recv_ref[0, 0:1, :]
    for n in range(1, NARROW):
        total = total + recv_ref[n, 0:1, :]
    scale = to_column(1.0 / jnp.sqrt(total / (D * NARROW) + EPSILON))
    need()
    for c in range(GROUPS):
        mixed_ref[c] = attended_refs[c][...] + gain_ref[...] * (readout_ref[c] * scale[c * TOK : (c + 1) * TOK])


def attention_body(c, args, lazy, results, scratch, need, send):
    (position_ref,), (qkv_ref, near_ref, far_ref), (out_ref,) = args, lazy, results
    position = position_ref[0]
    row = lax.broadcasted_iota(jnp.int32, (TOK, 3 * TOK), 0) + 2 * TOK
    col = lax.broadcasted_iota(jnp.int32, (TOK, 3 * TOK), 1)
    allowed = (row - col >= 0) & (row - col < WINDOW)
    if c == 0:
        first = jnp.where(position >= 2, 0, jnp.where(position >= 1, TOK, 2 * TOK))
        allowed = allowed & (col >= first)
    need()
    for h in range(D // ATT):
        at = slice(h * ATT, (h + 1) * ATT)
        keys, values = (
            jnp.concatenate([far_ref[a, :, at], near_ref[a, :, at], qkv_ref[1 + a, c, :, at]], axis=0)
            for a in range(2)
        )
        scores = dot(qkv_ref[0, c, :, at], keys, ((1,), (1,))) * (1.0 / math.sqrt(ATT))
        scores = jnp.where(allowed, scores, -1e30)
        weights = jnp.exp(scores - jnp.max(scores, axis=1, keepdims=True))
        weights = weights / jnp.sum(weights, axis=1, keepdims=True)
        out_ref[:, at] = dot(weights, values)


def behind(block, distance):
    axes = ("z", "x", "yh")
    return lax.ppermute(block, axes, [((i - distance) % BLOCKS, i) for i in range(BLOCKS)])


def from_neighbours(block):
    return [block] + [lax.ppermute(block, "x", [((i - s) % NX, i) for i in range(NX)]) for s in range(1, NX)]


def back_to_neighbours(blocks):
    return [blocks[0]] + [
        lax.ppermute(blocks[s], "x", [(i, (i - s) % NX) for i in range(NX)]) for s in range(1, NX)
    ]


def exchange(pieces, axes):
    return lax.all_to_all(pieces, axes, split_axis=0, concat_axis=0, tiled=True)


def scalar(value):
    return jnp.reshape(value, (1,)).astype(jnp.int32)


def whole(*arrays):
    return [(a, None) for a in arrays]


def local(qkv, eta, fast_weights, momentum, ttt_gain):
    own_weights, own_moment = fast_weights.reshape(3 * ROWS, 1, H), momentum.reshape(3 * ROWS, 1, H)
    x = lax.axis_index("x")
    position = scalar((lax.axis_index("z") * NX + x) * NY + lax.axis_index("yh"))
    x = scalar(x)
    everyone, cross = ("z", "x", "yh"), ("z", "yh")
    (send1,) = call(prepare_weights_body, [(BLOCKS, 24, LANES)], 1, own_weights, scratch=[(32, H)])
    (pairs,) = call(prepare_pairs_body, [(2 * TOK, D)], 1, eta, qkv)
    recv1 = exchange(send1, everyone).reshape(BLOCKS * 24, LANES)
    pairs = from_neighbours(pairs)
    weights, send2 = call(
        gradient_body, [(3 * D, LANES), (BLOCKS * 24, LANES)], 5, recv1, lazy=whole(*pairs),
        scratch=[(3 * D, LANES)], room=ROOM - 1024 * 1024,
    )
    recv2 = exchange(send2.reshape(NZ * NY, NX * 24, LANES), cross)
    queries, tail = call(
        prepare_queries_body, [(2 * TOK + 32, D), (2, TOK, D)], 1, own_moment, lazy=whole(qkv), scratch=[(32, H)],
        after=(weights,),
    )
    queries = from_neighbours(queries)
    near0, far0 = behind(tail, 1), behind(tail, 2)
    (send3,) = call(
        moment_body, [(NZ * NY, NX * 24, LANES)], 2, x, recv2, lazy=whole(*queries), smem=(0,), fan=(0,), room=ROOM
    )
    recv3 = exchange(send3, cross).reshape(BLOCKS * 24, LANES)
    near1, far1 = call(
        prepare_tails_body, [(2, TOK, D)] * 2, 1, position, lazy=whole(qkv), smem=(0,), after=(send3,)
    )
    near1, far1 = behind(near1, 1), behind(far1, 2)
    first = back_to_neighbours(
        call(first_read_body, [(TOK, D)] * NX, 4, lazy=whole(*queries, weights), after=(send3,))
    )
    (attended0,) = call(
        functools.partial(attention_body, 0), [(TOK, D)], 4, position, lazy=whole(qkv, near0, far0), smem=(0,),
        after=(send3,),
    )
    (send_second,) = call(
        second_read_body, [(NX, TOK + 8, D)], 5, x, recv3,
        lazy=[*whole(*queries, weights), (send3, 0)], scratch=[(3 * D, LANES)], smem=(0,),
        after=(*first[1:], attended0), room=ROOM,
    )
    second = exchange(send_second, "x")
    (attended1,) = call(
        functools.partial(attention_body, 1), [(TOK, D)], 4, position, lazy=whole(qkv, near1, far1), smem=(0,),
        after=(send_second,),
    )
    readout, send5 = call(
        squares_body, [(GROUPS, TOK, D), (NARROW, 8, GROUPS * TOK)], 1, second, lazy=whole(*first), fan=(1,),
        after=(attended1,), room=ROOM,
    )
    recv5 = exchange(send5, "narrow")
    new_weights, new_moment = call(
        own_rows_body, [(3 * ROWS, 1, H), (3 * ROWS, 1, H)], 1, second, own_weights, scratch=[(32, H)],
        after=(send5,),
    )
    (mixed,) = call(
        mix_body, [(GROUPS, TOK, D)], 1, recv5, ttt_gain.reshape(1, D), lazy=whole(readout, attended0, attended1),
        after=(new_weights,), room=ROOM,
    )
    return mixed, new_weights.reshape(1, ROWS, 3, H), new_moment.reshape(1, ROWS, 3, H)


def solution(mesh):
    fine = Mesh(mesh.devices.reshape(NZ, NX, NY, NARROW), ("z", "x", "yh", "narrow"))
    wide = ("z", "x", "yh")
    return jax.shard_map(
        local,
        mesh=fine,
        in_specs=(
            P(None, None, wide, "narrow"),
            P("narrow", wide),
            P("narrow", wide, None, None),
            P("narrow", wide, None, None),
            P("narrow"),
        ),
        out_specs=(
            P(None, wide, "narrow"),
            P("narrow", wide, None, None),
            P("narrow", wide, None, None),
        ),
        check_vma=False,
    )
```

```python
import functools
import math

import jax
import jax.numpy as jnp
from jax import lax
from jax.experimental import pallas as pl
from jax.experimental.pallas import tpu as pltpu
from jax.sharding import Mesh
from jax.sharding import PartitionSpec as P

ATT = 128
WINDOW = 128
EPSILON = 1e-06
MOMENTUM_RATE = 0.9
STEP_SIZE = 0.03
PRECISION = lax.Precision.HIGHEST

NZ, NX, NY = 8, 4, 2
BLOCKS = NZ * NX * NY
ROWS = 10
SLICE = 96
LANES = 128
TOK = 64
D = 640
H = 384
NARROW = 8
GROUPS = 2
VMEM_LIMIT = 58 * 1024 * 1024
ROOM = 8 * 1024 * 1024
SMALL = 42 * 1024 * 1024


def dot(left, right, dims=((1,), (0,))):
    return lax.dot_general(
        left, right, (dims, ((), ())), precision=PRECISION, preferred_element_type=jnp.float32
    )


def entry(group, sublane):
    q = group * 8 + sublane
    return (q // 3, q % 3) if q < 3 * ROWS else None


def call(body, outs, micros, *args, lazy=(), after=(), scratch=(), smem=(), fan=(), room=0):
    vmem, anywhere = pl.BlockSpec(memory_space=pltpu.VMEM), pl.BlockSpec(memory_space=pl.ANY)
    held = [outs[n][1:] if n in fan else outs[n] for n in range(len(outs))]
    lazy_shapes = [a.shape if at is None else (at[1], *a.shape[1:]) for a, at in lazy]
    sizes = (len(args), len(lazy), len(after), len(outs), len(outs), len(lazy), len(scratch))
    fetches = max(len(lazy), 1)
    sends = sum(outs[n][0] if n in fan else 1 for n in range(len(outs)))

    def kernel(*refs):
        split, at = [], 0
        for size in sizes:
            split.append(refs[at : at + size])
            at += size
        inputs, sources, _, targets, results, fetched, spare = split
        in_sems, out_sems = refs[at:]
        incoming = [
            pltpu.make_async_copy(ref if lazy[n][1] is None else ref.at[pl.ds(*lazy[n][1])], fetched[n], in_sems.at[n])
            for n, ref in enumerate(sources)
        ]
        for copy in incoming:
            copy.start()
        outgoing, base = [], 0
        for n in range(len(outs)):
            places = [targets[n].at[j] for j in range(outs[n][0])] if n in fan else [targets[n]]
            outgoing.append(
                [pltpu.make_async_copy(results[n], place, out_sems.at[base + j]) for j, place in enumerate(places)]
            )
            base += len(places)
        sent = set()

        def need():
            for copy in incoming:
                copy.wait()

        def send(n):
            sent.add(n)
            for copy in outgoing[n]:
                copy.start()

        body(inputs, fetched, results, spare, need, send)
        for n in range(len(outs)):
            if n not in sent:
                send(n)
        for copies in outgoing:
            for copy in copies:
                copy.wait()

    return pl.pallas_call(
        kernel,
        out_shape=[jax.ShapeDtypeStruct(s, jnp.float32) for s in outs],
        in_specs=[pl.BlockSpec(memory_space=pltpu.SMEM) if n in smem else vmem for n in range(len(args))]
        + [anywhere] * (len(lazy) + len(after)),
        out_specs=[anywhere] * len(outs),
        scratch_shapes=[
            *(pltpu.VMEM(tuple(s), jnp.float32) for s in (*held, *lazy_shapes, *scratch)),
            pltpu.SemaphoreType.DMA((fetches,)),
            pltpu.SemaphoreType.DMA((sends,)),
        ],
        compiler_params=pltpu.CompilerParams(vmem_limit_bytes=VMEM_LIMIT - room),
        cost_estimate=pl.CostEstimate(flops=int(micros * 1e9), bytes_accessed=10**6, transcendentals=0),
    )(*args, *(a for a, _ in lazy), *after)


def to_column(row):
    n = row.shape[1]
    same = lax.broadcasted_iota(jnp.int32, (n, n), 0) == lax.broadcasted_iota(jnp.int32, (n, n), 1)
    return jnp.sum(jnp.where(same, row, 0.0), axis=1, keepdims=True)


def to_row(column):
    n = column.shape[0]
    same = lax.broadcasted_iota(jnp.int32, (n, n), 0) == lax.broadcasted_iota(jnp.int32, (n, n), 1)
    return jnp.sum(jnp.where(same, column, 0.0), axis=0, keepdims=True)


def own_packs(own_ref, flat_ref):
    flat_ref[24:32, :] = jnp.zeros((8, H), jnp.float32)
    for q in range(3 * ROWS):
        flat_ref[q : q + 1, :] = own_ref[q]
    return [
        jnp.concatenate(
            [flat_ref[8 * g : 8 * g + 8, SLICE * x : SLICE * (x + 1)] for g in range(4)], axis=1
        )
        for x in range(NX)
    ]


def prepare_packs_body(args, lazy, results, scratch, need, send):
    for half, ref in enumerate(args):
        for x, block in enumerate(own_packs(ref, scratch[0])):
            for y in range(NY):
                for t in range(3):
                    rows = slice(24 * half + 8 * t, 24 * half + 8 * t + 8)
                    results[0][x * NY + y, rows, :] = block[:, LANES * t : LANES * (t + 1)]


def spread_body(args, lazy, results, scratch, need, send):
    results[0][...] = args[0][:, 0:24, :]


def prepare_pairs_body(args, lazy, results, scratch, need, send):
    eta_ref, qkv_ref = args
    results[0][0:TOK, :] = qkv_ref[1, 0]
    results[0][TOK : 2 * TOK, :] = to_column(eta_ref[...]) * qkv_ref[2, 0]


def prepare_queries_body(args, lazy, results, scratch, need, send):
    need()
    (queries_ref,) = results
    queries_ref[0:TOK, :] = lazy[0][0, 0]
    queries_ref[TOK : 2 * TOK, :] = lazy[0][0, 1]


def widened(part):
    return jnp.concatenate([part, jnp.zeros((part.shape[0], LANES - SLICE), jnp.float32)], axis=1)


def unpack(recv_ref, out_ref, x_stride, y_stride, z_stride):
    for s in range(8):
        for x in range(NX):
            for y in range(NY):
                start = x * x_stride + y * y_stride + s
                rows = jnp.concatenate(
                    [recv_ref[pl.ds(start + 8 * t, NZ, stride=z_stride), :] for t in range(3)], axis=1
                )
                for g in range(4):
                    at = entry(g, s)
                    if at is None:
                        continue
                    r, i = at
                    out_ref[pl.ds(i * D + (x * NY + y) * ROWS + r, NZ, stride=NX * NY * ROWS), :] = widened(
                        rows[:, SLICE * g : SLICE * (g + 1)]
                    )


def pack(in_ref, send_ref, x_stride, y_stride, z_stride):
    for s in range(8):
        for x in range(NX):
            for y in range(NY):
                parts = []
                for g in range(4):
                    at = entry(g, s)
                    if at is None:
                        parts.append(jnp.zeros((NZ, SLICE), jnp.float32))
                        continue
                    r, i = at
                    parts.append(in_ref[pl.ds(i * D + (x * NY + y) * ROWS + r, NZ, stride=NX * NY * ROWS), :][:, :SLICE])
                rows = jnp.concatenate(parts, axis=1)
                start = x * x_stride + y * y_stride + s
                for t in range(3):
                    send_ref[pl.ds(start + 8 * t, NZ, stride=z_stride), :] = rows[:, LANES * t : LANES * (t + 1)]


def token_rows(refs, start):
    return jnp.concatenate([ref[start : start + TOK, :] for ref in refs], axis=0)


def matrix(ref, i):
    return ref[i * D : (i + 1) * D, :]


def gradient_body(args, pairs, results, scratch, need, send):
    (recv_ref,), (w_ref, send_ref), (g_ref,) = args, results, scratch
    unpack(recv_ref, w_ref, 48, 24, 192)
    send(0)
    need()
    keys = token_rows(pairs, 0)
    weighted = token_rows(pairs, TOK)
    pre = dot(keys, jnp.concatenate([matrix(w_ref, 0), matrix(w_ref, 1)], axis=1))
    gate_pre, up_pre = pre[:, :LANES], pre[:, LANES:]
    back = -dot(weighted, matrix(w_ref, 2))
    sigmoid = jax.nn.sigmoid(gate_pre)
    gated = gate_pre * sigmoid
    hidden = gated * up_pre
    gate_back = back * up_pre * sigmoid * (1.0 + gate_pre * (1.0 - sigmoid))
    up_back = back * gated
    both = dot(keys, jnp.concatenate([gate_back, up_back], axis=1), ((0,), (0,)))
    g_ref[0:D, :] = both[:, :LANES]
    g_ref[D : 2 * D, :] = both[:, LANES:]
    g_ref[2 * D : 3 * D, :] = -dot(weighted, hidden, ((0,), (0,)))
    pack(g_ref, send_ref, 24, 96, 192)


def source(x_ref, s):
    return lax.rem(x_ref[0] + NX - s, NX)


def moment_body(args, lazy, results, scratch, need, send):
    (yh_ref, recv_ref, packs_ref), (own_ref,) = args, results
    total = recv_ref[0]
    for j in range(1, NZ * NY):
        total = total + recv_ref[j]
    old = jnp.concatenate([packs_ref[x * NY + yh_ref[0], 24:48, :] for x in range(NX)], axis=0)
    own_ref[...] = total + MOMENTUM_RATE * old


def hidden_of(inputs, w1, w3):
    pre = dot(inputs, jnp.concatenate([w1, w3], axis=1))
    gate_pre, up_pre = pre[:, :LANES], pre[:, LANES:]
    return gate_pre * jax.nn.sigmoid(gate_pre) * up_pre


def first_read_body(args, lazy, results, scratch, need, send):
    need()
    *queries, w_ref = lazy
    hidden = hidden_of(token_rows(queries, 0), matrix(w_ref, 0), matrix(w_ref, 1))
    partial = dot(hidden, matrix(w_ref, 2), ((1,), (1,)))
    for s in range(NX):
        results[s][...] = partial[s * TOK : (s + 1) * TOK]


def renormalized(weights, moment):
    rate = STEP_SIZE / jnp.sqrt(jnp.mean(moment * moment, axis=0, keepdims=True) + EPSILON)
    moved = weights - moment * rate
    ratio = jnp.sqrt(jnp.mean(weights * weights, axis=0, keepdims=True) + EPSILON) / jnp.sqrt(
        jnp.mean(moved * moved, axis=0, keepdims=True) + EPSILON
    )
    return moved * ratio, rate, ratio


def second_read_body(args, lazy, results, scratch, need, send):
    (x_ref, recv_ref), (*queries, w_ref, moment_ref), (send_ref,), (m_ref,) = args, lazy, results, scratch
    unpack(recv_ref, m_ref, 24, 96, 192)
    need()
    new1, rate1, ratio1 = renormalized(matrix(w_ref, 0), matrix(m_ref, 0))
    new3, rate3, ratio3 = renormalized(matrix(w_ref, 1), matrix(m_ref, 1))
    new2, rate2, ratio2 = renormalized(matrix(w_ref, 2), matrix(m_ref, 2))
    hidden = hidden_of(token_rows(queries, 0), new1, new3)
    partial = dot(hidden, new2, ((1,), (1,)))
    stats = [rate1, rate3, rate2, ratio1, ratio3, ratio2, jnp.zeros((2, LANES), jnp.float32)]
    stats = jnp.concatenate(stats, axis=0)
    for x in range(NX):
        tail = [stats, *(moment_ref[0, 24 * x + 8 * t : 24 * x + 8 * t + 8, :] for t in range(3))]
        tail.append(jnp.zeros((8, LANES), jnp.float32))
        send_ref[x, TOK : TOK + 8, :] = jnp.concatenate(tail, axis=1)
    for s in range(NX):
        send_ref[source(x_ref, s), 0:TOK, :] = partial[s * TOK : (s + 1) * TOK]


def squares_body(args, lazy, results, scratch, need, send):
    (second_ref,), (readout_ref, send_ref) = args, results
    need()
    first = lazy[0][...] + lazy[1][...] + lazy[2][...] + lazy[3][...]
    second = second_ref[0, 0:TOK, :]
    for x in range(1, NX):
        second = second + second_ref[x, 0:TOK, :]
    readout_ref[0] = first
    readout_ref[1] = second
    row = jnp.concatenate(
        [to_row(jnp.sum(total * total, axis=1, keepdims=True)) for total in (first, second)], axis=1
    )
    send_ref[...] = jnp.broadcast_to(row, (8, GROUPS * TOK))


def own_rows_body(args, lazy, results, scratch, need, send):
    (second_ref, fw_ref), (new_w_ref, new_m_ref), (flat_ref,) = args, results, scratch
    for g in range(4):
        flat_ref[8 * g : 8 * g + 8, :] = jnp.concatenate(
            [
                second_ref[x, TOK : TOK + 8, LANES + SLICE * g : LANES + SLICE * (g + 1)]
                for x in range(NX)
            ],
            axis=1,
        )
    stats = jnp.concatenate([second_ref[x, TOK : TOK + 8, 0:SLICE] for x in range(NX)], axis=1)
    for q in range(3 * ROWS):
        i = q % 3
        moment = flat_ref[q : q + 1, :]
        new_m_ref[q] = moment
        new_w_ref[q] = (fw_ref[q] - moment * stats[i : i + 1]) * stats[3 + i : 4 + i]


def mix_body(args, lazy, results, scratch, need, send):
    (recv_ref, gain_ref, readout_ref, attended_ref), (mixed_ref,) = args, results
    total = recv_ref[0, 0:1, :]
    for n in range(1, NARROW):
        total = total + recv_ref[n, 0:1, :]
    scale = to_column(1.0 / jnp.sqrt(total / (D * NARROW) + EPSILON))
    for c in range(GROUPS):
        mixed_ref[c] = attended_ref[c] + gain_ref[...] * (readout_ref[c] * scale[c * TOK : (c + 1) * TOK])


def attention_body(args, lazy, results, scratch, need, send):
    (position_ref,), (qkv_ref, near_ref, far_ref), (out_ref,) = args, lazy, results
    position = position_ref[0]
    row = lax.broadcasted_iota(jnp.int32, (TOK, 3 * TOK), 0) + 2 * TOK
    col = lax.broadcasted_iota(jnp.int32, (TOK, 3 * TOK), 1)
    window = (row - col >= 0) & (row - col < WINDOW)
    first = jnp.where(position >= 2, 0, jnp.where(position >= 1, TOK, 2 * TOK))
    need()
    for c in range(GROUPS):
        allowed = window & (col >= first) if c == 0 else window
        for h in range(D // ATT):
            at = slice(h * ATT, (h + 1) * ATT)
            parts = []
            for a in range(2):
                far, near = far_ref[a, c, :, at], near_ref[a, c, :, at]
                if c == 1:
                    far = jnp.where(position >= 2, far, far_ref[a, 0, :, at])
                    near = jnp.where(position >= 1, near, near_ref[a, 0, :, at])
                parts.append(jnp.concatenate([far, near, qkv_ref[1 + a, c, :, at]], axis=0))
            keys, values = parts
            scores = dot(qkv_ref[0, c, :, at], keys, ((1,), (1,))) * (1.0 / math.sqrt(ATT))
            scores = jnp.where(allowed, scores, -1e30)
            weights = jnp.exp(scores - jnp.max(scores, axis=1, keepdims=True))
            weights = weights / jnp.sum(weights, axis=1, keepdims=True)
            out_ref[c, :, at] = dot(weights, values)


def behind(block, distance):
    axes = ("z", "x", "yh")
    return lax.ppermute(block, axes, [((i - distance) % BLOCKS, i) for i in range(BLOCKS)])


def from_neighbours(block):
    return [block] + [lax.ppermute(block, "x", [((i - s) % NX, i) for i in range(NX)]) for s in range(1, NX)]


def back_to_neighbours(blocks):
    return [blocks[0]] + [
        lax.ppermute(blocks[s], "x", [(i, (i - s) % NX) for i in range(NX)]) for s in range(1, NX)
    ]


def exchange(pieces, axes):
    return lax.all_to_all(pieces, axes, split_axis=0, concat_axis=0, tiled=True)


def scalar(value):
    return jnp.reshape(value, (1,)).astype(jnp.int32)


def whole(*arrays):
    return [(a, None) for a in arrays]


def local(qkv, eta, fast_weights, momentum, ttt_gain):
    own_weights, own_moment = fast_weights.reshape(3 * ROWS, 1, H), momentum.reshape(3 * ROWS, 1, H)
    x, yh = lax.axis_index("x"), lax.axis_index("yh")
    position = scalar((lax.axis_index("z") * NX + x) * NY + yh)
    x, yh = scalar(x), scalar(yh)
    (packs,) = call(
        prepare_packs_body, [(NX * NY, 48, LANES)], 1, own_weights, own_moment, scratch=[(32, H)], room=SMALL
    )
    (pairs,) = call(prepare_pairs_body, [(2 * TOK, D)], 1, eta, qkv, room=SMALL)
    packs = exchange(packs, ("x", "yh"))
    (spread,) = call(spread_body, [(NZ, NX * NY, 24, LANES)], 1, packs, fan=(0,), room=SMALL)
    recv1 = exchange(spread.reshape(NZ, NX * NY * 24, LANES), "z").reshape(BLOCKS * 24, LANES)
    pairs = from_neighbours(pairs)
    near, far = behind(qkv[1:], 1), behind(qkv[1:], 2)
    weights, send2 = call(
        gradient_body, [(3 * D, LANES), (BLOCKS * 24, LANES)], 5, recv1, lazy=whole(*pairs),
        scratch=[(3 * D, LANES)], room=ROOM - 1024 * 1024,
    )
    recv2 = exchange(send2.reshape(NZ * NY, NX * 24, LANES), ("z", "yh"))
    (queries,) = call(prepare_queries_body, [(2 * TOK, D)], 1, lazy=[(qkv, (0, 1))], after=(weights,))
    queries = from_neighbours(queries)
    (attended,) = call(
        attention_body, [(GROUPS, TOK, D)], 8, position, lazy=whole(qkv, near, far), smem=(0,)
    )
    (send3,) = call(
        moment_body, [(NZ * NY, NX * 24, LANES)], 2, yh, recv2, packs, smem=(0,), fan=(0,),
        after=(attended, *queries[1:]),
        room=ROOM,
    )
    recv3 = exchange(send3, ("z", "yh")).reshape(BLOCKS * 24, LANES)
    first = back_to_neighbours(
        call(
            first_read_body, [(TOK, D)] * NX, 4, lazy=[*((q, (0, TOK)) for q in queries), (weights, None)],
            after=(send3,),
        )
    )
    (send_second,) = call(
        second_read_body, [(NX, TOK + 8, D)], 5, x, recv3,
        lazy=[*((q, (TOK, TOK)) for q in queries), (weights, None), (send3, (0, 1))], scratch=[(3 * D, LANES)],
        smem=(0,), after=first[1:], room=ROOM,
    )
    second = exchange(send_second, "x")
    readout, send5 = call(
        squares_body, [(GROUPS, TOK, D), (NARROW, 8, GROUPS * TOK)], 1, second, lazy=whole(*first), fan=(1,),
        room=SMALL,
    )
    recv5 = exchange(send5, "narrow")
    new_weights, new_moment = call(
        own_rows_body, [(3 * ROWS, 1, H), (3 * ROWS, 1, H)], 1, second, own_weights, scratch=[(32, H)],
        after=(send5,), room=SMALL,
    )
    (mixed,) = call(
        mix_body, [(GROUPS, TOK, D)], 1, recv5, ttt_gain.reshape(1, D), readout, attended, after=(new_weights,),
        room=SMALL,
    )
    return mixed, new_weights.reshape(1, ROWS, 3, H), new_moment.reshape(1, ROWS, 3, H)


def solution(mesh):
    fine = Mesh(mesh.devices.reshape(NZ, NX, NY, NARROW), ("z", "x", "yh", "narrow"))
    wide = ("z", "x", "yh")
    return jax.shard_map(
        local,
        mesh=fine,
        in_specs=(
            P(None, None, wide, "narrow"),
            P("narrow", wide),
            P("narrow", wide, None, None),
            P("narrow", wide, None, None),
            P("narrow"),
        ),
        out_specs=(
            P(None, wide, "narrow"),
            P("narrow", wide, None, None),
            P("narrow", wide, None, None),
        ),
        check_vma=False,
    )
```

```python
import functools
import math

import jax
import jax.numpy as jnp
from jax import lax
from jax.experimental import pallas as pl
from jax.experimental.pallas import tpu as pltpu
from jax.sharding import Mesh
from jax.sharding import PartitionSpec as P

ATT = 128
WINDOW = 128
EPSILON = 1e-06
MOMENTUM_RATE = 0.9
STEP_SIZE = 0.03
PRECISION = lax.Precision.HIGHEST

NZ, NX, NY = 8, 4, 2
BLOCKS = NZ * NX * NY
ROWS = 10
SLICE = 96
LANES = 128
TOK = 64
D = 640
H = 384
NARROW = 8
GROUPS = 2
VMEM_LIMIT = 58 * 1024 * 1024
ROOM = 8 * 1024 * 1024
SMALL = 42 * 1024 * 1024


def dot(left, right, dims=((1,), (0,))):
    return lax.dot_general(
        left, right, (dims, ((), ())), precision=PRECISION, preferred_element_type=jnp.float32
    )


def entry(group, sublane):
    q = group * 8 + sublane
    return (q // 3, q % 3) if q < 3 * ROWS else None


def call(body, outs, micros, *args, lazy=(), after=(), scratch=(), smem=(), fan=(), room=0):
    vmem, anywhere = pl.BlockSpec(memory_space=pltpu.VMEM), pl.BlockSpec(memory_space=pl.ANY)
    held = [outs[n][1:] if n in fan else outs[n] for n in range(len(outs))]
    lazy_shapes = [a.shape if at is None else (at[1], *a.shape[1:]) for a, at in lazy]
    sizes = (len(args), len(lazy), len(after), len(outs), len(outs), len(lazy), len(scratch))
    fetches = max(len(lazy), 1)
    sends = sum(outs[n][0] if n in fan else 1 for n in range(len(outs)))

    def kernel(*refs):
        split, at = [], 0
        for size in sizes:
            split.append(refs[at : at + size])
            at += size
        inputs, sources, _, targets, results, fetched, spare = split
        in_sems, out_sems = refs[at:]
        incoming = [
            pltpu.make_async_copy(ref if lazy[n][1] is None else ref.at[pl.ds(*lazy[n][1])], fetched[n], in_sems.at[n])
            for n, ref in enumerate(sources)
        ]
        for copy in incoming:
            copy.start()
        outgoing, base = [], 0
        for n in range(len(outs)):
            places = [targets[n].at[j] for j in range(outs[n][0])] if n in fan else [targets[n]]
            outgoing.append(
                [pltpu.make_async_copy(results[n], place, out_sems.at[base + j]) for j, place in enumerate(places)]
            )
            base += len(places)
        sent = set()

        def need():
            for copy in incoming:
                copy.wait()

        def send(n):
            sent.add(n)
            for copy in outgoing[n]:
                copy.start()

        body(inputs, fetched, results, spare, need, send)
        for n in range(len(outs)):
            if n not in sent:
                send(n)
        for copies in outgoing:
            for copy in copies:
                copy.wait()

    return pl.pallas_call(
        kernel,
        out_shape=[jax.ShapeDtypeStruct(s, jnp.float32) for s in outs],
        in_specs=[pl.BlockSpec(memory_space=pltpu.SMEM) if n in smem else vmem for n in range(len(args))]
        + [anywhere] * (len(lazy) + len(after)),
        out_specs=[anywhere] * len(outs),
        scratch_shapes=[
            *(pltpu.VMEM(tuple(s), jnp.float32) for s in (*held, *lazy_shapes, *scratch)),
            pltpu.SemaphoreType.DMA((fetches,)),
            pltpu.SemaphoreType.DMA((sends,)),
        ],
        compiler_params=pltpu.CompilerParams(vmem_limit_bytes=VMEM_LIMIT - room),
        cost_estimate=pl.CostEstimate(flops=int(micros * 1e9), bytes_accessed=10**6, transcendentals=0),
    )(*args, *(a for a, _ in lazy), *after)


def to_column(row):
    n = row.shape[1]
    same = lax.broadcasted_iota(jnp.int32, (n, n), 0) == lax.broadcasted_iota(jnp.int32, (n, n), 1)
    return jnp.sum(jnp.where(same, row, 0.0), axis=1, keepdims=True)


def to_row(column):
    n = column.shape[0]
    same = lax.broadcasted_iota(jnp.int32, (n, n), 0) == lax.broadcasted_iota(jnp.int32, (n, n), 1)
    return jnp.sum(jnp.where(same, column, 0.0), axis=0, keepdims=True)


def own_packs(own_ref, flat_ref):
    flat_ref[24:32, :] = jnp.zeros((8, H), jnp.float32)
    for q in range(3 * ROWS):
        flat_ref[q : q + 1, :] = own_ref[q]
    return [
        jnp.concatenate(
            [flat_ref[8 * g : 8 * g + 8, SLICE * x : SLICE * (x + 1)] for g in range(4)], axis=1
        )
        for x in range(NX)
    ]


def prepare_packs_body(args, lazy, results, scratch, need, send):
    for half, ref in enumerate(args):
        for x, block in enumerate(own_packs(ref, scratch[0])):
            for y in range(NY):
                for t in range(3):
                    rows = slice(24 * half + 8 * t, 24 * half + 8 * t + 8)
                    results[0][x * NY + y, rows, :] = block[:, LANES * t : LANES * (t + 1)]


def spread_body(args, lazy, results, scratch, need, send):
    results[0][...] = args[0][:, 0:24, :]


def prepare_pairs_body(args, lazy, results, scratch, need, send):
    eta_ref, qkv_ref = args
    results[0][0:TOK, :] = qkv_ref[1, 0]
    results[0][TOK : 2 * TOK, :] = to_column(eta_ref[...]) * qkv_ref[2, 0]


def prepare_queries_body(args, lazy, results, scratch, need, send):
    need()
    (queries_ref,) = results
    queries_ref[0:TOK, :] = lazy[0][0, 0]
    queries_ref[TOK : 2 * TOK, :] = lazy[0][0, 1]


def widened(part):
    return jnp.concatenate([part, jnp.zeros((part.shape[0], LANES - SLICE), jnp.float32)], axis=1)


def unpack(recv_ref, out_ref, x_stride, y_stride, z_stride):
    for s in range(8):
        for x in range(NX):
            for y in range(NY):
                start = x * x_stride + y * y_stride + s
                rows = jnp.concatenate(
                    [recv_ref[pl.ds(start + 8 * t, NZ, stride=z_stride), :] for t in range(3)], axis=1
                )
                for g in range(4):
                    at = entry(g, s)
                    if at is None:
                        continue
                    r, i = at
                    out_ref[pl.ds(i * D + (x * NY + y) * ROWS + r, NZ, stride=NX * NY * ROWS), :] = widened(
                        rows[:, SLICE * g : SLICE * (g + 1)]
                    )


def pack(in_ref, send_ref, x_stride, y_stride, z_stride):
    for s in range(8):
        for x in range(NX):
            for y in range(NY):
                parts = []
                for g in range(4):
                    at = entry(g, s)
                    if at is None:
                        parts.append(jnp.zeros((NZ, SLICE), jnp.float32))
                        continue
                    r, i = at
                    parts.append(in_ref[pl.ds(i * D + (x * NY + y) * ROWS + r, NZ, stride=NX * NY * ROWS), :][:, :SLICE])
                rows = jnp.concatenate(parts, axis=1)
                start = x * x_stride + y * y_stride + s
                for t in range(3):
                    send_ref[pl.ds(start + 8 * t, NZ, stride=z_stride), :] = rows[:, LANES * t : LANES * (t + 1)]


def token_rows(refs, start):
    return jnp.concatenate([ref[start : start + TOK, :] for ref in refs], axis=0)


def matrix(ref, i):
    return ref[i * D : (i + 1) * D, :]


def gradient_body(args, pairs, results, scratch, need, send):
    (recv_ref,), (w_ref, send_ref), (g_ref,) = args, results, scratch
    unpack(recv_ref, w_ref, 48, 24, 192)
    send(0)
    need()
    keys = token_rows(pairs, 0)
    weighted = token_rows(pairs, TOK)
    pre = dot(keys, jnp.concatenate([matrix(w_ref, 0), matrix(w_ref, 1)], axis=1))
    gate_pre, up_pre = pre[:, :LANES], pre[:, LANES:]
    back = -dot(weighted, matrix(w_ref, 2))
    sigmoid = jax.nn.sigmoid(gate_pre)
    gated = gate_pre * sigmoid
    hidden = gated * up_pre
    gate_back = back * up_pre * sigmoid * (1.0 + gate_pre * (1.0 - sigmoid))
    up_back = back * gated
    both = dot(keys, jnp.concatenate([gate_back, up_back], axis=1), ((0,), (0,)))
    g_ref[0:D, :] = both[:, :LANES]
    g_ref[D : 2 * D, :] = both[:, LANES:]
    g_ref[2 * D : 3 * D, :] = -dot(weighted, hidden, ((0,), (0,)))
    pack(g_ref, send_ref, 24, 96, 192)


def source(x_ref, s):
    return lax.rem(x_ref[0] + NX - s, NX)


def moment_body(args, lazy, results, scratch, need, send):
    (yh_ref, recv_ref, packs_ref), (own_ref,) = args, results
    total = recv_ref[0]
    for j in range(1, NZ * NY):
        total = total + recv_ref[j]
    old = jnp.concatenate([packs_ref[x * NY + yh_ref[0], 24:48, :] for x in range(NX)], axis=0)
    own_ref[...] = total + MOMENTUM_RATE * old


def hidden_of(inputs, w1, w3):
    pre = dot(inputs, jnp.concatenate([w1, w3], axis=1))
    gate_pre, up_pre = pre[:, :LANES], pre[:, LANES:]
    return gate_pre * jax.nn.sigmoid(gate_pre) * up_pre


def first_read_body(args, lazy, results, scratch, need, send):
    need()
    *queries, w_ref = lazy
    hidden = hidden_of(token_rows(queries, 0), matrix(w_ref, 0), matrix(w_ref, 1))
    partial = dot(hidden, matrix(w_ref, 2), ((1,), (1,)))
    for s in range(NX):
        results[s][...] = partial[s * TOK : (s + 1) * TOK]


def renormalized(weights, moment):
    rate = STEP_SIZE / jnp.sqrt(jnp.mean(moment * moment, axis=0, keepdims=True) + EPSILON)
    moved = weights - moment * rate
    ratio = jnp.sqrt(jnp.mean(weights * weights, axis=0, keepdims=True) + EPSILON) / jnp.sqrt(
        jnp.mean(moved * moved, axis=0, keepdims=True) + EPSILON
    )
    return moved * ratio, rate, ratio


def second_read_body(args, lazy, results, scratch, need, send):
    (x_ref, recv_ref), (*queries, w_ref, moment_ref), (send_ref,), (m_ref,) = args, lazy, results, scratch
    unpack(recv_ref, m_ref, 24, 96, 192)
    need()
    new1, rate1, ratio1 = renormalized(matrix(w_ref, 0), matrix(m_ref, 0))
    new3, rate3, ratio3 = renormalized(matrix(w_ref, 1), matrix(m_ref, 1))
    new2, rate2, ratio2 = renormalized(matrix(w_ref, 2), matrix(m_ref, 2))
    hidden = hidden_of(token_rows(queries, 0), new1, new3)
    partial = dot(hidden, new2, ((1,), (1,)))
    stats = [rate1, rate3, rate2, ratio1, ratio3, ratio2, jnp.zeros((2, LANES), jnp.float32)]
    stats = jnp.concatenate(stats, axis=0)
    for x in range(NX):
        tail = [stats, *(moment_ref[0, 24 * x + 8 * t : 24 * x + 8 * t + 8, :] for t in range(3))]
        tail.append(jnp.zeros((8, LANES), jnp.float32))
        send_ref[x, TOK : TOK + 8, :] = jnp.concatenate(tail, axis=1)
    for s in range(NX):
        send_ref[source(x_ref, s), 0:TOK, :] = partial[s * TOK : (s + 1) * TOK]


def squares_body(args, lazy, results, scratch, need, send):
    (second_ref,), (readout_ref, send_ref) = args, results
    need()
    first = lazy[0][...] + lazy[1][...] + lazy[2][...] + lazy[3][...]
    second = second_ref[0, 0:TOK, :]
    for x in range(1, NX):
        second = second + second_ref[x, 0:TOK, :]
    readout_ref[0] = first
    readout_ref[1] = second
    row = jnp.concatenate(
        [to_row(jnp.sum(total * total, axis=1, keepdims=True)) for total in (first, second)], axis=1
    )
    send_ref[...] = jnp.broadcast_to(row, (8, GROUPS * TOK))


def own_rows_body(args, lazy, results, scratch, need, send):
    (second_ref, fw_ref), (new_w_ref, new_m_ref), (flat_ref,) = args, results, scratch
    for g in range(4):
        flat_ref[8 * g : 8 * g + 8, :] = jnp.concatenate(
            [
                second_ref[x, TOK : TOK + 8, LANES + SLICE * g : LANES + SLICE * (g + 1)]
                for x in range(NX)
            ],
            axis=1,
        )
    stats = jnp.concatenate([second_ref[x, TOK : TOK + 8, 0:SLICE] for x in range(NX)], axis=1)
    for q in range(3 * ROWS):
        i = q % 3
        moment = flat_ref[q : q + 1, :]
        new_m_ref[q] = moment
        new_w_ref[q] = (fw_ref[q] - moment * stats[i : i + 1]) * stats[3 + i : 4 + i]


def mix_body(args, lazy, results, scratch, need, send):
    (recv_ref, gain_ref, readout_ref, attended_ref), (mixed_ref,) = args, results
    total = recv_ref[0, 0:1, :]
    for n in range(1, NARROW):
        total = total + recv_ref[n, 0:1, :]
    scale = to_column(1.0 / jnp.sqrt(total / (D * NARROW) + EPSILON))
    for c in range(GROUPS):
        mixed_ref[c] = attended_ref[c] + gain_ref[...] * (readout_ref[c] * scale[c * TOK : (c + 1) * TOK])


def attention_body(args, lazy, results, scratch, need, send):
    (position_ref,), (qkv_ref, near_ref, far_ref), (out_ref,) = args, lazy, results
    position = position_ref[0]
    row = lax.broadcasted_iota(jnp.int32, (TOK, 3 * TOK), 0) + 2 * TOK
    col = lax.broadcasted_iota(jnp.int32, (TOK, 3 * TOK), 1)
    window = (row - col >= 0) & (row - col < WINDOW)
    first = jnp.where(position >= 2, 0, jnp.where(position >= 1, TOK, 2 * TOK))
    need()
    for c in range(GROUPS):
        allowed = window & (col >= first) if c == 0 else window
        for h in range(D // ATT):
            at = slice(h * ATT, (h + 1) * ATT)
            parts = []
            for a in range(2):
                far, near = far_ref[a, c, :, at], near_ref[a, c, :, at]
                if c == 1:
                    far = jnp.where(position >= 2, far, far_ref[a, 0, :, at])
                    near = jnp.where(position >= 1, near, near_ref[a, 0, :, at])
                parts.append(jnp.concatenate([far, near, qkv_ref[1 + a, c, :, at]], axis=0))
            keys, values = parts
            scores = dot(qkv_ref[0, c, :, at], keys, ((1,), (1,))) * (1.0 / math.sqrt(ATT))
            scores = jnp.where(allowed, scores, -1e30)
            weights = jnp.exp(scores - jnp.max(scores, axis=1, keepdims=True))
            weights = weights / jnp.sum(weights, axis=1, keepdims=True)
            out_ref[c, :, at] = dot(weights, values)


def behind(block, distance):
    axes = ("z", "x", "yh")
    return lax.ppermute(block, axes, [((i - distance) % BLOCKS, i) for i in range(BLOCKS)])


def from_neighbours(block):
    return [block] + [lax.ppermute(block, "x", [((i - s) % NX, i) for i in range(NX)]) for s in range(1, NX)]


def back_to_neighbours(blocks):
    return [blocks[0]] + [
        lax.ppermute(blocks[s], "x", [(i, (i - s) % NX) for i in range(NX)]) for s in range(1, NX)
    ]


def exchange(pieces, axes):
    return lax.all_to_all(pieces, axes, split_axis=0, concat_axis=0, tiled=True)


def scalar(value):
    return jnp.reshape(value, (1,)).astype(jnp.int32)


def whole(*arrays):
    return [(a, None) for a in arrays]


def local(qkv, eta, fast_weights, momentum, ttt_gain):
    own_weights, own_moment = fast_weights.reshape(3 * ROWS, 1, H), momentum.reshape(3 * ROWS, 1, H)
    x, yh = lax.axis_index("x"), lax.axis_index("yh")
    position = scalar((lax.axis_index("z") * NX + x) * NY + yh)
    x, yh = scalar(x), scalar(yh)
    (packs,) = call(
        prepare_packs_body, [(NX * NY, 48, LANES)], 1, own_weights, own_moment, scratch=[(32, H)], room=SMALL
    )
    (pairs,) = call(prepare_pairs_body, [(2 * TOK, D)], 1, eta, qkv, room=SMALL)
    packs = exchange(packs, ("x", "yh"))
    (spread,) = call(spread_body, [(NZ, NX * NY, 24, LANES)], 1, packs, fan=(0,), room=SMALL)
    recv1 = exchange(spread.reshape(NZ, NX * NY * 24, LANES), "z").reshape(BLOCKS * 24, LANES)
    pairs = from_neighbours(pairs)
    near, far = behind(qkv[1:], 1), behind(qkv[1:], 2)
    weights, send2 = call(
        gradient_body, [(3 * D, LANES), (BLOCKS * 24, LANES)], 5, recv1, lazy=whole(*pairs),
        scratch=[(3 * D, LANES)], after=(near, far), room=ROOM - 1024 * 1024,
    )
    recv2 = exchange(send2.reshape(NZ * NY, NX * 24, LANES), ("z", "yh"))
    (queries,) = call(prepare_queries_body, [(2 * TOK, D)], 1, lazy=[(qkv, (0, 1))], after=(weights,))
    queries = from_neighbours(queries)
    (attended,) = call(
        attention_body, [(GROUPS, TOK, D)], 8, position, lazy=whole(qkv, near, far), smem=(0,)
    )
    (send3,) = call(
        moment_body, [(NZ * NY, NX * 24, LANES)], 2, yh, recv2, packs, smem=(0,), fan=(0,),
        after=(attended, *queries[1:]),
        room=ROOM,
    )
    recv3 = exchange(send3, ("z", "yh")).reshape(BLOCKS * 24, LANES)
    first = back_to_neighbours(
        call(
            first_read_body, [(TOK, D)] * NX, 4, lazy=[*((q, (0, TOK)) for q in queries), (weights, None)],
            after=(send3,),
        )
    )
    (send_second,) = call(
        second_read_body, [(NX, TOK + 8, D)], 5, x, recv3,
        lazy=[*((q, (TOK, TOK)) for q in queries), (weights, None), (send3, (0, 1))], scratch=[(3 * D, LANES)],
        smem=(0,), after=first[1:], room=ROOM,
    )
    second = exchange(send_second, "x")
    readout, send5 = call(
        squares_body, [(GROUPS, TOK, D), (NARROW, 8, GROUPS * TOK)], 1, second, lazy=whole(*first), fan=(1,),
        room=SMALL,
    )
    recv5 = exchange(send5, "narrow")
    new_weights, new_moment = call(
        own_rows_body, [(3 * ROWS, 1, H), (3 * ROWS, 1, H)], 1, second, own_weights, scratch=[(32, H)],
        after=(send5,), room=SMALL,
    )
    (mixed,) = call(
        mix_body, [(GROUPS, TOK, D)], 1, recv5, ttt_gain.reshape(1, D), readout, attended, after=(new_weights,),
        room=SMALL,
    )
    return mixed, new_weights.reshape(1, ROWS, 3, H), new_moment.reshape(1, ROWS, 3, H)


def solution(mesh):
    fine = Mesh(mesh.devices.reshape(NZ, NX, NY, NARROW), ("z", "x", "yh", "narrow"))
    wide = ("z", "x", "yh")
    return jax.shard_map(
        local,
        mesh=fine,
        in_specs=(
            P(None, None, wide, "narrow"),
            P("narrow", wide),
            P("narrow", wide, None, None),
            P("narrow", wide, None, None),
            P("narrow"),
        ),
        out_specs=(
            P(None, wide, "narrow"),
            P("narrow", wide, None, None),
            P("narrow", wide, None, None),
        ),
        check_vma=False,
    )
```

```python
import functools
import math

import jax
import jax.numpy as jnp
from jax import lax
from jax.experimental import pallas as pl
from jax.experimental.pallas import tpu as pltpu
from jax.sharding import Mesh
from jax.sharding import PartitionSpec as P

ATT = 128
WINDOW = 128
EPSILON = 1e-06
MOMENTUM_RATE = 0.9
STEP_SIZE = 0.03
PRECISION = lax.Precision.HIGHEST

NZ, NX, NY = 8, 4, 2
BLOCKS = NZ * NX * NY
ROWS = 10
SLICE = 96
LANES = 128
TOK = 64
D = 640
H = 384
NARROW = 8
GROUPS = 2
VMEM_LIMIT = 58 * 1024 * 1024
ROOM = 8 * 1024 * 1024
SMALL = 42 * 1024 * 1024


def dot(left, right, dims=((1,), (0,))):
    return lax.dot_general(
        left, right, (dims, ((), ())), precision=PRECISION, preferred_element_type=jnp.float32
    )


def entry(group, sublane):
    q = group * 8 + sublane
    return (q // 3, q % 3) if q < 3 * ROWS else None


def call(body, outs, micros, *args, lazy=(), after=(), scratch=(), smem=(), fan=(), room=0):
    vmem, anywhere = pl.BlockSpec(memory_space=pltpu.VMEM), pl.BlockSpec(memory_space=pl.ANY)
    held = [outs[n][1:] if n in fan else outs[n] for n in range(len(outs))]
    lazy_shapes = [a.shape if at is None else (at[1], *a.shape[1:]) for a, at in lazy]
    sizes = (len(args), len(lazy), len(after), len(outs), len(outs), len(lazy), len(scratch))
    fetches = max(len(lazy), 1)
    sends = sum(outs[n][0] if n in fan else 1 for n in range(len(outs)))

    def kernel(*refs):
        split, at = [], 0
        for size in sizes:
            split.append(refs[at : at + size])
            at += size
        inputs, sources, _, targets, results, fetched, spare = split
        in_sems, out_sems = refs[at:]
        incoming = [
            pltpu.make_async_copy(ref if lazy[n][1] is None else ref.at[pl.ds(*lazy[n][1])], fetched[n], in_sems.at[n])
            for n, ref in enumerate(sources)
        ]
        for copy in incoming:
            copy.start()
        outgoing, base = [], 0
        for n in range(len(outs)):
            places = [targets[n].at[j] for j in range(outs[n][0])] if n in fan else [targets[n]]
            outgoing.append(
                [pltpu.make_async_copy(results[n], place, out_sems.at[base + j]) for j, place in enumerate(places)]
            )
            base += len(places)
        sent = set()

        def need():
            for copy in incoming:
                copy.wait()

        def send(n):
            sent.add(n)
            for copy in outgoing[n]:
                copy.start()

        body(inputs, fetched, results, spare, need, send)
        for n in range(len(outs)):
            if n not in sent:
                send(n)
        for copies in outgoing:
            for copy in copies:
                copy.wait()

    return pl.pallas_call(
        kernel,
        out_shape=[jax.ShapeDtypeStruct(s, jnp.float32) for s in outs],
        in_specs=[pl.BlockSpec(memory_space=pltpu.SMEM) if n in smem else vmem for n in range(len(args))]
        + [anywhere] * (len(lazy) + len(after)),
        out_specs=[anywhere] * len(outs),
        scratch_shapes=[
            *(pltpu.VMEM(tuple(s), jnp.float32) for s in (*held, *lazy_shapes, *scratch)),
            pltpu.SemaphoreType.DMA((fetches,)),
            pltpu.SemaphoreType.DMA((sends,)),
        ],
        compiler_params=pltpu.CompilerParams(vmem_limit_bytes=VMEM_LIMIT - room),
        cost_estimate=pl.CostEstimate(flops=int(micros * 1e9), bytes_accessed=10**6, transcendentals=0),
    )(*args, *(a for a, _ in lazy), *after)


def to_column(row):
    n = row.shape[1]
    same = lax.broadcasted_iota(jnp.int32, (n, n), 0) == lax.broadcasted_iota(jnp.int32, (n, n), 1)
    return jnp.sum(jnp.where(same, row, 0.0), axis=1, keepdims=True)


def to_row(column):
    n = column.shape[0]
    same = lax.broadcasted_iota(jnp.int32, (n, n), 0) == lax.broadcasted_iota(jnp.int32, (n, n), 1)
    return jnp.sum(jnp.where(same, column, 0.0), axis=0, keepdims=True)


def own_packs(own_ref, flat_ref):
    flat_ref[24:32, :] = jnp.zeros((8, H), jnp.float32)
    for q in range(3 * ROWS):
        flat_ref[q : q + 1, :] = own_ref[q]
    return [
        jnp.concatenate(
            [flat_ref[8 * g : 8 * g + 8, SLICE * x : SLICE * (x + 1)] for g in range(4)], axis=1
        )
        for x in range(NX)
    ]


def prepare_packs_body(args, lazy, results, scratch, need, send):
    for half, ref in enumerate(args):
        for x, block in enumerate(own_packs(ref, scratch[0])):
            for y in range(NY):
                for t in range(3):
                    rows = slice(24 * half + 8 * t, 24 * half + 8 * t + 8)
                    results[0][x * NY + y, rows, :] = block[:, LANES * t : LANES * (t + 1)]


def spread_body(args, lazy, results, scratch, need, send):
    results[0][...] = args[0][:, 0:24, :]


def prepare_pairs_body(args, lazy, results, scratch, need, send):
    eta_ref, qkv_ref = args
    results[0][0:TOK, :] = qkv_ref[1, 0]
    results[0][TOK : 2 * TOK, :] = to_column(eta_ref[...]) * qkv_ref[2, 0]


def prepare_queries_body(args, lazy, results, scratch, need, send):
    (position_ref,), (qkv_ref,), (queries_ref, tail_ref) = args, lazy, results
    last = position_ref[0] == BLOCKS - 1
    need()
    queries_ref[0:TOK, :] = qkv_ref[0, 0]
    queries_ref[TOK : 2 * TOK, :] = qkv_ref[0, 1]
    send(0)
    for a in range(2):
        tail_ref[a] = jnp.where(last, qkv_ref[1 + a, 0], qkv_ref[1 + a, 1])


def prepare_far_body(args, lazy, results, scratch, need, send):
    need()
    results[0][...] = lazy[0][...]


def widened(part):
    return jnp.concatenate([part, jnp.zeros((part.shape[0], LANES - SLICE), jnp.float32)], axis=1)


def unpack(recv_ref, out_ref, x_stride, y_stride, z_stride):
    for s in range(8):
        for x in range(NX):
            for y in range(NY):
                start = x * x_stride + y * y_stride + s
                rows = jnp.concatenate(
                    [recv_ref[pl.ds(start + 8 * t, NZ, stride=z_stride), :] for t in range(3)], axis=1
                )
                for g in range(4):
                    at = entry(g, s)
                    if at is None:
                        continue
                    r, i = at
                    out_ref[pl.ds(i * D + (x * NY + y) * ROWS + r, NZ, stride=NX * NY * ROWS), :] = widened(
                        rows[:, SLICE * g : SLICE * (g + 1)]
                    )


def pack(in_ref, send_ref, x_stride, y_stride, z_stride):
    for s in range(8):
        for x in range(NX):
            for y in range(NY):
                parts = []
                for g in range(4):
                    at = entry(g, s)
                    if at is None:
                        parts.append(jnp.zeros((NZ, SLICE), jnp.float32))
                        continue
                    r, i = at
                    parts.append(in_ref[pl.ds(i * D + (x * NY + y) * ROWS + r, NZ, stride=NX * NY * ROWS), :][:, :SLICE])
                rows = jnp.concatenate(parts, axis=1)
                start = x * x_stride + y * y_stride + s
                for t in range(3):
                    send_ref[pl.ds(start + 8 * t, NZ, stride=z_stride), :] = rows[:, LANES * t : LANES * (t + 1)]


def token_rows(refs, start):
    return jnp.concatenate([ref[start : start + TOK, :] for ref in refs], axis=0)


def matrix(ref, i):
    return ref[i * D : (i + 1) * D, :]


def gradient_body(args, pairs, results, scratch, need, send):
    (recv_ref,), (w_ref, send_ref), (g_ref,) = args, results, scratch
    unpack(recv_ref, w_ref, 48, 24, 192)
    send(0)
    need()
    keys = token_rows(pairs, 0)
    weighted = token_rows(pairs, TOK)
    pre = dot(keys, jnp.concatenate([matrix(w_ref, 0), matrix(w_ref, 1)], axis=1))
    gate_pre, up_pre = pre[:, :LANES], pre[:, LANES:]
    back = -dot(weighted, matrix(w_ref, 2))
    sigmoid = jax.nn.sigmoid(gate_pre)
    gated = gate_pre * sigmoid
    hidden = gated * up_pre
    gate_back = back * up_pre * sigmoid * (1.0 + gate_pre * (1.0 - sigmoid))
    up_back = back * gated
    both = dot(keys, jnp.concatenate([gate_back, up_back], axis=1), ((0,), (0,)))
    g_ref[0:D, :] = both[:, :LANES]
    g_ref[D : 2 * D, :] = both[:, LANES:]
    g_ref[2 * D : 3 * D, :] = -dot(weighted, hidden, ((0,), (0,)))
    pack(g_ref, send_ref, 24, 96, 192)


def source(x_ref, s):
    return lax.rem(x_ref[0] + NX - s, NX)


def moment_body(args, lazy, results, scratch, need, send):
    (yh_ref, recv_ref, packs_ref), (own_ref,) = args, results
    total = recv_ref[0]
    for j in range(1, NZ * NY):
        total = total + recv_ref[j]
    old = jnp.concatenate([packs_ref[x * NY + yh_ref[0], 24:48, :] for x in range(NX)], axis=0)
    own_ref[...] = total + MOMENTUM_RATE * old


def hidden_of(inputs, w1, w3):
    pre = dot(inputs, jnp.concatenate([w1, w3], axis=1))
    gate_pre, up_pre = pre[:, :LANES], pre[:, LANES:]
    return gate_pre * jax.nn.sigmoid(gate_pre) * up_pre


def first_read_body(args, lazy, results, scratch, need, send):
    need()
    *queries, w_ref = lazy
    hidden = hidden_of(token_rows(queries, 0), matrix(w_ref, 0), matrix(w_ref, 1))
    partial = dot(hidden, matrix(w_ref, 2), ((1,), (1,)))
    for s in range(NX):
        results[s][...] = partial[s * TOK : (s + 1) * TOK]


def renormalized(weights, moment):
    rate = STEP_SIZE / jnp.sqrt(jnp.mean(moment * moment, axis=0, keepdims=True) + EPSILON)
    moved = weights - moment * rate
    ratio = jnp.sqrt(jnp.mean(weights * weights, axis=0, keepdims=True) + EPSILON) / jnp.sqrt(
        jnp.mean(moved * moved, axis=0, keepdims=True) + EPSILON
    )
    return moved * ratio, rate, ratio


def second_read_body(args, lazy, results, scratch, need, send):
    (x_ref, recv_ref), (*queries, w_ref, moment_ref), (send_ref,), (m_ref,) = args, lazy, results, scratch
    unpack(recv_ref, m_ref, 24, 96, 192)
    need()
    new1, rate1, ratio1 = renormalized(matrix(w_ref, 0), matrix(m_ref, 0))
    new3, rate3, ratio3 = renormalized(matrix(w_ref, 1), matrix(m_ref, 1))
    new2, rate2, ratio2 = renormalized(matrix(w_ref, 2), matrix(m_ref, 2))
    hidden = hidden_of(token_rows(queries, 0), new1, new3)
    partial = dot(hidden, new2, ((1,), (1,)))
    stats = [rate1, rate3, rate2, ratio1, ratio3, ratio2, jnp.zeros((2, LANES), jnp.float32)]
    stats = jnp.concatenate(stats, axis=0)
    for x in range(NX):
        tail = [stats, *(moment_ref[0, 24 * x + 8 * t : 24 * x + 8 * t + 8, :] for t in range(3))]
        tail.append(jnp.zeros((8, LANES), jnp.float32))
        send_ref[x, TOK : TOK + 8, :] = jnp.concatenate(tail, axis=1)
    for s in range(NX):
        send_ref[source(x_ref, s), 0:TOK, :] = partial[s * TOK : (s + 1) * TOK]


def squares_body(args, lazy, results, scratch, need, send):
    (second_ref,), (readout_ref, send_ref) = args, results
    need()
    first = lazy[0][...] + lazy[1][...] + lazy[2][...] + lazy[3][...]
    second = second_ref[0, 0:TOK, :]
    for x in range(1, NX):
        second = second + second_ref[x, 0:TOK, :]
    readout_ref[0] = first
    readout_ref[1] = second
    row = jnp.concatenate(
        [to_row(jnp.sum(total * total, axis=1, keepdims=True)) for total in (first, second)], axis=1
    )
    send_ref[...] = jnp.broadcast_to(row, (8, GROUPS * TOK))


def own_rows_body(args, lazy, results, scratch, need, send):
    (second_ref, fw_ref), (new_w_ref, new_m_ref), (flat_ref,) = args, results, scratch
    for g in range(4):
        flat_ref[8 * g : 8 * g + 8, :] = jnp.concatenate(
            [
                second_ref[x, TOK : TOK + 8, LANES + SLICE * g : LANES + SLICE * (g + 1)]
                for x in range(NX)
            ],
            axis=1,
        )
    stats = jnp.concatenate([second_ref[x, TOK : TOK + 8, 0:SLICE] for x in range(NX)], axis=1)
    for q in range(3 * ROWS):
        i = q % 3
        moment = flat_ref[q : q + 1, :]
        new_m_ref[q] = moment
        new_w_ref[q] = (fw_ref[q] - moment * stats[i : i + 1]) * stats[3 + i : 4 + i]


def mix_body(args, lazy, results, scratch, need, send):
    (recv_ref, gain_ref, readout_ref, attended_ref), (mixed_ref,) = args, results
    total = recv_ref[0, 0:1, :]
    for n in range(1, NARROW):
        total = total + recv_ref[n, 0:1, :]
    scale = to_column(1.0 / jnp.sqrt(total / (D * NARROW) + EPSILON))
    for c in range(GROUPS):
        mixed_ref[c] = attended_ref[c] + gain_ref[...] * (readout_ref[c] * scale[c * TOK : (c + 1) * TOK])


def attention_body(args, lazy, results, scratch, need, send):
    (position_ref,), (qkv_ref, *near_refs, far_ref), (out_ref,) = args, lazy, results
    position = position_ref[0]
    row = lax.broadcasted_iota(jnp.int32, (TOK, 3 * TOK), 0) + 2 * TOK
    col = lax.broadcasted_iota(jnp.int32, (TOK, 3 * TOK), 1)
    window = (row - col >= 0) & (row - col < WINDOW)
    first = jnp.where(position >= 2, 0, jnp.where(position >= 1, TOK, 2 * TOK))
    need()
    for c in range(GROUPS):
        allowed = window & (col >= first) if c == 0 else window
        for h in range(D // ATT):
            at = slice(h * ATT, (h + 1) * ATT)
            parts = []
            for a in range(2):
                far, near = far_ref[a, c, :, at], near_refs[c][a, :, at]
                if c == 1:
                    far = jnp.where(position >= 2, far, far_ref[a, 0, :, at])
                parts.append(jnp.concatenate([far, near, qkv_ref[1 + a, c, :, at]], axis=0))
            keys, values = parts
            scores = dot(qkv_ref[0, c, :, at], keys, ((1,), (1,))) * (1.0 / math.sqrt(ATT))
            scores = jnp.where(allowed, scores, -1e30)
            weights = jnp.exp(scores - jnp.max(scores, axis=1, keepdims=True))
            weights = weights / jnp.sum(weights, axis=1, keepdims=True)
            out_ref[c, :, at] = dot(weights, values)


def behind(block, distance):
    axes = ("z", "x", "yh")
    return lax.ppermute(block, axes, [((i - distance) % BLOCKS, i) for i in range(BLOCKS)])


def from_neighbours(block):
    return [block] + [lax.ppermute(block, "x", [((i - s) % NX, i) for i in range(NX)]) for s in range(1, NX)]


def back_to_neighbours(blocks):
    return [blocks[0]] + [
        lax.ppermute(blocks[s], "x", [(i, (i - s) % NX) for i in range(NX)]) for s in range(1, NX)
    ]


def exchange(pieces, axes):
    return lax.all_to_all(pieces, axes, split_axis=0, concat_axis=0, tiled=True)


def scalar(value):
    return jnp.reshape(value, (1,)).astype(jnp.int32)


def whole(*arrays):
    return [(a, None) for a in arrays]


def local(qkv, eta, fast_weights, momentum, ttt_gain):
    own_weights, own_moment = fast_weights.reshape(3 * ROWS, 1, H), momentum.reshape(3 * ROWS, 1, H)
    x, yh = lax.axis_index("x"), lax.axis_index("yh")
    position = scalar((lax.axis_index("z") * NX + x) * NY + yh)
    x, yh = scalar(x), scalar(yh)
    (packs,) = call(
        prepare_packs_body, [(NX * NY, 48, LANES)], 1, own_weights, own_moment, scratch=[(32, H)], room=SMALL
    )
    (pairs,) = call(prepare_pairs_body, [(2 * TOK, D)], 1, eta, qkv, room=SMALL)
    packs = exchange(packs, ("x", "yh"))
    (spread,) = call(spread_body, [(NZ, NX * NY, 24, LANES)], 1, packs, fan=(0,), room=SMALL)
    recv1 = exchange(spread.reshape(NZ, NX * NY * 24, LANES), "z").reshape(BLOCKS * 24, LANES)
    pairs = from_neighbours(pairs)
    near0 = behind(qkv[1:, 0], 1)
    weights, send2 = call(
        gradient_body, [(3 * D, LANES), (BLOCKS * 24, LANES)], 5, recv1, lazy=whole(*pairs),
        scratch=[(3 * D, LANES)], after=(near0,), room=ROOM - 512 * 1024,
    )
    recv2 = exchange(send2.reshape(NZ * NY, NX * 24, LANES), ("z", "yh"))
    queries, tail = call(
        prepare_queries_body, [(2 * TOK, D), (2, TOK, D)], 1, position, lazy=whole(qkv), smem=(0,), after=(weights,)
    )
    queries = from_neighbours(queries)
    near1 = behind(tail, 1)
    (send3,) = call(
        moment_body, [(NZ * NY, NX * 24, LANES)], 2, yh, recv2, packs, smem=(0,), fan=(0,),
        after=(near1, *queries[1:]),
        room=ROOM,
    )
    recv3 = exchange(send3, ("z", "yh")).reshape(BLOCKS * 24, LANES)
    first = back_to_neighbours(
        call(
            first_read_body, [(TOK, D)] * NX, 4, lazy=[*((q, (0, TOK)) for q in queries), (weights, None)],
            after=(send3,),
        )
    )
    (far,) = call(prepare_far_body, [(2, GROUPS, TOK, D)], 1, lazy=[(qkv, (1, 2))], after=(send3,))
    far = behind(far, 2)
    (send_second,) = call(
        second_read_body, [(NX, TOK + 8, D)], 5, x, recv3,
        lazy=[*((q, (TOK, TOK)) for q in queries), (weights, None), (send3, (0, 1))], scratch=[(3 * D, LANES)],
        smem=(0,), after=(far, *first[1:]), room=ROOM,
    )
    second = exchange(send_second, "x")
    (attended,) = call(
        attention_body, [(GROUPS, TOK, D)], 8, position, lazy=whole(qkv, near0, near1, far), smem=(0,),
        after=(send_second,),
    )
    readout, send5 = call(
        squares_body, [(GROUPS, TOK, D), (NARROW, 8, GROUPS * TOK)], 1, second, lazy=whole(*first), fan=(1,),
        after=(attended,), room=SMALL,
    )
    recv5 = exchange(send5, "narrow")
    new_weights, new_moment = call(
        own_rows_body, [(3 * ROWS, 1, H), (3 * ROWS, 1, H)], 1, second, own_weights, scratch=[(32, H)],
        after=(send5,), room=SMALL,
    )
    (mixed,) = call(
        mix_body, [(GROUPS, TOK, D)], 1, recv5, ttt_gain.reshape(1, D), readout, attended, after=(new_weights,),
        room=SMALL,
    )
    return mixed, new_weights.reshape(1, ROWS, 3, H), new_moment.reshape(1, ROWS, 3, H)


def solution(mesh):
    fine = Mesh(mesh.devices.reshape(NZ, NX, NY, NARROW), ("z", "x", "yh", "narrow"))
    wide = ("z", "x", "yh")
    return jax.shard_map(
        local,
        mesh=fine,
        in_specs=(
            P(None, None, wide, "narrow"),
            P("narrow", wide),
            P("narrow", wide, None, None),
            P("narrow", wide, None, None),
            P("narrow"),
        ),
        out_specs=(
            P(None, wide, "narrow"),
            P("narrow", wide, None, None),
            P("narrow", wide, None, None),
        ),
        check_vma=False,
    )
```

```python
import functools
import math

import jax
import jax.numpy as jnp
from jax import lax
from jax.experimental import pallas as pl
from jax.experimental.pallas import tpu as pltpu
from jax.sharding import Mesh
from jax.sharding import PartitionSpec as P

ATT = 128
WINDOW = 128
EPSILON = 1e-06
MOMENTUM_RATE = 0.9
STEP_SIZE = 0.03
PRECISION = lax.Precision.HIGHEST

NZ, NX, NY = 8, 4, 2
BLOCKS = NZ * NX * NY
ROWS = 10
SLICE = 96
LANES = 128
TOK = 64
D = 640
H = 384
NARROW = 8
GROUPS = 2
VMEM_LIMIT = 58 * 1024 * 1024
ROOM = 8 * 1024 * 1024
PAD = 8
SMALL = 42 * 1024 * 1024


def dot(left, right, dims=((1,), (0,))):
    return lax.dot_general(
        left, right, (dims, ((), ())), precision=PRECISION, preferred_element_type=jnp.float32
    )


def entry(group, sublane):
    q = group * 8 + sublane
    return (q // 3, q % 3) if q < 3 * ROWS else None


def call(body, outs, micros, *args, lazy=(), after=(), scratch=(), smem=(), fan=(), room=0):
    vmem, anywhere = pl.BlockSpec(memory_space=pltpu.VMEM), pl.BlockSpec(memory_space=pl.ANY)
    held = [outs[n][1:] if n in fan else outs[n] for n in range(len(outs))]
    lazy_shapes = [a.shape if at is None else (at[1], *a.shape[1:]) for a, at in lazy]
    sizes = (len(args), len(lazy), len(after), len(outs), len(outs), len(lazy), len(scratch))
    fetches = max(len(lazy), 1)
    sends = sum(outs[n][0] if n in fan else 1 for n in range(len(outs)))

    def kernel(*refs):
        split, at = [], 0
        for size in sizes:
            split.append(refs[at : at + size])
            at += size
        inputs, sources, _, targets, results, fetched, spare = split
        in_sems, out_sems = refs[at:]
        incoming = [
            pltpu.make_async_copy(ref if lazy[n][1] is None else ref.at[pl.ds(*lazy[n][1])], fetched[n], in_sems.at[n])
            for n, ref in enumerate(sources)
        ]
        for copy in incoming:
            copy.start()
        outgoing, base = [], 0
        for n in range(len(outs)):
            places = [targets[n].at[j] for j in range(outs[n][0])] if n in fan else [targets[n]]
            outgoing.append(
                [pltpu.make_async_copy(results[n], place, out_sems.at[base + j]) for j, place in enumerate(places)]
            )
            base += len(places)
        sent = set()

        def need():
            for copy in incoming:
                copy.wait()

        def send(n):
            sent.add(n)
            for copy in outgoing[n]:
                copy.start()

        body(inputs, fetched, results, spare, need, send)
        for n in range(len(outs)):
            if n not in sent:
                send(n)
        for copies in outgoing:
            for copy in copies:
                copy.wait()

    return pl.pallas_call(
        kernel,
        out_shape=[jax.ShapeDtypeStruct(s, jnp.float32) for s in outs],
        in_specs=[pl.BlockSpec(memory_space=pltpu.SMEM) if n in smem else vmem for n in range(len(args))]
        + [anywhere] * (len(lazy) + len(after)),
        out_specs=[anywhere] * len(outs),
        scratch_shapes=[
            *(pltpu.VMEM(tuple(s), jnp.float32) for s in (*held, *lazy_shapes, *scratch)),
            pltpu.SemaphoreType.DMA((fetches,)),
            pltpu.SemaphoreType.DMA((sends,)),
        ],
        compiler_params=pltpu.CompilerParams(vmem_limit_bytes=VMEM_LIMIT - room),
        cost_estimate=pl.CostEstimate(flops=int(micros * 1e9), bytes_accessed=10**6, transcendentals=0),
    )(*args, *(a for a, _ in lazy), *after)


def to_column(row):
    n = row.shape[1]
    same = lax.broadcasted_iota(jnp.int32, (n, n), 0) == lax.broadcasted_iota(jnp.int32, (n, n), 1)
    return jnp.sum(jnp.where(same, row, 0.0), axis=1, keepdims=True)


def to_row(column):
    n = column.shape[0]
    same = lax.broadcasted_iota(jnp.int32, (n, n), 0) == lax.broadcasted_iota(jnp.int32, (n, n), 1)
    return jnp.sum(jnp.where(same, column, 0.0), axis=0, keepdims=True)


def own_packs(own_ref, flat_ref):
    flat_ref[24:32, :] = jnp.zeros((8, H), jnp.float32)
    for q in range(3 * ROWS):
        flat_ref[q : q + 1, :] = own_ref[q]
    return [
        jnp.concatenate(
            [flat_ref[8 * g : 8 * g + 8, SLICE * x : SLICE * (x + 1)] for g in range(4)], axis=1
        )
        for x in range(NX)
    ]


def prepare_packs_body(args, lazy, results, scratch, need, send):
    for half, ref in enumerate(args):
        for x, block in enumerate(own_packs(ref, scratch[0])):
            for y in range(NY):
                for t in range(3):
                    rows = slice(24 * half + 8 * t, 24 * half + 8 * t + 8)
                    results[0][x * NY + y, rows, :] = block[:, LANES * t : LANES * (t + 1)]


def spread_body(args, lazy, results, scratch, need, send):
    results[0][...] = args[0][:, 0:24, :]


def prepare_pairs_body(args, lazy, results, scratch, need, send):
    eta_ref, qkv_ref = args
    results[0][0:TOK, :] = qkv_ref[1, 0]
    results[0][TOK : 2 * TOK, :] = to_column(eta_ref[...]) * qkv_ref[2, 0]


def prepare_queries_body(args, lazy, results, scratch, need, send):
    (qkv_ref,), (queries_ref, tail_ref) = lazy, results
    need()
    queries_ref[0:TOK, :] = qkv_ref[0, 0]
    queries_ref[TOK : 2 * TOK, :] = qkv_ref[0, 1]
    send(0)
    for a in range(2):
        tail_ref[a] = qkv_ref[1 + a, 0]


def prepare_tails_body(args, lazy, results, scratch, need, send):
    (position_ref,), (qkv_ref,) = args, lazy
    need()
    for distance, ref in zip((1, 2), results):
        for a in range(2):
            ref[a] = jnp.where(position_ref[0] >= BLOCKS - distance, qkv_ref[a, 0], qkv_ref[a, 1])


def widened(part):
    return jnp.concatenate([part, jnp.zeros((part.shape[0], LANES - SLICE), jnp.float32)], axis=1)


def unpack(recv_ref, out_ref, x_stride, y_stride, z_stride):
    for s in range(8):
        for x in range(NX):
            for y in range(NY):
                start = x * x_stride + y * y_stride + s
                rows = jnp.concatenate(
                    [recv_ref[pl.ds(start + 8 * t, NZ, stride=z_stride), :] for t in range(3)], axis=1
                )
                for g in range(4):
                    at = entry(g, s)
                    if at is None:
                        continue
                    r, i = at
                    out_ref[pl.ds(i * D + (x * NY + y) * ROWS + r, NZ, stride=NX * NY * ROWS), :] = widened(
                        rows[:, SLICE * g : SLICE * (g + 1)]
                    )


def pack(in_ref, send_ref, x_stride, y_stride, z_stride):
    for s in range(8):
        for x in range(NX):
            for y in range(NY):
                parts = []
                for g in range(4):
                    at = entry(g, s)
                    if at is None:
                        parts.append(jnp.zeros((NZ, SLICE), jnp.float32))
                        continue
                    r, i = at
                    parts.append(in_ref[pl.ds(i * D + (x * NY + y) * ROWS + r, NZ, stride=NX * NY * ROWS), :][:, :SLICE])
                rows = jnp.concatenate(parts, axis=1)
                start = x * x_stride + y * y_stride + s
                for t in range(3):
                    send_ref[pl.ds(start + 8 * t, NZ, stride=z_stride), :] = rows[:, LANES * t : LANES * (t + 1)]


def token_rows(refs, start):
    return jnp.concatenate([ref[start : start + TOK, :] for ref in refs], axis=0)


def matrix(ref, i):
    return ref[i * D : (i + 1) * D, :]


def gradient_body(args, pairs, results, scratch, need, send):
    (recv_ref,), (w_ref, send_ref), (g_ref,) = args, results, scratch
    unpack(recv_ref, w_ref, 48, 24, 192)
    send(0)
    need()
    keys = token_rows(pairs, 0)
    weighted = token_rows(pairs, TOK)
    pre = dot(keys, jnp.concatenate([matrix(w_ref, 0), matrix(w_ref, 1)], axis=1))
    gate_pre, up_pre = pre[:, :LANES], pre[:, LANES:]
    back = -dot(weighted, matrix(w_ref, 2))
    sigmoid = jax.nn.sigmoid(gate_pre)
    gated = gate_pre * sigmoid
    hidden = gated * up_pre
    gate_back = back * up_pre * sigmoid * (1.0 + gate_pre * (1.0 - sigmoid))
    up_back = back * gated
    both = dot(keys, jnp.concatenate([gate_back, up_back], axis=1), ((0,), (0,)))
    g_ref[0:D, :] = both[:, :LANES]
    g_ref[D : 2 * D, :] = both[:, LANES:]
    g_ref[2 * D : 3 * D, :] = -dot(weighted, hidden, ((0,), (0,)))
    pack(g_ref, send_ref, 24, 96, 192)


def source(x_ref, s):
    return lax.rem(x_ref[0] + NX - s, NX)


def moment_body(args, lazy, results, scratch, need, send):
    (yh_ref, recv_ref, packs_ref), (own_ref,) = args, results
    total = recv_ref[0]
    for j in range(1, NZ * NY):
        total = total + recv_ref[j]
    old = jnp.concatenate([packs_ref[x * NY + yh_ref[0], 24:48, :] for x in range(NX)], axis=0)
    own_ref[...] = total + MOMENTUM_RATE * old


def hidden_of(inputs, w1, w3):
    pre = dot(inputs, jnp.concatenate([w1, w3], axis=1))
    gate_pre, up_pre = pre[:, :LANES], pre[:, LANES:]
    return gate_pre * jax.nn.sigmoid(gate_pre) * up_pre


def first_read_body(args, lazy, results, scratch, need, send):
    need()
    *queries, w_ref = lazy
    hidden = hidden_of(token_rows(queries, 0), matrix(w_ref, 0), matrix(w_ref, 1))
    partial = dot(hidden, matrix(w_ref, 2), ((1,), (1,)))
    for s in range(NX):
        results[s][...] = partial[s * TOK : (s + 1) * TOK]


def renormalized(weights, moment):
    rate = STEP_SIZE / jnp.sqrt(jnp.mean(moment * moment, axis=0, keepdims=True) + EPSILON)
    moved = weights - moment * rate
    ratio = jnp.sqrt(jnp.mean(weights * weights, axis=0, keepdims=True) + EPSILON) / jnp.sqrt(
        jnp.mean(moved * moved, axis=0, keepdims=True) + EPSILON
    )
    return moved * ratio, rate, ratio


def second_read_body(args, lazy, results, scratch, need, send):
    (x_ref, recv_ref), (*queries, w_ref, moment_ref), (send_ref,), (m_ref,) = args, lazy, results, scratch
    unpack(recv_ref, m_ref, 24, 96, 192)
    need()
    new1, rate1, ratio1 = renormalized(matrix(w_ref, 0), matrix(m_ref, 0))
    new3, rate3, ratio3 = renormalized(matrix(w_ref, 1), matrix(m_ref, 1))
    new2, rate2, ratio2 = renormalized(matrix(w_ref, 2), matrix(m_ref, 2))
    hidden = hidden_of(token_rows(queries, 0), new1, new3)
    partial = dot(hidden, new2, ((1,), (1,)))
    stats = [rate1, rate3, rate2, ratio1, ratio3, ratio2, jnp.zeros((2, LANES), jnp.float32)]
    stats = jnp.concatenate(stats, axis=0)
    for x in range(NX):
        tail = [stats, *(moment_ref[0, 24 * x + 8 * t : 24 * x + 8 * t + 8, :] for t in range(3))]
        tail.append(jnp.zeros((8, LANES), jnp.float32))
        send_ref[x, TOK : TOK + 8, :] = jnp.concatenate(tail, axis=1)
    for s in range(NX):
        send_ref[source(x_ref, s), 0:TOK, :] = partial[s * TOK : (s + 1) * TOK]


def squares_body(args, lazy, results, scratch, need, send):
    (second_ref,), (readout_ref, send_ref) = args, results
    need()
    first = lazy[0][...] + lazy[1][...] + lazy[2][...] + lazy[3][...]
    second = second_ref[0, 0:TOK, :]
    for x in range(1, NX):
        second = second + second_ref[x, 0:TOK, :]
    readout_ref[0] = first
    readout_ref[1] = second
    row = jnp.concatenate(
        [to_row(jnp.sum(total * total, axis=1, keepdims=True)) for total in (first, second)], axis=1
    )
    send_ref[...] = jnp.broadcast_to(row, (8, GROUPS * TOK))


def own_rows_body(args, lazy, results, scratch, need, send):
    (second_ref, fw_ref), (new_w_ref, new_m_ref), (flat_ref,) = args, results, scratch
    for g in range(4):
        flat_ref[8 * g : 8 * g + 8, :] = jnp.concatenate(
            [
                second_ref[x, TOK : TOK + 8, LANES + SLICE * g : LANES + SLICE * (g + 1)]
                for x in range(NX)
            ],
            axis=1,
        )
    stats = jnp.concatenate([second_ref[x, TOK : TOK + 8, 0:SLICE] for x in range(NX)], axis=1)
    for q in range(3 * ROWS):
        i = q % 3
        moment = flat_ref[q : q + 1, :]
        new_m_ref[q] = moment
        new_w_ref[q] = (fw_ref[q] - moment * stats[i : i + 1]) * stats[3 + i : 4 + i]


def mix_body(args, lazy, results, scratch, need, send):
    (recv_ref, gain_ref, readout_ref, *attended_refs), (mixed_ref,) = args, results
    total = recv_ref[0, 0:1, :]
    for n in range(1, NARROW):
        total = total + recv_ref[n, 0:1, :]
    scale = to_column(1.0 / jnp.sqrt(total / (D * NARROW) + EPSILON))
    for c in range(GROUPS):
        mixed_ref[c] = attended_refs[c][...] + gain_ref[...] * (readout_ref[c] * scale[c * TOK : (c + 1) * TOK])


def attention_body(c, args, lazy, results, scratch, need, send):
    (position_ref,), (qkv_ref, near_ref, far_ref), (out_ref,) = args, lazy, results
    position = position_ref[0]
    row = lax.broadcasted_iota(jnp.int32, (TOK, 3 * TOK), 0) + 2 * TOK
    col = lax.broadcasted_iota(jnp.int32, (TOK, 3 * TOK), 1)
    allowed = (row - col >= 0) & (row - col < WINDOW)
    if c == 0:
        first = jnp.where(position >= 2, 0, jnp.where(position >= 1, TOK, 2 * TOK))
        allowed = allowed & (col >= first)
    need()
    for h in range(D // ATT):
        at = slice(h * ATT, (h + 1) * ATT)
        keys, values = (
            jnp.concatenate([far_ref[a, :, at], near_ref[a, 0:TOK, at], qkv_ref[1 + a, c, :, at]], axis=0)
            for a in range(2)
        )
        scores = dot(qkv_ref[0, c, :, at], keys, ((1,), (1,))) * (1.0 / math.sqrt(ATT))
        scores = jnp.where(allowed, scores, -1e30)
        weights = jnp.exp(scores - jnp.max(scores, axis=1, keepdims=True))
        weights = weights / jnp.sum(weights, axis=1, keepdims=True)
        out_ref[:, at] = dot(weights, values)


def behind(block, distance):
    axes = ("z", "x", "yh")
    return lax.ppermute(block, axes, [((i - distance) % BLOCKS, i) for i in range(BLOCKS)])


def from_neighbours(block):
    return [block] + [lax.ppermute(block, "x", [((i - s) % NX, i) for i in range(NX)]) for s in range(1, NX)]


def back_to_neighbours(blocks):
    return [blocks[0]] + [
        lax.ppermute(blocks[s], "x", [(i, (i - s) % NX) for i in range(NX)]) for s in range(1, NX)
    ]


def exchange(pieces, axes):
    return lax.all_to_all(pieces, axes, split_axis=0, concat_axis=0, tiled=True)


def scalar(value):
    return jnp.reshape(value, (1,)).astype(jnp.int32)


def whole(*arrays):
    return [(a, None) for a in arrays]


def local(qkv, eta, fast_weights, momentum, ttt_gain):
    own_weights, own_moment = fast_weights.reshape(3 * ROWS, 1, H), momentum.reshape(3 * ROWS, 1, H)
    x, yh = lax.axis_index("x"), lax.axis_index("yh")
    position = scalar((lax.axis_index("z") * NX + x) * NY + yh)
    x, yh = scalar(x), scalar(yh)
    (packs,) = call(
        prepare_packs_body, [(NX * NY, 48, LANES)], 1, own_weights, own_moment, scratch=[(32, H)], room=SMALL
    )
    (pairs,) = call(prepare_pairs_body, [(2 * TOK, D)], 1, eta, qkv, room=SMALL)
    packs = exchange(packs, ("x", "yh"))
    (spread,) = call(spread_body, [(NZ, NX * NY, 24, LANES)], 1, packs, fan=(0,), room=SMALL)
    recv1 = exchange(spread.reshape(NZ, NX * NY * 24, LANES), "z").reshape(BLOCKS * 24, LANES)
    pairs = from_neighbours(pairs)
    near0 = behind(jnp.pad(qkv[1:, 0], ((0, 0), (0, PAD), (0, 0))), 1)
    weights, send2 = call(
        gradient_body, [(3 * D, LANES), (BLOCKS * 24, LANES)], 5, recv1, lazy=whole(*pairs),
        scratch=[(3 * D, LANES)], after=(near0,), room=ROOM - 512 * 1024,
    )
    recv2 = exchange(send2.reshape(NZ * NY, NX * 24, LANES), ("z", "yh"))
    queries, tail = call(
        prepare_queries_body, [(2 * TOK, D), (2, TOK, D)], 1, lazy=whole(qkv), after=(weights,)
    )
    queries = from_neighbours(queries)
    far0 = behind(tail, 2)
    (send3,) = call(
        moment_body, [(NZ * NY, NX * 24, LANES)], 2, yh, recv2, packs, smem=(0,), fan=(0,),
        after=(far0, *queries[1:]),
        room=ROOM,
    )
    recv3 = exchange(send3, ("z", "yh")).reshape(BLOCKS * 24, LANES)
    send_first = call(
        first_read_body, [(TOK, D)] * NX, 4, lazy=[*((q, (0, TOK)) for q in queries), (weights, None)],
        after=(send3,),
    )
    first = back_to_neighbours(send_first)
    tails = call(
        prepare_tails_body, [(2, TOK, D)] * 2, 1, position, lazy=[(qkv, (1, 2))], smem=(0,), after=(send_first[0],)
    )
    near1, far1 = behind(tails[0], 1), behind(tails[1], 2)
    (send_second,) = call(
        second_read_body, [(NX, TOK + 8, D)], 5, x, recv3,
        lazy=[*((q, (TOK, TOK)) for q in queries), (weights, None), (send3, (0, 1))], scratch=[(3 * D, LANES)],
        smem=(0,), after=(tails[0], *first[1:]), room=ROOM,
    )
    second = exchange(send_second, "x")
    (attended0,) = call(
        functools.partial(attention_body, 0), [(TOK, D)], 5, position, lazy=whole(qkv, near0, far0), smem=(0,),
        after=(send_second,),
    )
    readout, send5 = call(
        squares_body, [(GROUPS, TOK, D), (NARROW, 8, GROUPS * TOK)], 1, second, lazy=whole(*first), fan=(1,),
        after=(attended0,), room=SMALL,
    )
    (attended1,) = call(
        functools.partial(attention_body, 1), [(TOK, D)], 5, position, lazy=whole(qkv, near1, far1), smem=(0,),
        after=(send5,),
    )
    recv5 = exchange(send5, "narrow")
    new_weights, new_moment = call(
        own_rows_body, [(3 * ROWS, 1, H), (3 * ROWS, 1, H)], 1, second, own_weights, scratch=[(32, H)],
        after=(send5,), room=SMALL,
    )
    (mixed,) = call(
        mix_body, [(GROUPS, TOK, D)], 1, recv5, ttt_gain.reshape(1, D), readout, attended0, attended1, after=(new_weights,),
        room=SMALL,
    )
    return mixed, new_weights.reshape(1, ROWS, 3, H), new_moment.reshape(1, ROWS, 3, H)


def solution(mesh):
    fine = Mesh(mesh.devices.reshape(NZ, NX, NY, NARROW), ("z", "x", "yh", "narrow"))
    wide = ("z", "x", "yh")
    return jax.shard_map(
        local,
        mesh=fine,
        in_specs=(
            P(None, None, wide, "narrow"),
            P("narrow", wide),
            P("narrow", wide, None, None),
            P("narrow", wide, None, None),
            P("narrow"),
        ),
        out_specs=(
            P(None, wide, "narrow"),
            P("narrow", wide, None, None),
            P("narrow", wide, None, None),
        ),
        check_vma=False,
    )
```

```python
import functools
import math

import jax
import jax.numpy as jnp
from jax import lax
from jax.experimental import pallas as pl
from jax.experimental.pallas import tpu as pltpu
from jax.sharding import Mesh
from jax.sharding import PartitionSpec as P

ATT = 128
WINDOW = 128
EPSILON = 1e-06
MOMENTUM_RATE = 0.9
STEP_SIZE = 0.03
PRECISION = lax.Precision.HIGHEST

NZ, NX, NY = 8, 4, 2
BLOCKS = NZ * NX * NY
ROWS = 10
SLICE = 96
LANES = 128
TOK = 64
D = 640
H = 384
NARROW = 8
GROUPS = 2
VMEM_LIMIT = 58 * 1024 * 1024
ROOM = 8 * 1024 * 1024
SMALL = 42 * 1024 * 1024


def dot(left, right, dims=((1,), (0,))):
    return lax.dot_general(
        left, right, (dims, ((), ())), precision=PRECISION, preferred_element_type=jnp.float32
    )


def entry(group, sublane):
    q = group * 8 + sublane
    return (q // 3, q % 3) if q < 3 * ROWS else None


def call(body, outs, micros, *args, lazy=(), after=(), scratch=(), smem=(), fan=(), room=0):
    vmem, anywhere = pl.BlockSpec(memory_space=pltpu.VMEM), pl.BlockSpec(memory_space=pl.ANY)
    held = [outs[n][1:] if n in fan else outs[n] for n in range(len(outs))]
    lazy_shapes = [a.shape if at is None else (at[1], *a.shape[1:]) for a, at in lazy]
    sizes = (len(args), len(lazy), len(after), len(outs), len(outs), len(lazy), len(scratch))
    fetches = max(len(lazy), 1)
    sends = sum(outs[n][0] if n in fan else 1 for n in range(len(outs)))

    def kernel(*refs):
        split, at = [], 0
        for size in sizes:
            split.append(refs[at : at + size])
            at += size
        inputs, sources, _, targets, results, fetched, spare = split
        in_sems, out_sems = refs[at:]
        incoming = [
            pltpu.make_async_copy(ref if lazy[n][1] is None else ref.at[pl.ds(*lazy[n][1])], fetched[n], in_sems.at[n])
            for n, ref in enumerate(sources)
        ]
        for copy in incoming:
            copy.start()
        outgoing, base = [], 0
        for n in range(len(outs)):
            places = [targets[n].at[j] for j in range(outs[n][0])] if n in fan else [targets[n]]
            outgoing.append(
                [pltpu.make_async_copy(results[n], place, out_sems.at[base + j]) for j, place in enumerate(places)]
            )
            base += len(places)
        sent = set()

        def need():
            for copy in incoming:
                copy.wait()

        def send(n):
            sent.add(n)
            for copy in outgoing[n]:
                copy.start()

        body(inputs, fetched, results, spare, need, send)
        for n in range(len(outs)):
            if n not in sent:
                send(n)
        for copies in outgoing:
            for copy in copies:
                copy.wait()

    return pl.pallas_call(
        kernel,
        out_shape=[jax.ShapeDtypeStruct(s, jnp.float32) for s in outs],
        in_specs=[pl.BlockSpec(memory_space=pltpu.SMEM) if n in smem else vmem for n in range(len(args))]
        + [anywhere] * (len(lazy) + len(after)),
        out_specs=[anywhere] * len(outs),
        scratch_shapes=[
            *(pltpu.VMEM(tuple(s), jnp.float32) for s in (*held, *lazy_shapes, *scratch)),
            pltpu.SemaphoreType.DMA((fetches,)),
            pltpu.SemaphoreType.DMA((sends,)),
        ],
        compiler_params=pltpu.CompilerParams(vmem_limit_bytes=VMEM_LIMIT - room),
        cost_estimate=pl.CostEstimate(flops=int(micros * 1e9), bytes_accessed=10**6, transcendentals=0),
    )(*args, *(a for a, _ in lazy), *after)


def to_column(row):
    n = row.shape[1]
    same = lax.broadcasted_iota(jnp.int32, (n, n), 0) == lax.broadcasted_iota(jnp.int32, (n, n), 1)
    return jnp.sum(jnp.where(same, row, 0.0), axis=1, keepdims=True)


def to_row(column):
    n = column.shape[0]
    same = lax.broadcasted_iota(jnp.int32, (n, n), 0) == lax.broadcasted_iota(jnp.int32, (n, n), 1)
    return jnp.sum(jnp.where(same, column, 0.0), axis=0, keepdims=True)


def own_packs(own_ref, flat_ref):
    flat_ref[24:32, :] = jnp.zeros((8, H), jnp.float32)
    for q in range(3 * ROWS):
        flat_ref[q : q + 1, :] = own_ref[q]
    return [
        jnp.concatenate(
            [flat_ref[8 * g : 8 * g + 8, SLICE * x : SLICE * (x + 1)] for g in range(4)], axis=1
        )
        for x in range(NX)
    ]


def prepare_weights_body(args, lazy, results, scratch, need, send):
    packs = own_packs(args[0], scratch[0])
    for z in range(NZ):
        for x in range(NX):
            for y in range(NY):
                for t in range(3):
                    results[0][(z * NX + x) * NY + y, 8 * t : 8 * t + 8, :] = packs[x][:, LANES * t : LANES * (t + 1)]


def prepare_pairs_body(args, lazy, results, scratch, need, send):
    eta_ref, qkv_ref = args
    results[0][0:TOK, :] = qkv_ref[1, 0]
    results[0][TOK : 2 * TOK, :] = to_column(eta_ref[...]) * qkv_ref[2, 0]


def prepare_queries_body(args, lazy, results, scratch, need, send):
    (mom_ref,), (qkv_ref,), (queries_ref,) = args, lazy, results
    packs = own_packs(mom_ref, scratch[0])
    for x in range(NX):
        queries_ref[2 * TOK + 8 * x : 2 * TOK + 8 * x + 8, 0:H] = packs[x]
        queries_ref[2 * TOK + 8 * x : 2 * TOK + 8 * x + 8, H:D] = jnp.zeros((8, D - H), jnp.float32)
    need()
    queries_ref[0:TOK, :] = qkv_ref[0, 0]
    queries_ref[TOK : 2 * TOK, :] = qkv_ref[0, 1]


def widened(part):
    return jnp.concatenate([part, jnp.zeros((part.shape[0], LANES - SLICE), jnp.float32)], axis=1)


def unpack(recv_ref, out_ref, x_stride, y_stride, z_stride):
    for s in range(8):
        for x in range(NX):
            for y in range(NY):
                start = x * x_stride + y * y_stride + s
                rows = jnp.concatenate(
                    [recv_ref[pl.ds(start + 8 * t, NZ, stride=z_stride), :] for t in range(3)], axis=1
                )
                for g in range(4):
                    at = entry(g, s)
                    if at is None:
                        continue
                    r, i = at
                    out_ref[pl.ds(i * D + (x * NY + y) * ROWS + r, NZ, stride=NX * NY * ROWS), :] = widened(
                        rows[:, SLICE * g : SLICE * (g + 1)]
                    )


def pack(in_ref, send_ref, x_stride, y_stride, z_stride):
    for s in range(8):
        for x in range(NX):
            for y in range(NY):
                parts = []
                for g in range(4):
                    at = entry(g, s)
                    if at is None:
                        parts.append(jnp.zeros((NZ, SLICE), jnp.float32))
                        continue
                    r, i = at
                    parts.append(in_ref[pl.ds(i * D + (x * NY + y) * ROWS + r, NZ, stride=NX * NY * ROWS), :][:, :SLICE])
                rows = jnp.concatenate(parts, axis=1)
                start = x * x_stride + y * y_stride + s
                for t in range(3):
                    send_ref[pl.ds(start + 8 * t, NZ, stride=z_stride), :] = rows[:, LANES * t : LANES * (t + 1)]


def token_rows(refs, start):
    return jnp.concatenate([ref[start : start + TOK, :] for ref in refs], axis=0)


def matrix(ref, i):
    return ref[i * D : (i + 1) * D, :]


def gradient_body(args, pairs, results, scratch, need, send):
    (recv_ref,), (w_ref, send_ref), (g_ref,) = args, results, scratch
    unpack(recv_ref, w_ref, 48, 24, 192)
    send(0)
    need()
    keys = token_rows(pairs, 0)
    weighted = token_rows(pairs, TOK)
    pre = dot(keys, jnp.concatenate([matrix(w_ref, 0), matrix(w_ref, 1)], axis=1))
    gate_pre, up_pre = pre[:, :LANES], pre[:, LANES:]
    back = -dot(weighted, matrix(w_ref, 2))
    sigmoid = jax.nn.sigmoid(gate_pre)
    gated = gate_pre * sigmoid
    hidden = gated * up_pre
    gate_back = back * up_pre * sigmoid * (1.0 + gate_pre * (1.0 - sigmoid))
    up_back = back * gated
    both = dot(keys, jnp.concatenate([gate_back, up_back], axis=1), ((0,), (0,)))
    g_ref[0:D, :] = both[:, :LANES]
    g_ref[D : 2 * D, :] = both[:, LANES:]
    g_ref[2 * D : 3 * D, :] = -dot(weighted, hidden, ((0,), (0,)))
    pack(g_ref, send_ref, 24, 96, 192)


def source(x_ref, s):
    return lax.rem(x_ref[0] + NX - s, NX)


def moment_body(args, tails, results, scratch, need, send):
    (x_ref, recv_ref), (own_ref,) = args, results
    total = recv_ref[0]
    for j in range(1, NZ * NY):
        total = total + recv_ref[j]
    own_ref[...] = total
    need()
    mine = pl.ds(pl.multiple_of(8 * x_ref[0], 8), 8)
    for s, ref in enumerate(tails):
        old = ref[mine, :]
        old = jnp.concatenate([old[:, LANES * t : LANES * (t + 1)] for t in range(3)], axis=0)
        rows = pl.ds(pl.multiple_of(24 * source(x_ref, s), 8), 24)
        own_ref[rows, :] = own_ref[rows, :] + MOMENTUM_RATE * old


def hidden_of(inputs, w1, w3):
    pre = dot(inputs, jnp.concatenate([w1, w3], axis=1))
    gate_pre, up_pre = pre[:, :LANES], pre[:, LANES:]
    return gate_pre * jax.nn.sigmoid(gate_pre) * up_pre


def first_read_body(args, lazy, results, scratch, need, send):
    need()
    *queries, w_ref = lazy
    hidden = hidden_of(token_rows(queries, 0), matrix(w_ref, 0), matrix(w_ref, 1))
    partial = dot(hidden, matrix(w_ref, 2), ((1,), (1,)))
    for s in range(NX):
        results[s][...] = partial[s * TOK : (s + 1) * TOK]


def renormalized(weights, moment):
    rate = STEP_SIZE / jnp.sqrt(jnp.mean(moment * moment, axis=0, keepdims=True) + EPSILON)
    moved = weights - moment * rate
    ratio = jnp.sqrt(jnp.mean(weights * weights, axis=0, keepdims=True) + EPSILON) / jnp.sqrt(
        jnp.mean(moved * moved, axis=0, keepdims=True) + EPSILON
    )
    return moved * ratio, rate, ratio


def second_read_body(args, lazy, results, scratch, need, send):
    (x_ref, recv_ref), (*queries, w_ref, moment_ref), (send_ref,), (m_ref,) = args, lazy, results, scratch
    unpack(recv_ref, m_ref, 24, 96, 192)
    need()
    new1, rate1, ratio1 = renormalized(matrix(w_ref, 0), matrix(m_ref, 0))
    new3, rate3, ratio3 = renormalized(matrix(w_ref, 1), matrix(m_ref, 1))
    new2, rate2, ratio2 = renormalized(matrix(w_ref, 2), matrix(m_ref, 2))
    hidden = hidden_of(token_rows(queries, 0), new1, new3)
    partial = dot(hidden, new2, ((1,), (1,)))
    stats = [rate1, rate3, rate2, ratio1, ratio3, ratio2, jnp.zeros((2, LANES), jnp.float32)]
    stats = jnp.concatenate(stats, axis=0)
    for x in range(NX):
        tail = [stats, *(moment_ref[0, 24 * x + 8 * t : 24 * x + 8 * t + 8, :] for t in range(3))]
        tail.append(jnp.zeros((8, LANES), jnp.float32))
        send_ref[x, TOK : TOK + 8, :] = jnp.concatenate(tail, axis=1)
    for s in range(NX):
        send_ref[source(x_ref, s), 0:TOK, :] = partial[s * TOK : (s + 1) * TOK]


def squares_body(args, lazy, results, scratch, need, send):
    (second_ref,), (readout_ref, send_ref) = args, results
    need()
    first = lazy[0][...] + lazy[1][...] + lazy[2][...] + lazy[3][...]
    second = second_ref[0, 0:TOK, :]
    for x in range(1, NX):
        second = second + second_ref[x, 0:TOK, :]
    readout_ref[0] = first
    readout_ref[1] = second
    row = jnp.concatenate(
        [to_row(jnp.sum(total * total, axis=1, keepdims=True)) for total in (first, second)], axis=1
    )
    send_ref[...] = jnp.broadcast_to(row, (8, GROUPS * TOK))


def own_rows_body(args, lazy, results, scratch, need, send):
    (second_ref, fw_ref), (new_w_ref, new_m_ref), (flat_ref,) = args, results, scratch
    for g in range(4):
        flat_ref[8 * g : 8 * g + 8, :] = jnp.concatenate(
            [
                second_ref[x, TOK : TOK + 8, LANES + SLICE * g : LANES + SLICE * (g + 1)]
                for x in range(NX)
            ],
            axis=1,
        )
    stats = jnp.concatenate([second_ref[x, TOK : TOK + 8, 0:SLICE] for x in range(NX)], axis=1)
    for q in range(3 * ROWS):
        i = q % 3
        moment = flat_ref[q : q + 1, :]
        new_m_ref[q] = moment
        new_w_ref[q] = (fw_ref[q] - moment * stats[i : i + 1]) * stats[3 + i : 4 + i]


def mix_body(args, lazy, results, scratch, need, send):
    (recv_ref, gain_ref, readout_ref, attended_ref), (mixed_ref,) = args, results
    total = recv_ref[0, 0:1, :]
    for n in range(1, NARROW):
        total = total + recv_ref[n, 0:1, :]
    scale = to_column(1.0 / jnp.sqrt(total / (D * NARROW) + EPSILON))
    for c in range(GROUPS):
        mixed_ref[c] = attended_ref[c] + gain_ref[...] * (readout_ref[c] * scale[c * TOK : (c + 1) * TOK])


def attention_body(args, lazy, results, scratch, need, send):
    (position_ref,), (qkv_ref, near_ref, far_ref), (out_ref,) = args, lazy, results
    position = position_ref[0]
    row = lax.broadcasted_iota(jnp.int32, (TOK, 3 * TOK), 0) + 2 * TOK
    col = lax.broadcasted_iota(jnp.int32, (TOK, 3 * TOK), 1)
    window = (row - col >= 0) & (row - col < WINDOW)
    first = jnp.where(position >= 2, 0, jnp.where(position >= 1, TOK, 2 * TOK))
    need()
    for c in range(GROUPS):
        allowed = window & (col >= first) if c == 0 else window
        for h in range(D // ATT):
            at = slice(h * ATT, (h + 1) * ATT)
            parts = []
            for a in range(2):
                far, near = far_ref[a, c, :, at], near_ref[a, c, :, at]
                if c == 1:
                    far = jnp.where(position >= 2, far, far_ref[a, 0, :, at])
                    near = jnp.where(position >= 1, near, near_ref[a, 0, :, at])
                parts.append(jnp.concatenate([far, near, qkv_ref[1 + a, c, :, at]], axis=0))
            keys, values = parts
            scores = dot(qkv_ref[0, c, :, at], keys, ((1,), (1,))) * (1.0 / math.sqrt(ATT))
            scores = jnp.where(allowed, scores, -1e30)
            weights = jnp.exp(scores - jnp.max(scores, axis=1, keepdims=True))
            weights = weights / jnp.sum(weights, axis=1, keepdims=True)
            out_ref[c, :, at] = dot(weights, values)


def behind(block, distance):
    axes = ("z", "x", "yh")
    return lax.ppermute(block, axes, [((i - distance) % BLOCKS, i) for i in range(BLOCKS)])


def from_neighbours(block):
    return [block] + [lax.ppermute(block, "x", [((i - s) % NX, i) for i in range(NX)]) for s in range(1, NX)]


def relayed_from_neighbours(block):
    behind_one = lax.ppermute(block, "x", [((i - 1) % NX, i) for i in range(NX)])
    from_ahead = [((i + 1) % NX, i) for i in range(NX)]
    ahead_one = lax.ppermute(block, "x", from_ahead)
    return [block, behind_one, lax.ppermute(ahead_one, "x", from_ahead), ahead_one]


def back_to_neighbours(blocks):
    return [blocks[0]] + [
        lax.ppermute(blocks[s], "x", [(i, (i - s) % NX) for i in range(NX)]) for s in range(1, NX)
    ]


def exchange(pieces, axes):
    return lax.all_to_all(pieces, axes, split_axis=0, concat_axis=0, tiled=True)


def scalar(value):
    return jnp.reshape(value, (1,)).astype(jnp.int32)


def whole(*arrays):
    return [(a, None) for a in arrays]


def local(qkv, eta, fast_weights, momentum, ttt_gain):
    own_weights, own_moment = fast_weights.reshape(3 * ROWS, 1, H), momentum.reshape(3 * ROWS, 1, H)
    x = lax.axis_index("x")
    position = scalar((lax.axis_index("z") * NX + x) * NY + lax.axis_index("yh"))
    x = scalar(x)
    (send1,) = call(prepare_weights_body, [(BLOCKS, 24, LANES)], 1, own_weights, scratch=[(32, H)], room=SMALL)
    (pairs,) = call(prepare_pairs_body, [(2 * TOK, D)], 1, eta, qkv, room=SMALL)
    recv1 = exchange(send1, ("z", "x", "yh")).reshape(BLOCKS * 24, LANES)
    pairs = relayed_from_neighbours(pairs)
    near, far = behind(qkv[1:], 1), behind(qkv[1:], 2)
    weights, send2 = call(
        gradient_body, [(3 * D, LANES), (BLOCKS * 24, LANES)], 5, recv1, lazy=whole(*pairs),
        scratch=[(3 * D, LANES)], room=ROOM - 512 * 1024,
    )
    recv2 = exchange(send2.reshape(NZ * NY, NX * 24, LANES), ("z", "yh"))
    (queries,) = call(
        prepare_queries_body, [(2 * TOK + 32, D)], 0.1, own_moment, lazy=[(qkv, (0, 1))], scratch=[(32, H)],
        after=(weights,),
    )
    queries = from_neighbours(queries)
    (attended,) = call(
        attention_body, [(GROUPS, TOK, D)], 12, position, lazy=whole(qkv, near, far), smem=(0,)
    )
    (send3,) = call(
        moment_body, [(NZ * NY, NX * 24, LANES)], 2, x, recv2, lazy=[(q, (2 * TOK, 32)) for q in queries],
        smem=(0,), fan=(0,), after=(attended,), room=ROOM,
    )
    recv3 = exchange(send3, ("z", "yh")).reshape(BLOCKS * 24, LANES)
    first = back_to_neighbours(
        call(
            first_read_body, [(TOK, D)] * NX, 4, lazy=[*((q, (0, TOK)) for q in queries), (weights, None)],
            after=(send3,),
        )
    )
    (send_second,) = call(
        second_read_body, [(NX, TOK + 8, D)], 5, x, recv3,
        lazy=[*((q, (TOK, TOK)) for q in queries), (weights, None), (send3, (0, 1))], scratch=[(3 * D, LANES)],
        smem=(0,), after=first[1:], room=ROOM,
    )
    second = exchange(send_second, "x")
    readout, send5 = call(
        squares_body, [(GROUPS, TOK, D), (NARROW, 8, GROUPS * TOK)], 1, second, lazy=whole(*first), fan=(1,),
        room=SMALL,
    )
    recv5 = exchange(send5, "narrow")
    new_weights, new_moment = call(
        own_rows_body, [(3 * ROWS, 1, H), (3 * ROWS, 1, H)], 1, second, own_weights, scratch=[(32, H)],
        after=(send5,), room=SMALL,
    )
    (mixed,) = call(
        mix_body, [(GROUPS, TOK, D)], 1, recv5, ttt_gain.reshape(1, D), readout, attended, after=(new_weights,),
        room=SMALL,
    )
    return mixed, new_weights.reshape(1, ROWS, 3, H), new_moment.reshape(1, ROWS, 3, H)


def solution(mesh):
    fine = Mesh(mesh.devices.reshape(NZ, NX, NY, NARROW), ("z", "x", "yh", "narrow"))
    wide = ("z", "x", "yh")
    return jax.shard_map(
        local,
        mesh=fine,
        in_specs=(
            P(None, None, wide, "narrow"),
            P("narrow", wide),
            P("narrow", wide, None, None),
            P("narrow", wide, None, None),
            P("narrow"),
        ),
        out_specs=(
            P(None, wide, "narrow"),
            P("narrow", wide, None, None),
            P("narrow", wide, None, None),
        ),
        check_vma=False,
    )
```

```python
import functools
import math

import jax
import jax.numpy as jnp
from jax import lax
from jax.experimental import pallas as pl
from jax.experimental.pallas import tpu as pltpu
from jax.sharding import Mesh
from jax.sharding import PartitionSpec as P

ATT = 128
WINDOW = 128
EPSILON = 1e-06
MOMENTUM_RATE = 0.9
STEP_SIZE = 0.03
PRECISION = lax.Precision.HIGHEST

NZ, NX, NY = 8, 4, 2
BLOCKS = NZ * NX * NY
ROWS = 10
SLICE = 96
LANES = 128
TOK = 64
D = 640
H = 384
NARROW = 8
GROUPS = 2
VMEM_LIMIT = 58 * 1024 * 1024
ROOM = 8 * 1024 * 1024
SMALL = 42 * 1024 * 1024


def dot(left, right, dims=((1,), (0,))):
    return lax.dot_general(
        left, right, (dims, ((), ())), precision=PRECISION, preferred_element_type=jnp.float32
    )


def entry(group, sublane):
    q = group * 8 + sublane
    return (q // 3, q % 3) if q < 3 * ROWS else None


def call(body, outs, micros, *args, lazy=(), after=(), scratch=(), smem=(), fan=(), room=0):
    vmem, anywhere = pl.BlockSpec(memory_space=pltpu.VMEM), pl.BlockSpec(memory_space=pl.ANY)
    held = [outs[n][1:] if n in fan else outs[n] for n in range(len(outs))]
    lazy_shapes = [a.shape if at is None else (at[1], *a.shape[1:]) for a, at in lazy]
    sizes = (len(args), len(lazy), len(after), len(outs), len(outs), len(lazy), len(scratch))
    fetches = max(len(lazy), 1)
    sends = sum(outs[n][0] if n in fan else 1 for n in range(len(outs)))

    def kernel(*refs):
        split, at = [], 0
        for size in sizes:
            split.append(refs[at : at + size])
            at += size
        inputs, sources, _, targets, results, fetched, spare = split
        in_sems, out_sems = refs[at:]
        incoming = [
            pltpu.make_async_copy(ref if lazy[n][1] is None else ref.at[pl.ds(*lazy[n][1])], fetched[n], in_sems.at[n])
            for n, ref in enumerate(sources)
        ]
        for copy in incoming:
            copy.start()
        outgoing, base = [], 0
        for n in range(len(outs)):
            places = [targets[n].at[j] for j in range(outs[n][0])] if n in fan else [targets[n]]
            outgoing.append(
                [pltpu.make_async_copy(results[n], place, out_sems.at[base + j]) for j, place in enumerate(places)]
            )
            base += len(places)
        sent = set()

        def need():
            for copy in incoming:
                copy.wait()

        def send(n):
            sent.add(n)
            for copy in outgoing[n]:
                copy.start()

        body(inputs, fetched, results, spare, need, send)
        for n in range(len(outs)):
            if n not in sent:
                send(n)
        for copies in outgoing:
            for copy in copies:
                copy.wait()

    return pl.pallas_call(
        kernel,
        out_shape=[jax.ShapeDtypeStruct(s, jnp.float32) for s in outs],
        in_specs=[pl.BlockSpec(memory_space=pltpu.SMEM) if n in smem else vmem for n in range(len(args))]
        + [anywhere] * (len(lazy) + len(after)),
        out_specs=[anywhere] * len(outs),
        scratch_shapes=[
            *(pltpu.VMEM(tuple(s), jnp.float32) for s in (*held, *lazy_shapes, *scratch)),
            pltpu.SemaphoreType.DMA((fetches,)),
            pltpu.SemaphoreType.DMA((sends,)),
        ],
        compiler_params=pltpu.CompilerParams(vmem_limit_bytes=VMEM_LIMIT - room),
        cost_estimate=pl.CostEstimate(flops=int(micros * 1e9), bytes_accessed=10**6, transcendentals=0),
    )(*args, *(a for a, _ in lazy), *after)


def to_column(row):
    n = row.shape[1]
    same = lax.broadcasted_iota(jnp.int32, (n, n), 0) == lax.broadcasted_iota(jnp.int32, (n, n), 1)
    return jnp.sum(jnp.where(same, row, 0.0), axis=1, keepdims=True)


def to_row(column):
    n = column.shape[0]
    same = lax.broadcasted_iota(jnp.int32, (n, n), 0) == lax.broadcasted_iota(jnp.int32, (n, n), 1)
    return jnp.sum(jnp.where(same, column, 0.0), axis=0, keepdims=True)


def own_packs(own_ref, flat_ref):
    flat_ref[24:32, :] = jnp.zeros((8, H), jnp.float32)
    for q in range(3 * ROWS):
        flat_ref[q : q + 1, :] = own_ref[q]
    return [
        jnp.concatenate(
            [flat_ref[8 * g : 8 * g + 8, SLICE * x : SLICE * (x + 1)] for g in range(4)], axis=1
        )
        for x in range(NX)
    ]


def prepare_weights_body(args, lazy, results, scratch, need, send):
    packs = own_packs(args[0], scratch[0])
    for z in range(NZ):
        for x in range(NX):
            for y in range(NY):
                for t in range(3):
                    results[0][(z * NX + x) * NY + y, 8 * t : 8 * t + 8, :] = packs[x][:, LANES * t : LANES * (t + 1)]


def prepare_pairs_body(args, lazy, results, scratch, need, send):
    eta_ref, qkv_ref = args
    results[0][0:TOK, :] = qkv_ref[1, 0]
    results[0][TOK : 2 * TOK, :] = to_column(eta_ref[...]) * qkv_ref[2, 0]


def prepare_queries_body(args, lazy, results, scratch, need, send):
    (mom_ref,), (qkv_ref,), (queries_ref,) = args, lazy, results
    packs = own_packs(mom_ref, scratch[0])
    for x in range(NX):
        queries_ref[2 * TOK + 8 * x : 2 * TOK + 8 * x + 8, 0:H] = packs[x]
        queries_ref[2 * TOK + 8 * x : 2 * TOK + 8 * x + 8, H:D] = jnp.zeros((8, D - H), jnp.float32)
    need()
    queries_ref[0:TOK, :] = qkv_ref[0, 0]
    queries_ref[TOK : 2 * TOK, :] = qkv_ref[0, 1]


def marker_body(args, lazy, results, scratch, need, send):
    results[0][...] = jnp.zeros((8, LANES), jnp.float32)


def widened(part):
    return jnp.concatenate([part, jnp.zeros((part.shape[0], LANES - SLICE), jnp.float32)], axis=1)


def unpack(recv_ref, out_ref, x_stride, y_stride, z_stride):
    for s in range(8):
        for x in range(NX):
            for y in range(NY):
                start = x * x_stride + y * y_stride + s
                rows = jnp.concatenate(
                    [recv_ref[pl.ds(start + 8 * t, NZ, stride=z_stride), :] for t in range(3)], axis=1
                )
                for g in range(4):
                    at = entry(g, s)
                    if at is None:
                        continue
                    r, i = at
                    out_ref[pl.ds(i * D + (x * NY + y) * ROWS + r, NZ, stride=NX * NY * ROWS), :] = widened(
                        rows[:, SLICE * g : SLICE * (g + 1)]
                    )


def pack(in_ref, send_ref, x_stride, y_stride, z_stride):
    for s in range(8):
        for x in range(NX):
            for y in range(NY):
                parts = []
                for g in range(4):
                    at = entry(g, s)
                    if at is None:
                        parts.append(jnp.zeros((NZ, SLICE), jnp.float32))
                        continue
                    r, i = at
                    parts.append(in_ref[pl.ds(i * D + (x * NY + y) * ROWS + r, NZ, stride=NX * NY * ROWS), :][:, :SLICE])
                rows = jnp.concatenate(parts, axis=1)
                start = x * x_stride + y * y_stride + s
                for t in range(3):
                    send_ref[pl.ds(start + 8 * t, NZ, stride=z_stride), :] = rows[:, LANES * t : LANES * (t + 1)]


def token_rows(refs, start):
    return jnp.concatenate([ref[start : start + TOK, :] for ref in refs], axis=0)


def matrix(ref, i):
    return ref[i * D : (i + 1) * D, :]


def gradient_body(args, pairs, results, scratch, need, send):
    (recv_ref,), (w_ref, send_ref), (g_ref,) = args, results, scratch
    unpack(recv_ref, w_ref, 48, 24, 192)
    send(0)
    need()
    keys = token_rows(pairs, 0)
    weighted = token_rows(pairs, TOK)
    pre = dot(keys, jnp.concatenate([matrix(w_ref, 0), matrix(w_ref, 1)], axis=1))
    gate_pre, up_pre = pre[:, :LANES], pre[:, LANES:]
    back = -dot(weighted, matrix(w_ref, 2))
    sigmoid = jax.nn.sigmoid(gate_pre)
    gated = gate_pre * sigmoid
    hidden = gated * up_pre
    gate_back = back * up_pre * sigmoid * (1.0 + gate_pre * (1.0 - sigmoid))
    up_back = back * gated
    both = dot(keys, jnp.concatenate([gate_back, up_back], axis=1), ((0,), (0,)))
    g_ref[0:D, :] = both[:, :LANES]
    g_ref[D : 2 * D, :] = both[:, LANES:]
    g_ref[2 * D : 3 * D, :] = -dot(weighted, hidden, ((0,), (0,)))
    pack(g_ref, send_ref, 24, 96, 192)


def source(x_ref, s):
    return lax.rem(x_ref[0] + NX - s, NX)


def moment_body(args, tails, results, scratch, need, send):
    (x_ref, recv_ref), (own_ref,) = args, results
    total = recv_ref[0]
    for j in range(1, NZ * NY):
        total = total + recv_ref[j]
    own_ref[...] = total
    need()
    mine = pl.ds(pl.multiple_of(8 * x_ref[0], 8), 8)
    for s, ref in enumerate(tails):
        old = ref[mine, :]
        old = jnp.concatenate([old[:, LANES * t : LANES * (t + 1)] for t in range(3)], axis=0)
        rows = pl.ds(pl.multiple_of(24 * source(x_ref, s), 8), 24)
        own_ref[rows, :] = own_ref[rows, :] + MOMENTUM_RATE * old


def hidden_of(inputs, w1, w3):
    pre = dot(inputs, jnp.concatenate([w1, w3], axis=1))
    gate_pre, up_pre = pre[:, :LANES], pre[:, LANES:]
    return gate_pre * jax.nn.sigmoid(gate_pre) * up_pre


def first_read_body(args, lazy, results, scratch, need, send):
    need()
    *queries, w_ref = lazy
    hidden = hidden_of(token_rows(queries, 0), matrix(w_ref, 0), matrix(w_ref, 1))
    partial = dot(hidden, matrix(w_ref, 2), ((1,), (1,)))
    for s in range(NX):
        results[s][...] = partial[s * TOK : (s + 1) * TOK]


def renormalized(weights, moment):
    rate = STEP_SIZE / jnp.sqrt(jnp.mean(moment * moment, axis=0, keepdims=True) + EPSILON)
    moved = weights - moment * rate
    ratio = jnp.sqrt(jnp.mean(weights * weights, axis=0, keepdims=True) + EPSILON) / jnp.sqrt(
        jnp.mean(moved * moved, axis=0, keepdims=True) + EPSILON
    )
    return moved * ratio, rate, ratio


def second_read_body(args, lazy, results, scratch, need, send):
    (x_ref, recv_ref), (*queries, w_ref, moment_ref), (send_ref,), (m_ref,) = args, lazy, results, scratch
    unpack(recv_ref, m_ref, 24, 96, 192)
    need()
    new1, rate1, ratio1 = renormalized(matrix(w_ref, 0), matrix(m_ref, 0))
    new3, rate3, ratio3 = renormalized(matrix(w_ref, 1), matrix(m_ref, 1))
    new2, rate2, ratio2 = renormalized(matrix(w_ref, 2), matrix(m_ref, 2))
    hidden = hidden_of(token_rows(queries, 0), new1, new3)
    partial = dot(hidden, new2, ((1,), (1,)))
    stats = [rate1, rate3, rate2, ratio1, ratio3, ratio2, jnp.zeros((2, LANES), jnp.float32)]
    stats = jnp.concatenate(stats, axis=0)
    for x in range(NX):
        tail = [stats, *(moment_ref[0, 24 * x + 8 * t : 24 * x + 8 * t + 8, :] for t in range(3))]
        tail.append(jnp.zeros((8, LANES), jnp.float32))
        send_ref[x, TOK : TOK + 8, :] = jnp.concatenate(tail, axis=1)
    for s in range(NX):
        send_ref[source(x_ref, s), 0:TOK, :] = partial[s * TOK : (s + 1) * TOK]


def squares_body(args, lazy, results, scratch, need, send):
    (second_ref,), (readout_ref, send_ref) = args, results
    need()
    first = lazy[0][...] + lazy[1][...] + lazy[2][...] + lazy[3][...]
    second = second_ref[0, 0:TOK, :]
    for x in range(1, NX):
        second = second + second_ref[x, 0:TOK, :]
    readout_ref[0] = first
    readout_ref[1] = second
    row = jnp.concatenate(
        [to_row(jnp.sum(total * total, axis=1, keepdims=True)) for total in (first, second)], axis=1
    )
    send_ref[...] = jnp.broadcast_to(row, (8, GROUPS * TOK))


def own_rows_body(args, lazy, results, scratch, need, send):
    (second_ref, fw_ref), (new_w_ref, new_m_ref), (flat_ref,) = args, results, scratch
    for g in range(4):
        flat_ref[8 * g : 8 * g + 8, :] = jnp.concatenate(
            [
                second_ref[x, TOK : TOK + 8, LANES + SLICE * g : LANES + SLICE * (g + 1)]
                for x in range(NX)
            ],
            axis=1,
        )
    stats = jnp.concatenate([second_ref[x, TOK : TOK + 8, 0:SLICE] for x in range(NX)], axis=1)
    for q in range(3 * ROWS):
        i = q % 3
        moment = flat_ref[q : q + 1, :]
        new_m_ref[q] = moment
        new_w_ref[q] = (fw_ref[q] - moment * stats[i : i + 1]) * stats[3 + i : 4 + i]


def mix_body(args, lazy, results, scratch, need, send):
    (recv_ref, gain_ref, readout_ref, attended_ref), (mixed_ref,) = args, results
    total = recv_ref[0, 0:1, :]
    for n in range(1, NARROW):
        total = total + recv_ref[n, 0:1, :]
    scale = to_column(1.0 / jnp.sqrt(total / (D * NARROW) + EPSILON))
    for c in range(GROUPS):
        mixed_ref[c] = attended_ref[c] + gain_ref[...] * (readout_ref[c] * scale[c * TOK : (c + 1) * TOK])


def attention_body(args, lazy, results, scratch, need, send):
    (position_ref,), (qkv_ref, near_ref, far_ref), (out_ref,) = args, lazy, results
    position = position_ref[0]
    row = lax.broadcasted_iota(jnp.int32, (TOK, 3 * TOK), 0) + 2 * TOK
    col = lax.broadcasted_iota(jnp.int32, (TOK, 3 * TOK), 1)
    window = (row - col >= 0) & (row - col < WINDOW)
    first = jnp.where(position >= 2, 0, jnp.where(position >= 1, TOK, 2 * TOK))
    need()
    for c in range(GROUPS):
        allowed = window & (col >= first) if c == 0 else window
        for h in range(D // ATT):
            at = slice(h * ATT, (h + 1) * ATT)
            parts = []
            for a in range(2):
                far, near = far_ref[a, c, :, at], near_ref[a, c, :, at]
                if c == 1:
                    far = jnp.where(position >= 2, far, far_ref[a, 0, :, at])
                    near = jnp.where(position >= 1, near, near_ref[a, 0, :, at])
                parts.append(jnp.concatenate([far, near, qkv_ref[1 + a, c, :, at]], axis=0))
            keys, values = parts
            scores = dot(qkv_ref[0, c, :, at], keys, ((1,), (1,))) * (1.0 / math.sqrt(ATT))
            scores = jnp.where(allowed, scores, -1e30)
            weights = jnp.exp(scores - jnp.max(scores, axis=1, keepdims=True))
            weights = weights / jnp.sum(weights, axis=1, keepdims=True)
            out_ref[c, :, at] = dot(weights, values)


def behind(block, distance):
    axes = ("z", "x", "yh")
    return lax.ppermute(block, axes, [((i - distance) % BLOCKS, i) for i in range(BLOCKS)])


def from_neighbours(block):
    return [block] + [lax.ppermute(block, "x", [((i - s) % NX, i) for i in range(NX)]) for s in range(1, NX)]


def relayed_from_neighbours(block):
    behind_one = lax.ppermute(block, "x", [((i - 1) % NX, i) for i in range(NX)])
    from_ahead = [((i + 1) % NX, i) for i in range(NX)]
    ahead_one = lax.ppermute(block, "x", from_ahead)
    return [block, behind_one, lax.ppermute(ahead_one, "x", from_ahead), ahead_one]


def back_to_neighbours(blocks):
    return [blocks[0]] + [
        lax.ppermute(blocks[s], "x", [(i, (i - s) % NX) for i in range(NX)]) for s in range(1, NX)
    ]


def exchange(pieces, axes):
    return lax.all_to_all(pieces, axes, split_axis=0, concat_axis=0, tiled=True)


def scalar(value):
    return jnp.reshape(value, (1,)).astype(jnp.int32)


def whole(*arrays):
    return [(a, None) for a in arrays]


def local(qkv, eta, fast_weights, momentum, ttt_gain):
    own_weights, own_moment = fast_weights.reshape(3 * ROWS, 1, H), momentum.reshape(3 * ROWS, 1, H)
    x = lax.axis_index("x")
    position = scalar((lax.axis_index("z") * NX + x) * NY + lax.axis_index("yh"))
    x = scalar(x)
    (send1,) = call(prepare_weights_body, [(BLOCKS, 24, LANES)], 1, own_weights, scratch=[(32, H)], room=SMALL)
    (pairs,) = call(prepare_pairs_body, [(2 * TOK, D)], 1, eta, qkv, room=SMALL)
    recv1 = exchange(send1, ("z", "x", "yh")).reshape(BLOCKS * 24, LANES)
    pairs = relayed_from_neighbours(pairs)
    near, far = behind(qkv[1:], 1), behind(qkv[1:], 2)
    weights, send2 = call(
        gradient_body, [(3 * D, LANES), (BLOCKS * 24, LANES)], 5, recv1, lazy=whole(*pairs),
        scratch=[(3 * D, LANES)], room=ROOM - 512 * 1024,
    )
    recv2 = exchange(send2.reshape(NZ * NY, NX * 24, LANES), ("z", "yh"))
    (queries,) = call(
        prepare_queries_body, [(2 * TOK + 32, D)], 0.1, own_moment, lazy=[(qkv, (0, 1))], scratch=[(32, H)],
        after=(weights,),
    )
    queries = from_neighbours(queries)
    (marker,) = call(marker_body, [(8, LANES)], 12, after=(near, far))
    (send3,) = call(
        moment_body, [(NZ * NY, NX * 24, LANES)], 2, x, recv2, lazy=[(q, (2 * TOK, 32)) for q in queries],
        smem=(0,), fan=(0,), after=(marker,), room=ROOM,
    )
    recv3 = exchange(send3, ("z", "yh")).reshape(BLOCKS * 24, LANES)
    first = back_to_neighbours(
        call(
            first_read_body, [(TOK, D)] * NX, 4, lazy=[*((q, (0, TOK)) for q in queries), (weights, None)],
            after=(send3,),
        )
    )
    (send_second,) = call(
        second_read_body, [(NX, TOK + 8, D)], 5, x, recv3,
        lazy=[*((q, (TOK, TOK)) for q in queries), (weights, None), (send3, (0, 1))], scratch=[(3 * D, LANES)],
        smem=(0,), after=first[1:], room=ROOM,
    )
    second = exchange(send_second, "x")
    (attended,) = call(
        attention_body, [(GROUPS, TOK, D)], 8, position, lazy=whole(qkv, near, far), smem=(0,), after=(send_second,)
    )
    readout, send5 = call(
        squares_body, [(GROUPS, TOK, D), (NARROW, 8, GROUPS * TOK)], 1, second, lazy=whole(*first), fan=(1,),
        after=(attended,), room=SMALL,
    )
    recv5 = exchange(send5, "narrow")
    new_weights, new_moment = call(
        own_rows_body, [(3 * ROWS, 1, H), (3 * ROWS, 1, H)], 1, second, own_weights, scratch=[(32, H)],
        after=(send5,), room=SMALL,
    )
    (mixed,) = call(
        mix_body, [(GROUPS, TOK, D)], 1, recv5, ttt_gain.reshape(1, D), readout, attended, after=(new_weights,),
        room=SMALL,
    )
    return mixed, new_weights.reshape(1, ROWS, 3, H), new_moment.reshape(1, ROWS, 3, H)


def solution(mesh):
    fine = Mesh(mesh.devices.reshape(NZ, NX, NY, NARROW), ("z", "x", "yh", "narrow"))
    wide = ("z", "x", "yh")
    return jax.shard_map(
        local,
        mesh=fine,
        in_specs=(
            P(None, None, wide, "narrow"),
            P("narrow", wide),
            P("narrow", wide, None, None),
            P("narrow", wide, None, None),
            P("narrow"),
        ),
        out_specs=(
            P(None, wide, "narrow"),
            P("narrow", wide, None, None),
            P("narrow", wide, None, None),
        ),
        check_vma=False,
    )
```

```python
import functools
import math

import jax
import jax.numpy as jnp
from jax import lax
from jax.experimental import pallas as pl
from jax.experimental.pallas import tpu as pltpu
from jax.sharding import Mesh
from jax.sharding import PartitionSpec as P

ATT = 128
WINDOW = 128
EPSILON = 1e-06
MOMENTUM_RATE = 0.9
STEP_SIZE = 0.03
PRECISION = lax.Precision.HIGHEST

NZ, NX, NY = 8, 4, 2
BLOCKS = NZ * NX * NY
ROWS = 10
SLICE = 96
LANES = 128
TOK = 64
D = 640
H = 384
NARROW = 8
GROUPS = 2
VMEM_LIMIT = 58 * 1024 * 1024
ROOM = 8 * 1024 * 1024
SMALL = 42 * 1024 * 1024


def dot(left, right, dims=((1,), (0,))):
    return lax.dot_general(
        left, right, (dims, ((), ())), precision=PRECISION, preferred_element_type=jnp.float32
    )


def entry(group, sublane):
    q = group * 8 + sublane
    return (q // 3, q % 3) if q < 3 * ROWS else None


def call(body, outs, micros, *args, lazy=(), after=(), scratch=(), smem=(), fan=(), room=0):
    vmem, anywhere = pl.BlockSpec(memory_space=pltpu.VMEM), pl.BlockSpec(memory_space=pl.ANY)
    held = [outs[n][1:] if n in fan else outs[n] for n in range(len(outs))]
    lazy_shapes = [a.shape if at is None else (at[1], *a.shape[1:]) for a, at in lazy]
    sizes = (len(args), len(lazy), len(after), len(outs), len(outs), len(lazy), len(scratch))
    fetches = max(len(lazy), 1)
    sends = sum(outs[n][0] if n in fan else 1 for n in range(len(outs)))

    def kernel(*refs):
        split, at = [], 0
        for size in sizes:
            split.append(refs[at : at + size])
            at += size
        inputs, sources, _, targets, results, fetched, spare = split
        in_sems, out_sems = refs[at:]
        incoming = [
            pltpu.make_async_copy(ref if lazy[n][1] is None else ref.at[pl.ds(*lazy[n][1])], fetched[n], in_sems.at[n])
            for n, ref in enumerate(sources)
        ]
        for copy in incoming:
            copy.start()
        outgoing, base = [], 0
        for n in range(len(outs)):
            places = [targets[n].at[j] for j in range(outs[n][0])] if n in fan else [targets[n]]
            outgoing.append(
                [pltpu.make_async_copy(results[n], place, out_sems.at[base + j]) for j, place in enumerate(places)]
            )
            base += len(places)
        sent = set()

        def need():
            for copy in incoming:
                copy.wait()

        def send(n):
            sent.add(n)
            for copy in outgoing[n]:
                copy.start()

        body(inputs, fetched, results, spare, need, send)
        for n in range(len(outs)):
            if n not in sent:
                send(n)
        for copies in outgoing:
            for copy in copies:
                copy.wait()

    return pl.pallas_call(
        kernel,
        out_shape=[jax.ShapeDtypeStruct(s, jnp.float32) for s in outs],
        in_specs=[pl.BlockSpec(memory_space=pltpu.SMEM) if n in smem else vmem for n in range(len(args))]
        + [anywhere] * (len(lazy) + len(after)),
        out_specs=[anywhere] * len(outs),
        scratch_shapes=[
            *(pltpu.VMEM(tuple(s), jnp.float32) for s in (*held, *lazy_shapes, *scratch)),
            pltpu.SemaphoreType.DMA((fetches,)),
            pltpu.SemaphoreType.DMA((sends,)),
        ],
        compiler_params=pltpu.CompilerParams(vmem_limit_bytes=VMEM_LIMIT - room),
        cost_estimate=pl.CostEstimate(flops=int(micros * 1e9), bytes_accessed=10**6, transcendentals=0),
    )(*args, *(a for a, _ in lazy), *after)


def to_column(row):
    n = row.shape[1]
    same = lax.broadcasted_iota(jnp.int32, (n, n), 0) == lax.broadcasted_iota(jnp.int32, (n, n), 1)
    return jnp.sum(jnp.where(same, row, 0.0), axis=1, keepdims=True)


def to_row(column):
    n = column.shape[0]
    same = lax.broadcasted_iota(jnp.int32, (n, n), 0) == lax.broadcasted_iota(jnp.int32, (n, n), 1)
    return jnp.sum(jnp.where(same, column, 0.0), axis=0, keepdims=True)


def own_packs(own_ref, flat_ref):
    flat_ref[24:32, :] = jnp.zeros((8, H), jnp.float32)
    for q in range(3 * ROWS):
        flat_ref[q : q + 1, :] = own_ref[q]
    return [
        jnp.concatenate(
            [flat_ref[8 * g : 8 * g + 8, SLICE * x : SLICE * (x + 1)] for g in range(4)], axis=1
        )
        for x in range(NX)
    ]


def prepare_weights_body(args, lazy, results, scratch, need, send):
    packs = own_packs(args[0], scratch[0])
    for z in range(NZ):
        for x in range(NX):
            for y in range(NY):
                for t in range(3):
                    results[0][(z * NX + x) * NY + y, 8 * t : 8 * t + 8, :] = packs[x][:, LANES * t : LANES * (t + 1)]


def prepare_pairs_body(args, lazy, results, scratch, need, send):
    (eta_ref, qkv_ref, mom_ref), (pairs_ref,) = args, results
    pairs_ref[0:TOK, :] = qkv_ref[1, 0]
    pairs_ref[TOK : 2 * TOK, :] = to_column(eta_ref[...]) * qkv_ref[2, 0]
    packs = own_packs(mom_ref, scratch[0])
    for x in range(NX):
        pairs_ref[2 * TOK + 8 * x : 2 * TOK + 8 * x + 8, 0:H] = packs[x]
        pairs_ref[2 * TOK + 8 * x : 2 * TOK + 8 * x + 8, H:D] = jnp.zeros((8, D - H), jnp.float32)


def prepare_queries_body(args, lazy, results, scratch, need, send):
    need()
    (queries_ref,) = results
    queries_ref[0:TOK, :] = lazy[0][0, 0]
    queries_ref[TOK : 2 * TOK, :] = lazy[0][0, 1]


def marker_body(args, lazy, results, scratch, need, send):
    results[0][...] = jnp.zeros((8, LANES), jnp.float32)


def widened(part):
    return jnp.concatenate([part, jnp.zeros((part.shape[0], LANES - SLICE), jnp.float32)], axis=1)


def unpack(recv_ref, out_ref, x_stride, y_stride, z_stride):
    for s in range(8):
        for x in range(NX):
            for y in range(NY):
                start = x * x_stride + y * y_stride + s
                rows = jnp.concatenate(
                    [recv_ref[pl.ds(start + 8 * t, NZ, stride=z_stride), :] for t in range(3)], axis=1
                )
                for g in range(4):
                    at = entry(g, s)
                    if at is None:
                        continue
                    r, i = at
                    out_ref[pl.ds(i * D + (x * NY + y) * ROWS + r, NZ, stride=NX * NY * ROWS), :] = widened(
                        rows[:, SLICE * g : SLICE * (g + 1)]
                    )


def pack(in_ref, send_ref, x_stride, y_stride, z_stride):
    for s in range(8):
        for x in range(NX):
            for y in range(NY):
                parts = []
                for g in range(4):
                    at = entry(g, s)
                    if at is None:
                        parts.append(jnp.zeros((NZ, SLICE), jnp.float32))
                        continue
                    r, i = at
                    parts.append(in_ref[pl.ds(i * D + (x * NY + y) * ROWS + r, NZ, stride=NX * NY * ROWS), :][:, :SLICE])
                rows = jnp.concatenate(parts, axis=1)
                start = x * x_stride + y * y_stride + s
                for t in range(3):
                    send_ref[pl.ds(start + 8 * t, NZ, stride=z_stride), :] = rows[:, LANES * t : LANES * (t + 1)]


def token_rows(refs, start):
    return jnp.concatenate([ref[start : start + TOK, :] for ref in refs], axis=0)


def matrix(ref, i):
    return ref[i * D : (i + 1) * D, :]


def gradient_body(args, pairs, results, scratch, need, send):
    (recv_ref,), (w_ref, send_ref), (g_ref,) = args, results, scratch
    unpack(recv_ref, w_ref, 48, 24, 192)
    send(0)
    need()
    keys = token_rows(pairs, 0)
    weighted = token_rows(pairs, TOK)
    pre = dot(keys, jnp.concatenate([matrix(w_ref, 0), matrix(w_ref, 1)], axis=1))
    gate_pre, up_pre = pre[:, :LANES], pre[:, LANES:]
    back = -dot(weighted, matrix(w_ref, 2))
    sigmoid = jax.nn.sigmoid(gate_pre)
    gated = gate_pre * sigmoid
    hidden = gated * up_pre
    gate_back = back * up_pre * sigmoid * (1.0 + gate_pre * (1.0 - sigmoid))
    up_back = back * gated
    both = dot(keys, jnp.concatenate([gate_back, up_back], axis=1), ((0,), (0,)))
    g_ref[0:D, :] = both[:, :LANES]
    g_ref[D : 2 * D, :] = both[:, LANES:]
    g_ref[2 * D : 3 * D, :] = -dot(weighted, hidden, ((0,), (0,)))
    pack(g_ref, send_ref, 24, 96, 192)


def source(x_ref, s):
    return lax.rem(x_ref[0] + NX - s, NX)


def moment_body(args, tails, results, scratch, need, send):
    (x_ref, recv_ref), (own_ref,) = args, results
    total = recv_ref[0]
    for j in range(1, NZ * NY):
        total = total + recv_ref[j]
    own_ref[...] = total
    need()
    mine = pl.ds(pl.multiple_of(8 * x_ref[0], 8), 8)
    for s, ref in enumerate(tails):
        old = ref[mine, :]
        old = jnp.concatenate([old[:, LANES * t : LANES * (t + 1)] for t in range(3)], axis=0)
        rows = pl.ds(pl.multiple_of(24 * source(x_ref, s), 8), 24)
        own_ref[rows, :] = own_ref[rows, :] + MOMENTUM_RATE * old


def hidden_of(inputs, w1, w3):
    pre = dot(inputs, jnp.concatenate([w1, w3], axis=1))
    gate_pre, up_pre = pre[:, :LANES], pre[:, LANES:]
    return gate_pre * jax.nn.sigmoid(gate_pre) * up_pre


def first_read_body(args, lazy, results, scratch, need, send):
    need()
    *queries, w_ref = lazy
    hidden = hidden_of(token_rows(queries, 0), matrix(w_ref, 0), matrix(w_ref, 1))
    partial = dot(hidden, matrix(w_ref, 2), ((1,), (1,)))
    for s in range(NX):
        results[s][...] = partial[s * TOK : (s + 1) * TOK]


def renormalized(weights, moment):
    rate = STEP_SIZE / jnp.sqrt(jnp.mean(moment * moment, axis=0, keepdims=True) + EPSILON)
    moved = weights - moment * rate
    ratio = jnp.sqrt(jnp.mean(weights * weights, axis=0, keepdims=True) + EPSILON) / jnp.sqrt(
        jnp.mean(moved * moved, axis=0, keepdims=True) + EPSILON
    )
    return moved * ratio, rate, ratio


def second_read_body(args, lazy, results, scratch, need, send):
    (x_ref, recv_ref), (*queries, w_ref, moment_ref), (send_ref,), (m_ref,) = args, lazy, results, scratch
    unpack(recv_ref, m_ref, 24, 96, 192)
    need()
    new1, rate1, ratio1 = renormalized(matrix(w_ref, 0), matrix(m_ref, 0))
    new3, rate3, ratio3 = renormalized(matrix(w_ref, 1), matrix(m_ref, 1))
    new2, rate2, ratio2 = renormalized(matrix(w_ref, 2), matrix(m_ref, 2))
    hidden = hidden_of(token_rows(queries, 0), new1, new3)
    partial = dot(hidden, new2, ((1,), (1,)))
    stats = [rate1, rate3, rate2, ratio1, ratio3, ratio2, jnp.zeros((2, LANES), jnp.float32)]
    stats = jnp.concatenate(stats, axis=0)
    for x in range(NX):
        tail = [stats, *(moment_ref[0, 24 * x + 8 * t : 24 * x + 8 * t + 8, :] for t in range(3))]
        tail.append(jnp.zeros((8, LANES), jnp.float32))
        send_ref[x, TOK : TOK + 8, :] = jnp.concatenate(tail, axis=1)
    for s in range(NX):
        send_ref[source(x_ref, s), 0:TOK, :] = partial[s * TOK : (s + 1) * TOK]


def squares_body(args, lazy, results, scratch, need, send):
    (second_ref,), (readout_ref, send_ref) = args, results
    need()
    first = lazy[0][...] + lazy[1][...] + lazy[2][...] + lazy[3][...]
    second = second_ref[0, 0:TOK, :]
    for x in range(1, NX):
        second = second + second_ref[x, 0:TOK, :]
    readout_ref[0] = first
    readout_ref[1] = second
    row = jnp.concatenate(
        [to_row(jnp.sum(total * total, axis=1, keepdims=True)) for total in (first, second)], axis=1
    )
    send_ref[...] = jnp.broadcast_to(row, (8, GROUPS * TOK))


def own_rows_body(args, lazy, results, scratch, need, send):
    (second_ref, fw_ref), (new_w_ref, new_m_ref), (flat_ref,) = args, results, scratch
    for g in range(4):
        flat_ref[8 * g : 8 * g + 8, :] = jnp.concatenate(
            [
                second_ref[x, TOK : TOK + 8, LANES + SLICE * g : LANES + SLICE * (g + 1)]
                for x in range(NX)
            ],
            axis=1,
        )
    stats = jnp.concatenate([second_ref[x, TOK : TOK + 8, 0:SLICE] for x in range(NX)], axis=1)
    for q in range(3 * ROWS):
        i = q % 3
        moment = flat_ref[q : q + 1, :]
        new_m_ref[q] = moment
        new_w_ref[q] = (fw_ref[q] - moment * stats[i : i + 1]) * stats[3 + i : 4 + i]


def mix_body(args, lazy, results, scratch, need, send):
    (recv_ref, gain_ref, readout_ref, attended_ref), (mixed_ref,) = args, results
    total = recv_ref[0, 0:1, :]
    for n in range(1, NARROW):
        total = total + recv_ref[n, 0:1, :]
    scale = to_column(1.0 / jnp.sqrt(total / (D * NARROW) + EPSILON))
    for c in range(GROUPS):
        mixed_ref[c] = attended_ref[c] + gain_ref[...] * (readout_ref[c] * scale[c * TOK : (c + 1) * TOK])


def attention_body(args, lazy, results, scratch, need, send):
    (position_ref,), (qkv_ref, near_ref, far_ref), (out_ref,) = args, lazy, results
    position = position_ref[0]
    row = lax.broadcasted_iota(jnp.int32, (TOK, 3 * TOK), 0) + 2 * TOK
    col = lax.broadcasted_iota(jnp.int32, (TOK, 3 * TOK), 1)
    window = (row - col >= 0) & (row - col < WINDOW)
    first = jnp.where(position >= 2, 0, jnp.where(position >= 1, TOK, 2 * TOK))
    need()
    for c in range(GROUPS):
        allowed = window & (col >= first) if c == 0 else window
        for h in range(D // ATT):
            at = slice(h * ATT, (h + 1) * ATT)
            parts = []
            for a in range(2):
                far, near = far_ref[a, c, :, at], near_ref[a, c, :, at]
                if c == 1:
                    far = jnp.where(position >= 2, far, far_ref[a, 0, :, at])
                    near = jnp.where(position >= 1, near, near_ref[a, 0, :, at])
                parts.append(jnp.concatenate([far, near, qkv_ref[1 + a, c, :, at]], axis=0))
            keys, values = parts
            scores = dot(qkv_ref[0, c, :, at], keys, ((1,), (1,))) * (1.0 / math.sqrt(ATT))
            scores = jnp.where(allowed, scores, -1e30)
            weights = jnp.exp(scores - jnp.max(scores, axis=1, keepdims=True))
            weights = weights / jnp.sum(weights, axis=1, keepdims=True)
            out_ref[c, :, at] = dot(weights, values)


def behind(block, distance):
    axes = ("z", "x", "yh")
    return lax.ppermute(block, axes, [((i - distance) % BLOCKS, i) for i in range(BLOCKS)])


def relayed_from_neighbours(block):
    behind_one = lax.ppermute(block, "x", [((i - 1) % NX, i) for i in range(NX)])
    from_ahead = [((i + 1) % NX, i) for i in range(NX)]
    ahead_one = lax.ppermute(block, "x", from_ahead)
    return [block, behind_one, lax.ppermute(ahead_one, "x", from_ahead), ahead_one]


def back_to_neighbours(blocks):
    return [blocks[0]] + [
        lax.ppermute(blocks[s], "x", [(i, (i - s) % NX) for i in range(NX)]) for s in range(1, NX)
    ]


def exchange(pieces, axes):
    return lax.all_to_all(pieces, axes, split_axis=0, concat_axis=0, tiled=True)


def scalar(value):
    return jnp.reshape(value, (1,)).astype(jnp.int32)


def whole(*arrays):
    return [(a, None) for a in arrays]


def local(qkv, eta, fast_weights, momentum, ttt_gain):
    own_weights, own_moment = fast_weights.reshape(3 * ROWS, 1, H), momentum.reshape(3 * ROWS, 1, H)
    x = lax.axis_index("x")
    position = scalar((lax.axis_index("z") * NX + x) * NY + lax.axis_index("yh"))
    x = scalar(x)
    (send1,) = call(prepare_weights_body, [(BLOCKS, 24, LANES)], 1, own_weights, scratch=[(32, H)], room=SMALL)
    (pairs,) = call(
        prepare_pairs_body, [(2 * TOK + 32, D)], 1, eta, qkv, own_moment, scratch=[(32, H)], room=SMALL
    )
    recv1 = exchange(send1, ("z", "x", "yh")).reshape(BLOCKS * 24, LANES)
    pairs = relayed_from_neighbours(pairs)
    near, far = behind(qkv[1:], 1), behind(qkv[1:], 2)
    weights, send2 = call(
        gradient_body, [(3 * D, LANES), (BLOCKS * 24, LANES)], 5, recv1, lazy=[(p, (0, 2 * TOK)) for p in pairs],
        scratch=[(3 * D, LANES)], room=ROOM - 512 * 1024,
    )
    recv2 = exchange(send2.reshape(NZ * NY, NX * 24, LANES), ("z", "yh"))
    (queries,) = call(prepare_queries_body, [(2 * TOK, D)], 0.1, lazy=[(qkv, (0, 1))], after=(weights,))
    queries = relayed_from_neighbours(queries)
    (marker,) = call(marker_body, [(8, LANES)], 12, after=(near, far))
    (send3,) = call(
        moment_body, [(NZ * NY, NX * 24, LANES)], 2, x, recv2, lazy=[(p, (2 * TOK, 32)) for p in pairs],
        smem=(0,), fan=(0,), after=(marker, *queries[1:]), room=ROOM,
    )
    recv3 = exchange(send3, ("z", "yh")).reshape(BLOCKS * 24, LANES)
    first = back_to_neighbours(
        call(
            first_read_body, [(TOK, D)] * NX, 4, lazy=[*((q, (0, TOK)) for q in queries), (weights, None)],
            after=(send3,),
        )
    )
    (send_second,) = call(
        second_read_body, [(NX, TOK + 8, D)], 5, x, recv3,
        lazy=[*((q, (TOK, TOK)) for q in queries), (weights, None), (send3, (0, 1))], scratch=[(3 * D, LANES)],
        smem=(0,), after=first[1:], room=ROOM,
    )
    second = exchange(send_second, "x")
    (attended,) = call(
        attention_body, [(GROUPS, TOK, D)], 8, position, lazy=whole(qkv, near, far), smem=(0,), after=(send_second,)
    )
    readout, send5 = call(
        squares_body, [(GROUPS, TOK, D), (NARROW, 8, GROUPS * TOK)], 1, second, lazy=whole(*first), fan=(1,),
        after=(attended,), room=SMALL,
    )
    recv5 = exchange(send5, "narrow")
    new_weights, new_moment = call(
        own_rows_body, [(3 * ROWS, 1, H), (3 * ROWS, 1, H)], 1, second, own_weights, scratch=[(32, H)],
        after=(send5,), room=SMALL,
    )
    (mixed,) = call(
        mix_body, [(GROUPS, TOK, D)], 1, recv5, ttt_gain.reshape(1, D), readout, attended, after=(new_weights,),
        room=SMALL,
    )
    return mixed, new_weights.reshape(1, ROWS, 3, H), new_moment.reshape(1, ROWS, 3, H)


def solution(mesh):
    fine = Mesh(mesh.devices.reshape(NZ, NX, NY, NARROW), ("z", "x", "yh", "narrow"))
    wide = ("z", "x", "yh")
    return jax.shard_map(
        local,
        mesh=fine,
        in_specs=(
            P(None, None, wide, "narrow"),
            P("narrow", wide),
            P("narrow", wide, None, None),
            P("narrow", wide, None, None),
            P("narrow"),
        ),
        out_specs=(
            P(None, wide, "narrow"),
            P("narrow", wide, None, None),
            P("narrow", wide, None, None),
        ),
        check_vma=False,
    )
```

```python
import functools
import math

import jax
import jax.numpy as jnp
from jax import lax
from jax.experimental import pallas as pl
from jax.experimental.pallas import tpu as pltpu
from jax.sharding import Mesh
from jax.sharding import PartitionSpec as P

ATT = 128
WINDOW = 128
EPSILON = 1e-06
MOMENTUM_RATE = 0.9
STEP_SIZE = 0.03
PRECISION = lax.Precision.HIGHEST

NZ, NX, NY = 8, 4, 2
BLOCKS = NZ * NX * NY
ROWS = 10
SLICE = 96
LANES = 128
TOK = 64
D = 640
H = 384
NARROW = 8
GROUPS = 2
VMEM_LIMIT = 58 * 1024 * 1024
ROOM = 8 * 1024 * 1024
SMALL = 42 * 1024 * 1024


def dot(left, right, dims=((1,), (0,))):
    return lax.dot_general(
        left, right, (dims, ((), ())), precision=PRECISION, preferred_element_type=jnp.float32
    )


def halves(x):
    high = x.astype(jnp.bfloat16)
    return high, (x - high.astype(jnp.float32)).astype(jnp.bfloat16)


def split_dot(left, right, dims=((1,), (0,))):
    def one(a, b):
        return lax.dot_general(a, b, (dims, ((), ())), preferred_element_type=jnp.float32)

    left_high, left_low = halves(left)
    right_high, right_low = halves(right)
    return one(left_high, right_high) + (one(left_high, right_low) + one(left_low, right_high))


def entry(group, sublane):
    q = group * 8 + sublane
    return (q // 3, q % 3) if q < 3 * ROWS else None


def call(body, outs, micros, *args, lazy=(), after=(), scratch=(), smem=(), fan=(), room=0):
    vmem, anywhere = pl.BlockSpec(memory_space=pltpu.VMEM), pl.BlockSpec(memory_space=pl.ANY)
    held = [outs[n][1:] if n in fan else outs[n] for n in range(len(outs))]
    lazy_shapes = [a.shape if at is None else (at[1], *a.shape[1:]) for a, at in lazy]
    sizes = (len(args), len(lazy), len(after), len(outs), len(outs), len(lazy), len(scratch))
    fetches = max(len(lazy), 1)
    sends = sum(outs[n][0] if n in fan else 1 for n in range(len(outs)))

    def kernel(*refs):
        split, at = [], 0
        for size in sizes:
            split.append(refs[at : at + size])
            at += size
        inputs, sources, _, targets, results, fetched, spare = split
        in_sems, out_sems = refs[at:]
        incoming = [
            pltpu.make_async_copy(ref if lazy[n][1] is None else ref.at[pl.ds(*lazy[n][1])], fetched[n], in_sems.at[n])
            for n, ref in enumerate(sources)
        ]
        for copy in incoming:
            copy.start()
        outgoing, base = [], 0
        for n in range(len(outs)):
            places = [targets[n].at[j] for j in range(outs[n][0])] if n in fan else [targets[n]]
            outgoing.append(
                [pltpu.make_async_copy(results[n], place, out_sems.at[base + j]) for j, place in enumerate(places)]
            )
            base += len(places)
        sent = set()

        def need():
            for copy in incoming:
                copy.wait()

        def send(n):
            sent.add(n)
            for copy in outgoing[n]:
                copy.start()

        body(inputs, fetched, results, spare, need, send)
        for n in range(len(outs)):
            if n not in sent:
                send(n)
        for copies in outgoing:
            for copy in copies:
                copy.wait()

    return pl.pallas_call(
        kernel,
        out_shape=[jax.ShapeDtypeStruct(s, jnp.float32) for s in outs],
        in_specs=[pl.BlockSpec(memory_space=pltpu.SMEM) if n in smem else vmem for n in range(len(args))]
        + [anywhere] * (len(lazy) + len(after)),
        out_specs=[anywhere] * len(outs),
        scratch_shapes=[
            *(pltpu.VMEM(tuple(s), jnp.float32) for s in (*held, *lazy_shapes, *scratch)),
            pltpu.SemaphoreType.DMA((fetches,)),
            pltpu.SemaphoreType.DMA((sends,)),
        ],
        compiler_params=pltpu.CompilerParams(vmem_limit_bytes=VMEM_LIMIT - room),
        cost_estimate=pl.CostEstimate(flops=int(micros * 1e9), bytes_accessed=10**6, transcendentals=0),
    )(*args, *(a for a, _ in lazy), *after)


def to_column(row):
    n = row.shape[1]
    same = lax.broadcasted_iota(jnp.int32, (n, n), 0) == lax.broadcasted_iota(jnp.int32, (n, n), 1)
    return jnp.sum(jnp.where(same, row, 0.0), axis=1, keepdims=True)


def to_row(column):
    n = column.shape[0]
    same = lax.broadcasted_iota(jnp.int32, (n, n), 0) == lax.broadcasted_iota(jnp.int32, (n, n), 1)
    return jnp.sum(jnp.where(same, column, 0.0), axis=0, keepdims=True)


def own_packs(own_ref, flat_ref):
    flat_ref[24:32, :] = jnp.zeros((8, H), jnp.float32)
    for q in range(3 * ROWS):
        flat_ref[q : q + 1, :] = own_ref[q]
    return [
        jnp.concatenate(
            [flat_ref[8 * g : 8 * g + 8, SLICE * x : SLICE * (x + 1)] for g in range(4)], axis=1
        )
        for x in range(NX)
    ]


def prepare_weights_body(args, lazy, results, scratch, need, send):
    packs = own_packs(args[0], scratch[0])
    for z in range(NZ):
        for x in range(NX):
            for y in range(NY):
                for t in range(3):
                    results[0][(z * NX + x) * NY + y, 8 * t : 8 * t + 8, :] = packs[x][:, LANES * t : LANES * (t + 1)]


def prepare_pairs_body(args, lazy, results, scratch, need, send):
    eta_ref, qkv_ref = args
    results[0][0:TOK, :] = qkv_ref[1, 0]
    results[0][TOK : 2 * TOK, :] = to_column(eta_ref[...]) * qkv_ref[2, 0]


def prepare_queries_body(args, lazy, results, scratch, need, send):
    (mom_ref,), (qkv_ref,), (queries_ref,) = args, lazy, results
    packs = own_packs(mom_ref, scratch[0])
    for x in range(NX):
        queries_ref[2 * TOK + 8 * x : 2 * TOK + 8 * x + 8, 0:H] = packs[x]
        queries_ref[2 * TOK + 8 * x : 2 * TOK + 8 * x + 8, H:D] = jnp.zeros((8, D - H), jnp.float32)
    need()
    queries_ref[0:TOK, :] = qkv_ref[0, 0]
    queries_ref[TOK : 2 * TOK, :] = qkv_ref[0, 1]


def marker_body(args, lazy, results, scratch, need, send):
    results[0][...] = jnp.zeros((8, LANES), jnp.float32)


def widened(part):
    return jnp.concatenate([part, jnp.zeros((part.shape[0], LANES - SLICE), jnp.float32)], axis=1)


def unpack(recv_ref, out_ref, x_stride, y_stride, z_stride):
    for s in range(8):
        for x in range(NX):
            for y in range(NY):
                start = x * x_stride + y * y_stride + s
                rows = jnp.concatenate(
                    [recv_ref[pl.ds(start + 8 * t, NZ, stride=z_stride), :] for t in range(3)], axis=1
                )
                for g in range(4):
                    at = entry(g, s)
                    if at is None:
                        continue
                    r, i = at
                    out_ref[pl.ds(i * D + (x * NY + y) * ROWS + r, NZ, stride=NX * NY * ROWS), :] = widened(
                        rows[:, SLICE * g : SLICE * (g + 1)]
                    )


def pack(in_ref, send_ref, x_stride, y_stride, z_stride):
    for s in range(8):
        for x in range(NX):
            for y in range(NY):
                parts = []
                for g in range(4):
                    at = entry(g, s)
                    if at is None:
                        parts.append(jnp.zeros((NZ, SLICE), jnp.float32))
                        continue
                    r, i = at
                    parts.append(in_ref[pl.ds(i * D + (x * NY + y) * ROWS + r, NZ, stride=NX * NY * ROWS), :][:, :SLICE])
                rows = jnp.concatenate(parts, axis=1)
                start = x * x_stride + y * y_stride + s
                for t in range(3):
                    send_ref[pl.ds(start + 8 * t, NZ, stride=z_stride), :] = rows[:, LANES * t : LANES * (t + 1)]


def token_rows(refs, start):
    return jnp.concatenate([ref[start : start + TOK, :] for ref in refs], axis=0)


def matrix(ref, i):
    return ref[i * D : (i + 1) * D, :]


def gradient_body(args, pairs, results, scratch, need, send):
    (recv_ref,), (w_ref, send_ref), (g_ref,) = args, results, scratch
    unpack(recv_ref, w_ref, 48, 24, 192)
    send(0)
    need()
    keys = token_rows(pairs, 0)
    weighted = token_rows(pairs, TOK)
    pre = split_dot(keys, jnp.concatenate([matrix(w_ref, 0), matrix(w_ref, 1)], axis=1))
    gate_pre, up_pre = pre[:, :LANES], pre[:, LANES:]
    back = -split_dot(weighted, matrix(w_ref, 2))
    sigmoid = jax.nn.sigmoid(gate_pre)
    gated = gate_pre * sigmoid
    hidden = gated * up_pre
    gate_back = back * up_pre * sigmoid * (1.0 + gate_pre * (1.0 - sigmoid))
    up_back = back * gated
    both = split_dot(keys, jnp.concatenate([gate_back, up_back], axis=1), ((0,), (0,)))
    g_ref[0:D, :] = both[:, :LANES]
    g_ref[D : 2 * D, :] = both[:, LANES:]
    g_ref[2 * D : 3 * D, :] = -split_dot(weighted, hidden, ((0,), (0,)))
    pack(g_ref, send_ref, 24, 96, 192)


def source(x_ref, s):
    return lax.rem(x_ref[0] + NX - s, NX)


def moment_body(args, tails, results, scratch, need, send):
    (x_ref, recv_ref), (own_ref,) = args, results
    total = recv_ref[0]
    for j in range(1, NZ * NY):
        total = total + recv_ref[j]
    own_ref[...] = total
    need()
    mine = pl.ds(pl.multiple_of(8 * x_ref[0], 8), 8)
    for s, ref in enumerate(tails):
        old = ref[mine, :]
        old = jnp.concatenate([old[:, LANES * t : LANES * (t + 1)] for t in range(3)], axis=0)
        rows = pl.ds(pl.multiple_of(24 * source(x_ref, s), 8), 24)
        own_ref[rows, :] = own_ref[rows, :] + MOMENTUM_RATE * old


def hidden_of(inputs, w1, w3):
    pre = split_dot(inputs, jnp.concatenate([w1, w3], axis=1))
    gate_pre, up_pre = pre[:, :LANES], pre[:, LANES:]
    return gate_pre * jax.nn.sigmoid(gate_pre) * up_pre


def first_read_body(args, lazy, results, scratch, need, send):
    need()
    *queries, w_ref = lazy
    hidden = hidden_of(token_rows(queries, 0), matrix(w_ref, 0), matrix(w_ref, 1))
    partial = split_dot(hidden, matrix(w_ref, 2), ((1,), (1,)))
    for s in range(NX):
        results[s][...] = partial[s * TOK : (s + 1) * TOK]


def renormalized(weights, moment):
    rate = STEP_SIZE / jnp.sqrt(jnp.mean(moment * moment, axis=0, keepdims=True) + EPSILON)
    moved = weights - moment * rate
    ratio = jnp.sqrt(jnp.mean(weights * weights, axis=0, keepdims=True) + EPSILON) / jnp.sqrt(
        jnp.mean(moved * moved, axis=0, keepdims=True) + EPSILON
    )
    return moved * ratio, rate, ratio


def second_read_body(args, lazy, results, scratch, need, send):
    (x_ref, recv_ref), (*queries, w_ref, moment_ref), (send_ref,), (m_ref,) = args, lazy, results, scratch
    unpack(recv_ref, m_ref, 24, 96, 192)
    need()
    new1, rate1, ratio1 = renormalized(matrix(w_ref, 0), matrix(m_ref, 0))
    new3, rate3, ratio3 = renormalized(matrix(w_ref, 1), matrix(m_ref, 1))
    new2, rate2, ratio2 = renormalized(matrix(w_ref, 2), matrix(m_ref, 2))
    hidden = hidden_of(token_rows(queries, 0), new1, new3)
    partial = split_dot(hidden, new2, ((1,), (1,)))
    stats = [rate1, rate3, rate2, ratio1, ratio3, ratio2, jnp.zeros((2, LANES), jnp.float32)]
    stats = jnp.concatenate(stats, axis=0)
    for x in range(NX):
        tail = [stats, *(moment_ref[0, 24 * x + 8 * t : 24 * x + 8 * t + 8, :] for t in range(3))]
        tail.append(jnp.zeros((8, LANES), jnp.float32))
        send_ref[x, TOK : TOK + 8, :] = jnp.concatenate(tail, axis=1)
    for s in range(NX):
        send_ref[source(x_ref, s), 0:TOK, :] = partial[s * TOK : (s + 1) * TOK]


def squares_body(args, lazy, results, scratch, need, send):
    (second_ref,), (readout_ref, send_ref) = args, results
    need()
    first = lazy[0][...] + lazy[1][...] + lazy[2][...] + lazy[3][...]
    second = second_ref[0, 0:TOK, :]
    for x in range(1, NX):
        second = second + second_ref[x, 0:TOK, :]
    readout_ref[0] = first
    readout_ref[1] = second
    row = jnp.concatenate(
        [to_row(jnp.sum(total * total, axis=1, keepdims=True)) for total in (first, second)], axis=1
    )
    send_ref[...] = jnp.broadcast_to(row, (8, GROUPS * TOK))


def own_rows_body(args, lazy, results, scratch, need, send):
    (second_ref, fw_ref), (new_w_ref, new_m_ref), (flat_ref,) = args, results, scratch
    for g in range(4):
        flat_ref[8 * g : 8 * g + 8, :] = jnp.concatenate(
            [
                second_ref[x, TOK : TOK + 8, LANES + SLICE * g : LANES + SLICE * (g + 1)]
                for x in range(NX)
            ],
            axis=1,
        )
    stats = jnp.concatenate([second_ref[x, TOK : TOK + 8, 0:SLICE] for x in range(NX)], axis=1)
    for q in range(3 * ROWS):
        i = q % 3
        moment = flat_ref[q : q + 1, :]
        new_m_ref[q] = moment
        new_w_ref[q] = (fw_ref[q] - moment * stats[i : i + 1]) * stats[3 + i : 4 + i]


def mix_body(args, lazy, results, scratch, need, send):
    (recv_ref, gain_ref, readout_ref, attended_ref), (mixed_ref,) = args, results
    total = recv_ref[0, 0:1, :]
    for n in range(1, NARROW):
        total = total + recv_ref[n, 0:1, :]
    scale = to_column(1.0 / jnp.sqrt(total / (D * NARROW) + EPSILON))
    for c in range(GROUPS):
        mixed_ref[c] = attended_ref[c] + gain_ref[...] * (readout_ref[c] * scale[c * TOK : (c + 1) * TOK])


def attention_body(args, lazy, results, scratch, need, send):
    (position_ref,), (qkv_ref, near_ref, far_ref), (out_ref,) = args, lazy, results
    position = position_ref[0]
    row = lax.broadcasted_iota(jnp.int32, (TOK, 3 * TOK), 0) + 2 * TOK
    col = lax.broadcasted_iota(jnp.int32, (TOK, 3 * TOK), 1)
    window = (row - col >= 0) & (row - col < WINDOW)
    first = jnp.where(position >= 2, 0, jnp.where(position >= 1, TOK, 2 * TOK))
    need()
    for c in range(GROUPS):
        allowed = window & (col >= first) if c == 0 else window
        for h in range(D // ATT):
            at = slice(h * ATT, (h + 1) * ATT)
            parts = []
            for a in range(2):
                far, near = far_ref[a, c, :, at], near_ref[a, c, :, at]
                if c == 1:
                    far = jnp.where(position >= 2, far, far_ref[a, 0, :, at])
                    near = jnp.where(position >= 1, near, near_ref[a, 0, :, at])
                parts.append(jnp.concatenate([far, near, qkv_ref[1 + a, c, :, at]], axis=0))
            keys, values = parts
            scores = dot(qkv_ref[0, c, :, at], keys, ((1,), (1,))) * (1.0 / math.sqrt(ATT))
            scores = jnp.where(allowed, scores, -1e30)
            weights = jnp.exp(scores - jnp.max(scores, axis=1, keepdims=True))
            weights = weights / jnp.sum(weights, axis=1, keepdims=True)
            out_ref[c, :, at] = dot(weights, values)


def behind(block, distance):
    axes = ("z", "x", "yh")
    return lax.ppermute(block, axes, [((i - distance) % BLOCKS, i) for i in range(BLOCKS)])


def from_neighbours(block):
    return [block] + [lax.ppermute(block, "x", [((i - s) % NX, i) for i in range(NX)]) for s in range(1, NX)]


def relayed_from_neighbours(block):
    behind_one = lax.ppermute(block, "x", [((i - 1) % NX, i) for i in range(NX)])
    from_ahead = [((i + 1) % NX, i) for i in range(NX)]
    ahead_one = lax.ppermute(block, "x", from_ahead)
    return [block, behind_one, lax.ppermute(ahead_one, "x", from_ahead), ahead_one]


def back_to_neighbours(blocks):
    return [blocks[0]] + [
        lax.ppermute(blocks[s], "x", [(i, (i - s) % NX) for i in range(NX)]) for s in range(1, NX)
    ]


def exchange(pieces, axes):
    return lax.all_to_all(pieces, axes, split_axis=0, concat_axis=0, tiled=True)


def scalar(value):
    return jnp.reshape(value, (1,)).astype(jnp.int32)


def whole(*arrays):
    return [(a, None) for a in arrays]


def local(qkv, eta, fast_weights, momentum, ttt_gain):
    own_weights, own_moment = fast_weights.reshape(3 * ROWS, 1, H), momentum.reshape(3 * ROWS, 1, H)
    x = lax.axis_index("x")
    position = scalar((lax.axis_index("z") * NX + x) * NY + lax.axis_index("yh"))
    x = scalar(x)
    (send1,) = call(prepare_weights_body, [(BLOCKS, 24, LANES)], 1, own_weights, scratch=[(32, H)], room=SMALL)
    (pairs,) = call(prepare_pairs_body, [(2 * TOK, D)], 1, eta, qkv, room=SMALL)
    recv1 = exchange(send1, ("z", "x", "yh")).reshape(BLOCKS * 24, LANES)
    pairs = relayed_from_neighbours(pairs)
    near, far = behind(qkv[1:], 1), behind(qkv[1:], 2)
    weights, send2 = call(
        gradient_body, [(3 * D, LANES), (BLOCKS * 24, LANES)], 5, recv1, lazy=whole(*pairs),
        scratch=[(3 * D, LANES)], room=ROOM - 512 * 1024,
    )
    recv2 = exchange(send2.reshape(NZ * NY, NX * 24, LANES), ("z", "yh"))
    (queries,) = call(
        prepare_queries_body, [(2 * TOK + 32, D)], 0.1, own_moment, lazy=[(qkv, (0, 1))], scratch=[(32, H)],
        after=(weights,),
    )
    queries = from_neighbours(queries)
    (marker,) = call(marker_body, [(8, LANES)], 12, after=(near, far))
    (send3,) = call(
        moment_body, [(NZ * NY, NX * 24, LANES)], 2, x, recv2, lazy=[(q, (2 * TOK, 32)) for q in queries],
        smem=(0,), fan=(0,), after=(marker,), room=ROOM,
    )
    recv3 = exchange(send3, ("z", "yh")).reshape(BLOCKS * 24, LANES)
    first = back_to_neighbours(
        call(
            first_read_body, [(TOK, D)] * NX, 4, lazy=[*((q, (0, TOK)) for q in queries), (weights, None)],
            after=(send3,),
        )
    )
    (send_second,) = call(
        second_read_body, [(NX, TOK + 8, D)], 5, x, recv3,
        lazy=[*((q, (TOK, TOK)) for q in queries), (weights, None), (send3, (0, 1))], scratch=[(3 * D, LANES)],
        smem=(0,), after=first[1:], room=ROOM,
    )
    second = exchange(send_second, "x")
    (attended,) = call(
        attention_body, [(GROUPS, TOK, D)], 8, position, lazy=whole(qkv, near, far), smem=(0,), after=(send_second,)
    )
    readout, send5 = call(
        squares_body, [(GROUPS, TOK, D), (NARROW, 8, GROUPS * TOK)], 1, second, lazy=whole(*first), fan=(1,),
        after=(attended,), room=SMALL,
    )
    recv5 = exchange(send5, "narrow")
    new_weights, new_moment = call(
        own_rows_body, [(3 * ROWS, 1, H), (3 * ROWS, 1, H)], 1, second, own_weights, scratch=[(32, H)],
        after=(send5,), room=SMALL,
    )
    (mixed,) = call(
        mix_body, [(GROUPS, TOK, D)], 1, recv5, ttt_gain.reshape(1, D), readout, attended, after=(new_weights,),
        room=SMALL,
    )
    return mixed, new_weights.reshape(1, ROWS, 3, H), new_moment.reshape(1, ROWS, 3, H)


def solution(mesh):
    fine = Mesh(mesh.devices.reshape(NZ, NX, NY, NARROW), ("z", "x", "yh", "narrow"))
    wide = ("z", "x", "yh")
    return jax.shard_map(
        local,
        mesh=fine,
        in_specs=(
            P(None, None, wide, "narrow"),
            P("narrow", wide),
            P("narrow", wide, None, None),
            P("narrow", wide, None, None),
            P("narrow"),
        ),
        out_specs=(
            P(None, wide, "narrow"),
            P("narrow", wide, None, None),
            P("narrow", wide, None, None),
        ),
        check_vma=False,
    )
```

```python
import functools
import math

import jax
import jax.numpy as jnp
from jax import lax
from jax.experimental import pallas as pl
from jax.experimental.pallas import tpu as pltpu
from jax.sharding import Mesh
from jax.sharding import PartitionSpec as P

ATT = 128
WINDOW = 128
EPSILON = 1e-06
MOMENTUM_RATE = 0.9
STEP_SIZE = 0.03
PRECISION = lax.Precision.HIGHEST

NZ, NX, NY = 8, 4, 2
BLOCKS = NZ * NX * NY
ROWS = 10
SLICE = 96
LANES = 128
TOK = 64
D = 640
H = 384
NARROW = 8
GROUPS = 2
VMEM_LIMIT = 58 * 1024 * 1024
ROOM = 8 * 1024 * 1024
SMALL = 42 * 1024 * 1024


def dot(left, right, dims=((1,), (0,))):
    return lax.dot_general(
        left, right, (dims, ((), ())), precision=PRECISION, preferred_element_type=jnp.float32
    )


def halves(x):
    high = x.astype(jnp.bfloat16)
    return high, (x - high.astype(jnp.float32)).astype(jnp.bfloat16)


def split_dot(left, right, dims=((1,), (0,))):
    def one(a, b):
        return lax.dot_general(a, b, (dims, ((), ())), preferred_element_type=jnp.float32)

    left_high, left_low = halves(left)
    right_high, right_low = halves(right)
    return one(left_high, right_high) + (one(left_high, right_low) + one(left_low, right_high))


def entry(group, sublane):
    q = group * 8 + sublane
    return (q // 3, q % 3) if q < 3 * ROWS else None


def call(body, outs, micros, *args, lazy=(), after=(), scratch=(), smem=(), fan=(), room=0):
    vmem, anywhere = pl.BlockSpec(memory_space=pltpu.VMEM), pl.BlockSpec(memory_space=pl.ANY)
    held = [outs[n][1:] if n in fan else outs[n] for n in range(len(outs))]
    lazy_shapes = [a.shape if at is None else (at[1], *a.shape[1:]) for a, at in lazy]
    sizes = (len(args), len(lazy), len(after), len(outs), len(outs), len(lazy), len(scratch))
    fetches = max(len(lazy), 1)
    sends = sum(outs[n][0] if n in fan else 1 for n in range(len(outs)))

    def kernel(*refs):
        split, at = [], 0
        for size in sizes:
            split.append(refs[at : at + size])
            at += size
        inputs, sources, _, targets, results, fetched, spare = split
        in_sems, out_sems = refs[at:]
        incoming = [
            pltpu.make_async_copy(ref if lazy[n][1] is None else ref.at[pl.ds(*lazy[n][1])], fetched[n], in_sems.at[n])
            for n, ref in enumerate(sources)
        ]
        for copy in incoming:
            copy.start()
        outgoing, base = [], 0
        for n in range(len(outs)):
            places = [targets[n].at[j] for j in range(outs[n][0])] if n in fan else [targets[n]]
            outgoing.append(
                [pltpu.make_async_copy(results[n], place, out_sems.at[base + j]) for j, place in enumerate(places)]
            )
            base += len(places)
        sent = set()

        def need():
            for copy in incoming:
                copy.wait()

        def send(n):
            sent.add(n)
            for copy in outgoing[n]:
                copy.start()

        body(inputs, fetched, results, spare, need, send)
        for n in range(len(outs)):
            if n not in sent:
                send(n)
        for copies in outgoing:
            for copy in copies:
                copy.wait()

    return pl.pallas_call(
        kernel,
        out_shape=[jax.ShapeDtypeStruct(s, jnp.float32) for s in outs],
        in_specs=[pl.BlockSpec(memory_space=pltpu.SMEM) if n in smem else vmem for n in range(len(args))]
        + [anywhere] * (len(lazy) + len(after)),
        out_specs=[anywhere] * len(outs),
        scratch_shapes=[
            *(pltpu.VMEM(tuple(s), jnp.float32) for s in (*held, *lazy_shapes, *scratch)),
            pltpu.SemaphoreType.DMA((fetches,)),
            pltpu.SemaphoreType.DMA((sends,)),
        ],
        compiler_params=pltpu.CompilerParams(vmem_limit_bytes=VMEM_LIMIT - room),
        cost_estimate=pl.CostEstimate(flops=int(micros * 1e9), bytes_accessed=10**6, transcendentals=0),
    )(*args, *(a for a, _ in lazy), *after)


def to_column(row):
    n = row.shape[1]
    same = lax.broadcasted_iota(jnp.int32, (n, n), 0) == lax.broadcasted_iota(jnp.int32, (n, n), 1)
    return jnp.sum(jnp.where(same, row, 0.0), axis=1, keepdims=True)


def to_row(column):
    n = column.shape[0]
    same = lax.broadcasted_iota(jnp.int32, (n, n), 0) == lax.broadcasted_iota(jnp.int32, (n, n), 1)
    return jnp.sum(jnp.where(same, column, 0.0), axis=0, keepdims=True)


def own_packs(own_ref, flat_ref):
    flat_ref[24:32, :] = jnp.zeros((8, H), jnp.float32)
    for q in range(3 * ROWS):
        flat_ref[q : q + 1, :] = own_ref[q]
    return [
        jnp.concatenate(
            [flat_ref[8 * g : 8 * g + 8, SLICE * x : SLICE * (x + 1)] for g in range(4)], axis=1
        )
        for x in range(NX)
    ]


def prepare_weights_body(args, lazy, results, scratch, need, send):
    packs = own_packs(args[0], scratch[0])
    for z in range(NZ):
        for x in range(NX):
            for y in range(NY):
                for t in range(3):
                    results[0][(z * NX + x) * NY + y, 8 * t : 8 * t + 8, :] = packs[x][:, LANES * t : LANES * (t + 1)]


def prepare_pairs_body(args, lazy, results, scratch, need, send):
    eta_ref, qkv_ref = args
    results[0][0:TOK, :] = qkv_ref[1, 0]
    results[0][TOK : 2 * TOK, :] = to_column(eta_ref[...]) * qkv_ref[2, 0]


def prepare_queries_body(args, lazy, results, scratch, need, send):
    (mom_ref,), (qkv_ref,), (queries_ref,) = args, lazy, results
    packs = own_packs(mom_ref, scratch[0])
    for x in range(NX):
        queries_ref[2 * TOK + 8 * x : 2 * TOK + 8 * x + 8, 0:H] = packs[x]
        queries_ref[2 * TOK + 8 * x : 2 * TOK + 8 * x + 8, H:D] = jnp.zeros((8, D - H), jnp.float32)
    need()
    queries_ref[0:TOK, :] = qkv_ref[0, 0]
    queries_ref[TOK : 2 * TOK, :] = qkv_ref[0, 1]


def marker_body(args, lazy, results, scratch, need, send):
    results[0][...] = jnp.zeros((8, LANES), jnp.float32)


def widened(part):
    return jnp.concatenate([part, jnp.zeros((part.shape[0], LANES - SLICE), jnp.float32)], axis=1)


def unpack(recv_ref, out_ref, x_stride, y_stride, z_stride):
    for s in range(8):
        for x in range(NX):
            for y in range(NY):
                start = x * x_stride + y * y_stride + s
                rows = jnp.concatenate(
                    [recv_ref[pl.ds(start + 8 * t, NZ, stride=z_stride), :] for t in range(3)], axis=1
                )
                for g in range(4):
                    at = entry(g, s)
                    if at is None:
                        continue
                    r, i = at
                    out_ref[pl.ds(i * D + (x * NY + y) * ROWS + r, NZ, stride=NX * NY * ROWS), :] = widened(
                        rows[:, SLICE * g : SLICE * (g + 1)]
                    )


def pack(in_ref, send_ref, x_stride, y_stride, z_stride):
    for s in range(8):
        for x in range(NX):
            for y in range(NY):
                parts = []
                for g in range(4):
                    at = entry(g, s)
                    if at is None:
                        parts.append(jnp.zeros((NZ, SLICE), jnp.float32))
                        continue
                    r, i = at
                    parts.append(in_ref[pl.ds(i * D + (x * NY + y) * ROWS + r, NZ, stride=NX * NY * ROWS), :][:, :SLICE])
                rows = jnp.concatenate(parts, axis=1)
                start = x * x_stride + y * y_stride + s
                for t in range(3):
                    send_ref[pl.ds(start + 8 * t, NZ, stride=z_stride), :] = rows[:, LANES * t : LANES * (t + 1)]


def token_rows(refs, start):
    return jnp.concatenate([ref[start : start + TOK, :] for ref in refs], axis=0)


def matrix(ref, i):
    return ref[i * D : (i + 1) * D, :]


def gradient_body(args, pairs, results, scratch, need, send):
    (recv_ref,), (w_ref, send_ref), (g_ref,) = args, results, scratch
    unpack(recv_ref, w_ref, 48, 24, 192)
    send(0)
    need()
    keys = token_rows(pairs, 0)
    weighted = token_rows(pairs, TOK)
    pre = split_dot(keys, jnp.concatenate([matrix(w_ref, 0), matrix(w_ref, 1)], axis=1))
    gate_pre, up_pre = pre[:, :LANES], pre[:, LANES:]
    back = -split_dot(weighted, matrix(w_ref, 2))
    sigmoid = jax.nn.sigmoid(gate_pre)
    gated = gate_pre * sigmoid
    hidden = gated * up_pre
    gate_back = back * up_pre * sigmoid * (1.0 + gate_pre * (1.0 - sigmoid))
    up_back = back * gated
    both = split_dot(keys, jnp.concatenate([gate_back, up_back], axis=1), ((0,), (0,)))
    g_ref[0:D, :] = both[:, :LANES]
    g_ref[D : 2 * D, :] = both[:, LANES:]
    g_ref[2 * D : 3 * D, :] = -split_dot(weighted, hidden, ((0,), (0,)))
    pack(g_ref, send_ref, 24, 96, 192)


def source(x_ref, s):
    return lax.rem(x_ref[0] + NX - s, NX)


def moment_body(args, tails, results, scratch, need, send):
    (x_ref, recv_ref), (own_ref,) = args, results
    total = recv_ref[0]
    for j in range(1, NZ * NY):
        total = total + recv_ref[j]
    own_ref[...] = total
    need()
    mine = pl.ds(pl.multiple_of(8 * x_ref[0], 8), 8)
    for s, ref in enumerate(tails):
        old = ref[mine, :]
        old = jnp.concatenate([old[:, LANES * t : LANES * (t + 1)] for t in range(3)], axis=0)
        rows = pl.ds(pl.multiple_of(24 * source(x_ref, s), 8), 24)
        own_ref[rows, :] = own_ref[rows, :] + MOMENTUM_RATE * old


def hidden_of(inputs, w1, w3):
    pre = split_dot(inputs, jnp.concatenate([w1, w3], axis=1))
    gate_pre, up_pre = pre[:, :LANES], pre[:, LANES:]
    return gate_pre * jax.nn.sigmoid(gate_pre) * up_pre


def first_read_body(args, lazy, results, scratch, need, send):
    need()
    *queries, w_ref = lazy
    hidden = hidden_of(token_rows(queries, 0), matrix(w_ref, 0), matrix(w_ref, 1))
    partial = split_dot(hidden, matrix(w_ref, 2), ((1,), (1,)))
    for s in range(NX):
        results[s][...] = partial[s * TOK : (s + 1) * TOK]


def renormalized(weights, moment):
    rate = STEP_SIZE / jnp.sqrt(jnp.mean(moment * moment, axis=0, keepdims=True) + EPSILON)
    moved = weights - moment * rate
    ratio = jnp.sqrt(jnp.mean(weights * weights, axis=0, keepdims=True) + EPSILON) / jnp.sqrt(
        jnp.mean(moved * moved, axis=0, keepdims=True) + EPSILON
    )
    return moved * ratio, rate, ratio


def second_read_body(args, lazy, results, scratch, need, send):
    (x_ref, recv_ref), (*queries, w_ref, moment_ref), (send_ref,), (m_ref,) = args, lazy, results, scratch
    unpack(recv_ref, m_ref, 24, 96, 192)
    need()
    new1, rate1, ratio1 = renormalized(matrix(w_ref, 0), matrix(m_ref, 0))
    new3, rate3, ratio3 = renormalized(matrix(w_ref, 1), matrix(m_ref, 1))
    new2, rate2, ratio2 = renormalized(matrix(w_ref, 2), matrix(m_ref, 2))
    hidden = hidden_of(token_rows(queries, 0), new1, new3)
    partial = split_dot(hidden, new2, ((1,), (1,)))
    stats = [rate1, rate3, rate2, ratio1, ratio3, ratio2, jnp.zeros((2, LANES), jnp.float32)]
    stats = jnp.concatenate(stats, axis=0)
    for x in range(NX):
        tail = [stats, *(moment_ref[0, 24 * x + 8 * t : 24 * x + 8 * t + 8, :] for t in range(3))]
        tail.append(jnp.zeros((8, LANES), jnp.float32))
        send_ref[x, TOK : TOK + 8, :] = jnp.concatenate(tail, axis=1)
    for s in range(NX):
        send_ref[source(x_ref, s), 0:TOK, :] = partial[s * TOK : (s + 1) * TOK]


def squares_body(args, lazy, results, scratch, need, send):
    (second_ref,), (readout_ref, send_ref) = args, results
    need()
    first = lazy[0][...] + lazy[1][...] + lazy[2][...] + lazy[3][...]
    second = second_ref[0, 0:TOK, :]
    for x in range(1, NX):
        second = second + second_ref[x, 0:TOK, :]
    readout_ref[0] = first
    readout_ref[1] = second
    row = jnp.concatenate(
        [to_row(jnp.sum(total * total, axis=1, keepdims=True)) for total in (first, second)], axis=1
    )
    send_ref[...] = jnp.broadcast_to(row, (8, GROUPS * TOK))


def own_rows_body(args, lazy, results, scratch, need, send):
    (second_ref, fw_ref), (new_w_ref, new_m_ref), (flat_ref,) = args, results, scratch
    for g in range(4):
        flat_ref[8 * g : 8 * g + 8, :] = jnp.concatenate(
            [
                second_ref[x, TOK : TOK + 8, LANES + SLICE * g : LANES + SLICE * (g + 1)]
                for x in range(NX)
            ],
            axis=1,
        )
    stats = jnp.concatenate([second_ref[x, TOK : TOK + 8, 0:SLICE] for x in range(NX)], axis=1)
    for q in range(3 * ROWS):
        i = q % 3
        moment = flat_ref[q : q + 1, :]
        new_m_ref[q] = moment
        new_w_ref[q] = (fw_ref[q] - moment * stats[i : i + 1]) * stats[3 + i : 4 + i]


def mix_body(args, lazy, results, scratch, need, send):
    (recv_ref, gain_ref, readout_ref, *attended_refs), (mixed_ref,) = args, results
    total = recv_ref[0, 0:1, :]
    for n in range(1, NARROW):
        total = total + recv_ref[n, 0:1, :]
    scale = to_column(1.0 / jnp.sqrt(total / (D * NARROW) + EPSILON))
    for c in range(GROUPS):
        mixed_ref[c] = attended_refs[c][...] + gain_ref[...] * (readout_ref[c] * scale[c * TOK : (c + 1) * TOK])


def attention_body(c, args, lazy, results, scratch, need, send):
    (position_ref,), (qkv_ref, near_ref, far_ref), (out_ref,) = args, lazy, results
    position = position_ref[0]
    row = lax.broadcasted_iota(jnp.int32, (TOK, 3 * TOK), 0) + 2 * TOK
    col = lax.broadcasted_iota(jnp.int32, (TOK, 3 * TOK), 1)
    window = (row - col >= 0) & (row - col < WINDOW)
    first = jnp.where(position >= 2, 0, jnp.where(position >= 1, TOK, 2 * TOK))
    need()
    allowed = window & (col >= first) if c == 0 else window
    for h in range(D // ATT):
        at = slice(h * ATT, (h + 1) * ATT)
        parts = []
        for a in range(2):
            far, near = far_ref[a, c, :, at], near_ref[a, c, :, at]
            if c == 1:
                far = jnp.where(position >= 2, far, far_ref[a, 0, :, at])
                near = jnp.where(position >= 1, near, near_ref[a, 0, :, at])
            parts.append(jnp.concatenate([far, near, qkv_ref[1 + a, c, :, at]], axis=0))
        keys, values = parts
        scores = dot(qkv_ref[0, c, :, at], keys, ((1,), (1,))) * (1.0 / math.sqrt(ATT))
        scores = jnp.where(allowed, scores, -1e30)
        weights = jnp.exp(scores - jnp.max(scores, axis=1, keepdims=True))
        weights = weights / jnp.sum(weights, axis=1, keepdims=True)
        out_ref[:, at] = dot(weights, values)


def behind(block, distance):
    axes = ("z", "x", "yh")
    return lax.ppermute(block, axes, [((i - distance) % BLOCKS, i) for i in range(BLOCKS)])


def from_neighbours(block):
    return [block] + [lax.ppermute(block, "x", [((i - s) % NX, i) for i in range(NX)]) for s in range(1, NX)]


def relayed_from_neighbours(block):
    behind_one = lax.ppermute(block, "x", [((i - 1) % NX, i) for i in range(NX)])
    from_ahead = [((i + 1) % NX, i) for i in range(NX)]
    ahead_one = lax.ppermute(block, "x", from_ahead)
    return [block, behind_one, lax.ppermute(ahead_one, "x", from_ahead), ahead_one]


def back_to_neighbours(blocks):
    return [blocks[0]] + [
        lax.ppermute(blocks[s], "x", [(i, (i - s) % NX) for i in range(NX)]) for s in range(1, NX)
    ]


def exchange(pieces, axes):
    return lax.all_to_all(pieces, axes, split_axis=0, concat_axis=0, tiled=True)


def scalar(value):
    return jnp.reshape(value, (1,)).astype(jnp.int32)


def whole(*arrays):
    return [(a, None) for a in arrays]


def local(qkv, eta, fast_weights, momentum, ttt_gain):
    own_weights, own_moment = fast_weights.reshape(3 * ROWS, 1, H), momentum.reshape(3 * ROWS, 1, H)
    x = lax.axis_index("x")
    position = scalar((lax.axis_index("z") * NX + x) * NY + lax.axis_index("yh"))
    x = scalar(x)
    (send1,) = call(prepare_weights_body, [(BLOCKS, 24, LANES)], 1, own_weights, scratch=[(32, H)], room=SMALL)
    (pairs,) = call(prepare_pairs_body, [(2 * TOK, D)], 1, eta, qkv, room=SMALL)
    recv1 = exchange(send1, ("z", "x", "yh")).reshape(BLOCKS * 24, LANES)
    pairs = relayed_from_neighbours(pairs)
    near, far = behind(qkv[1:], 1), behind(qkv[1:], 2)
    weights, send2 = call(
        gradient_body, [(3 * D, LANES), (BLOCKS * 24, LANES)], 5, recv1, lazy=whole(*pairs),
        scratch=[(3 * D, LANES)], room=ROOM - 512 * 1024,
    )
    recv2 = exchange(send2.reshape(NZ * NY, NX * 24, LANES), ("z", "yh"))
    (queries,) = call(
        prepare_queries_body, [(2 * TOK + 32, D)], 0.1, own_moment, lazy=[(qkv, (0, 1))], scratch=[(32, H)],
        after=(weights,),
    )
    queries = from_neighbours(queries)
    (marker,) = call(marker_body, [(8, LANES)], 12, after=(near, far))
    (send3,) = call(
        moment_body, [(NZ * NY, NX * 24, LANES)], 2, x, recv2, lazy=[(q, (2 * TOK, 32)) for q in queries],
        smem=(0,), fan=(0,), after=(marker,), room=ROOM,
    )
    recv3 = exchange(send3, ("z", "yh")).reshape(BLOCKS * 24, LANES)
    send_first = call(
        first_read_body, [(TOK, D)] * NX, 4, lazy=[*((q, (0, TOK)) for q in queries), (weights, None)],
        after=(send3,),
    )
    first = back_to_neighbours(send_first)
    (attended0,) = call(
        functools.partial(attention_body, 0), [(TOK, D)], 1, position, lazy=whole(qkv, near, far), smem=(0,),
        after=(send_first[0],),
    )
    (send_second,) = call(
        second_read_body, [(NX, TOK + 8, D)], 5, x, recv3,
        lazy=[*((q, (TOK, TOK)) for q in queries), (weights, None), (send3, (0, 1))], scratch=[(3 * D, LANES)],
        smem=(0,), after=(attended0, *first[1:]), room=ROOM,
    )
    second = exchange(send_second, "x")
    (attended1,) = call(
        functools.partial(attention_body, 1), [(TOK, D)], 5, position, lazy=whole(qkv, near, far), smem=(0,),
        after=(send_second,),
    )
    readout, send5 = call(
        squares_body, [(GROUPS, TOK, D), (NARROW, 8, GROUPS * TOK)], 1, second, lazy=whole(*first), fan=(1,),
        after=(attended1,), room=SMALL,
    )
    recv5 = exchange(send5, "narrow")
    new_weights, new_moment = call(
        own_rows_body, [(3 * ROWS, 1, H), (3 * ROWS, 1, H)], 1, second, own_weights, scratch=[(32, H)],
        after=(send5,), room=SMALL,
    )
    (mixed,) = call(
        mix_body, [(GROUPS, TOK, D)], 1, recv5, ttt_gain.reshape(1, D), readout, attended0, attended1, after=(new_weights,),
        room=SMALL,
    )
    return mixed, new_weights.reshape(1, ROWS, 3, H), new_moment.reshape(1, ROWS, 3, H)


def solution(mesh):
    fine = Mesh(mesh.devices.reshape(NZ, NX, NY, NARROW), ("z", "x", "yh", "narrow"))
    wide = ("z", "x", "yh")
    return jax.shard_map(
        local,
        mesh=fine,
        in_specs=(
            P(None, None, wide, "narrow"),
            P("narrow", wide),
            P("narrow", wide, None, None),
            P("narrow", wide, None, None),
            P("narrow"),
        ),
        out_specs=(
            P(None, wide, "narrow"),
            P("narrow", wide, None, None),
            P("narrow", wide, None, None),
        ),
        check_vma=False,
    )
```
